32 devices in a mesh: gx: 2 (over x), gy: 4 (over z), gz: 4 (over y, core).
Axes of the slice: x: 2, y: 2, z: 4, core: 2. Of those that a mesh axis runs over, the one named last changes fastest.
Arguments:
- fluid_temp: float32 [32, 256, 512], P('gx', 'gy', 'gz'), may hold values from -6 to 6
- liquid: int32 [32, 256, 512], P('gx', 'gy', 'gz'), may hold values 0 or 1
- face_src: int32 [4, 4, 4, 128], P('gx', 'gy', 'gz'), may hold values from -1 to 131071, as said below
- face_dst: int32 [4, 4, 4, 128], P('gx', 'gy', 'gz'), may hold values from -1 to 1023, as said below
- solid_old: float32 [16, 16, 128], P(('gy', 'gz'), 'gx'), may hold values from -6 to 6
- solid_diag: float32 [16, 16, 128], P(('gy', 'gz'), 'gx'), may hold values from 4 to 16
- blocks: float32 [16, 16, 5, 128, 128], P(('gy', 'gz'), 'gx'), may hold values from -0.25 to 0.25
- pattern: int32 [16, 16, 5], P(('gy', 'gz'), 'gx'), may hold values 0 or 1
Outputs:
- fluid_new: float32 [32, 256, 512], P('gx', 'gy', 'gz')
- solid_temp: float32 [16, 16, 128], P(('gy', 'gz'), 'gx')
The draws below stay inside these ranges and needn't reach their ends.
Inputs may be any that keep to these rules, and one draw needn't show every extreme that they name: `face_src`: entry q * 2 + r of slab (a, b) lists in its first c slots local cells of brick (q, a, b) whose temperatures go to run r, c from 1 to 128 and 128 in some blocks of every draw; the other slots hold -1; cells may repeat. `face_dst`: entry r * 2 + q of slab (a, b) names, slot by slot, the local solid cell of run r that receives the matching slot of face_src entry q * 2 + r, and -1 exactly where that slot of face_src is -1; cells may repeat.
All inputs are finite; a program needn't handle non-finite values. No bound on the sum of `liquid` or of `pattern` on one device may be relied on, other than what follows from the above.
Results may differ from the reference program's by a relative error of at most 0.00014.
Values sent between devices are 32-bit elements; how exact they have to be, the bound alone decides.
A program may use at most 64 MiB of HBM per device.

```python
import math
import jax
import jax.numpy as jnp
from jax import lax

CX = 16
CY = 64
CZ = 128
TILE = 128
TILE_DEV = 8
REACH = 2
FACE_CAP = 128
SWEEPS = 4
NB = 5
SENDERS = 2
BRICKS_Y = 4
BRICKS_Z = 4
SLABS = 16
TILES = 16
NX = 32
NY = 256
NZ = 512


def face_lists(key):
    base = jax.random.fold_in(key, 7301)
    key_small, key_full, key_source, key_target = jax.random.split(base, 4)
    grid = (SENDERS, SENDERS, BRICKS_Y, BRICKS_Z)
    small = jax.random.randint(key_small, grid, 1, FACE_CAP // 2 + 1)
    full = jax.random.randint(key_full, grid, 0, 8) == 0
    counts = jnp.where(full, FACE_CAP, small)
    counts = counts.at[0, 0].set(FACE_CAP)
    slot_ids = jnp.arange(FACE_CAP, dtype=jnp.int32)
    live = slot_ids < counts[..., None]
    sources = jax.random.randint(key_source, grid + (FACE_CAP,), 0, CX * CY * CZ)
    targets = jax.random.randint(key_target, grid + (FACE_CAP,), 0, TILE_DEV * TILE)
    sources = sources.at[0, 0, :, :, 0].set(CX * CY * CZ - 1).at[0, 0, :, :, 1].set(0)
    targets = targets.at[0, 0, :, :, 0].set(TILE_DEV * TILE - 1).at[0, 0, :, :, 1].set(0)
    sources = jnp.where(live, sources, -1).astype(jnp.int32)
    targets = jnp.where(live, targets, -1).astype(jnp.int32)
    sources = sources.reshape(SENDERS * SENDERS, BRICKS_Y, BRICKS_Z, FACE_CAP)
    targets = jnp.transpose(targets, (1, 0, 2, 3, 4)).reshape(SENDERS * SENDERS, BRICKS_Y, BRICKS_Z, FACE_CAP)
    return (sources, targets)


def draw_face_src(key, part):
    return face_lists(key)[0]


def draw_face_dst(key, part):
    return face_lists(key)[1]


def touch_ends(entries, own_key, least, largest):
    extent = entries.shape
    place = [jax.random.randint(jax.random.fold_in(own_key, axis), (), 0, extent[axis]) for axis in range(len(extent))]
    entries = entries.at[tuple(place)].set(least)
    longest = extent.index(max(extent))
    place[longest] = (place[longest] + 1) % extent[longest]
    return entries.at[tuple(place)].set(largest)


def shard_levels(own_key, dims, cuts, smallest, largest):
    factor_of, own = 1.0, jax.random.fold_in(own_key, 6)
    for dim, blocks in cuts:
        heights = jnp.exp(jax.random.uniform(jax.random.fold_in(own, dim), (blocks,), jnp.float32, smallest / len(cuts), largest / len(cuts)))
        factor_of = factor_of * jnp.repeat(heights, dims[dim] // blocks).reshape([-1 if axis == dim else 1 for axis in range(len(dims))])
    return factor_of


def gaussian(stream_key, shape, scale, limit, cuts=(), held_as=jnp.bfloat16):
    drawn = jax.random.normal(stream_key, shape, jnp.float32) * scale
    if len(cuts) > 0:
        drawn = shard_levels(stream_key, shape, cuts, -0.22, 0.18) * drawn
    return jnp.clip(drawn, min=-limit, max=limit).astype(held_as)


def setup_inputs(seed: int = 0) -> dict:
    key_list = jax.random.split(jax.random.key(seed), 9)
    fluid_temp = gaussian(key_list[0], (NX, NY, NZ), 1.0, 6.0, ((0, 2), (1, 4), (2, 4)), jnp.float32)
    liquid = touch_ends((jax.random.randint(key_list[1], (NX, NY, NZ), 0, 2) < 1).astype(jnp.int32), jax.random.fold_in(key_list[1], 1), 0, 1)
    face_src = draw_face_src(jax.random.fold_in(key_list[8], 71), 0)
    face_dst = draw_face_dst(jax.random.fold_in(key_list[8], 71), 0)
    solid_old = gaussian(key_list[4], (SLABS, TILES, TILE), 1.0, 6.0, ((0, 16), (1, 2)), jnp.float32)
    solid_diag = jnp.clip(jnp.exp(math.log(16.0) - 1.3862944 * jax.random.uniform(key_list[5], (SLABS, TILES, TILE), jnp.float32) ** shard_levels(key_list[5], (SLABS, TILES, TILE), ((0, 16), (1, 2)), -0.2, 0.2)), 4.0, 16.0)
    blocks = gaussian(key_list[6], (SLABS, TILES, NB, TILE, TILE), (NB * TILE) ** -0.5, 0.25, ((0, 16), (1, 2)), jnp.float32)
    pattern = touch_ends((jax.random.randint(key_list[7], (SLABS, TILES, NB), 0, 4) < 3).astype(jnp.int32), jax.random.fold_in(key_list[7], 1), 0, 1)
    return dict(fluid_temp=fluid_temp, liquid=liquid, face_src=face_src, face_dst=face_dst, solid_old=solid_old, solid_diag=solid_diag, blocks=blocks, pattern=pattern)


DIFFUSION = 0.12
EVAPORATION = 0.5
SATURATION = 0.25
WALL_COUPLING = 0.2


def apply_tiles(values, blocks_slab, pattern_slab, diagonal):
    padded = jnp.pad(values, ((REACH, REACH), (0, 0)))
    summed = diagonal * values
    for offset in range(NB):
        neighbour = padded[offset:offset + TILES]
        product = jnp.einsum("tab,tb->ta", blocks_slab[:, offset], neighbour, precision=lax.Precision.HIGHEST)
        summed = summed + pattern_slab[:, offset][:, None].astype(jnp.float32) * product
    return summed


def solve_slab(operands):
    right_side, blocks_slab, pattern_slab, diagonal = operands
    inverse = 1.0 / diagonal
    iterate = inverse * right_side
    residual = right_side - apply_tiles(iterate, blocks_slab, pattern_slab, diagonal)
    update = inverse * residual
    iterate = iterate + update
    rho_old = 0.5
    for sweep in range(1, SWEEPS):
        rho_next = 1.0 / (4.0 - rho_old)
        residual = right_side - apply_tiles(iterate, blocks_slab, pattern_slab, diagonal)
        update = (rho_next * rho_old) * update + (4.0 * rho_next) * inverse * residual
        iterate = iterate + update
        rho_old = rho_next
    return iterate


def reference(fluid_temp, liquid, face_src, face_dst, solid_old, solid_diag, blocks, pattern):
    fluid_cells = NX * NY * NZ
    solid_total = SLABS * TILES * TILE
    sources = face_src.reshape(SENDERS, SENDERS, BRICKS_Y, BRICKS_Z, FACE_CAP)
    first_ids = jnp.arange(SENDERS, dtype=jnp.int32).reshape(-1, 1, 1, 1, 1)
    y_ids = jnp.arange(BRICKS_Y, dtype=jnp.int32).reshape(1, 1, -1, 1, 1)
    z_ids = jnp.arange(BRICKS_Z, dtype=jnp.int32).reshape(1, 1, 1, -1, 1)
    clipped = jnp.maximum(sources, 0)
    row_in = clipped // (CY * CZ)
    column = (clipped // CZ) % CY
    depth = clipped % CZ
    global_ids = ((first_ids * CX + row_in) * NY + y_ids * CY + column) * NZ + z_ids * CZ + depth
    global_ids = jnp.where(sources >= 0, global_ids, fluid_cells).astype(jnp.int32)
    flat_temp = jnp.concatenate([fluid_temp.reshape(-1), jnp.zeros((1,), jnp.float32)])
    outgoing = flat_temp[global_ids]
    targets = face_dst.reshape(SENDERS, SENDERS, BRICKS_Y, BRICKS_Z, FACE_CAP)
    slab_ids = y_ids * BRICKS_Z + z_ids
    solid_ids = slab_ids * (TILES * TILE) + first_ids * (TILE_DEV * TILE) + jnp.maximum(targets, 0)
    solid_ids = jnp.where(targets >= 0, solid_ids, solid_total).astype(jnp.int32)
    arriving = jnp.transpose(outgoing, (1, 0, 2, 3, 4))
    gathered = jnp.zeros((solid_total + 1,), jnp.float32).at[solid_ids].add(arriving)[:solid_total]
    right_side = solid_diag * solid_old + gathered.reshape(SLABS, TILES, TILE)
    solid_temp = lax.map(solve_slab, (right_side, blocks, pattern, solid_diag))
    solid_flat = jnp.concatenate([solid_temp.reshape(-1), jnp.zeros((1,), jnp.float32)])
    returned = jnp.transpose(solid_flat[solid_ids], (1, 0, 2, 3, 4))
    wall_sum = jnp.zeros((fluid_cells + 1,), jnp.float32).at[global_ids].add(returned - outgoing)[:fluid_cells]
    wall_sum = wall_sum.reshape(NX, NY, NZ)
    laplacian = -6.0 * fluid_temp
    for dimension in range(3):
        laplacian = laplacian + jnp.roll(fluid_temp, 1, dimension) + jnp.roll(fluid_temp, -1, dimension)
    liquid_share = liquid.astype(jnp.float32)
    fluid_new = fluid_temp + DIFFUSION * laplacian - EVAPORATION * liquid_share * jnp.maximum(fluid_temp - SATURATION, 0.0) + WALL_COUPLING * wall_sum
    return fluid_new, solid_temp
```

```python
import functools

import jax
import jax.numpy as jnp
from jax import lax
from jax.experimental import pallas as pl
from jax.experimental.pallas import tpu as pltpu
from jax.sharding import PartitionSpec as P

REACH = 2
SWEEPS = 4
NB = 5
DIFFUSION = 0.12
EVAPORATION = 0.5
SATURATION = 0.25
WALL_COUPLING = 0.2
MESH = pl.DeviceIdType.MESH
F32 = jnp.float32
BF16 = jnp.bfloat16


def split(values):
    high = values.astype(BF16)
    return high, (values - high.astype(F32)).astype(BF16)


def dot(a, b):
    return jnp.dot(a, b, preferred_element_type=F32)


def dot_nt(a, b):
    return lax.dot_general(a, b, (((1,), (1,)), ((), ())), preferred_element_type=F32)


def rows_of(shape):
    return lax.broadcasted_iota(jnp.int32, shape, 0)


def repeat(count, body):
    if count == 1:
        body(0)
    else:
        pl.loop(0, count)(body)


def kernel(
    senders, group,
    fluid_h, liquid_h, src_h, dst_h, old_h, diag_h, blocks_h, pat_h,
    new_ref, solid_ref,
    fluid, liquid, src, dst, old, diag, blocks, pat,
    hot, table, base, outp, arr, sent, ret, pre_out, pre_in, halo_out, halo,
    x_in, y_out, y_in, z_out, z_in, ext, gather, win, sums,
    load_sem, arr_send, arr_recv, ret_send, ret_recv, pre_send, pre_recv,
    halo_send, halo_recv, face_send, face_recv,
):
    cx, cy, cz = fluid.shape
    rows = cx * cy
    tiles, width = old.shape[1], old.shape[2]
    chunks = senders // group
    me = lax.axis_index("gx")
    gy, gz = lax.axis_index("gy"), lax.axis_index("gz")
    ny, nz = lax.axis_size("gy"), lax.axis_size("gz")
    left, right = lax.rem(me + senders - 1, senders), lax.rem(me + 1, senders)
    below, above = lax.rem(gy + ny - 1, ny), lax.rem(gy + 1, ny)
    before, after = lax.rem(gz + nz - 1, nz), lax.rem(gz + 1, nz)
    has_left, has_right = me > 0, me < senders - 1

    barrier = pltpu.get_barrier_semaphore()
    peers = [{"gx": lax.rem(me + d, senders)} for d in range(1, senders)]
    peers += [{"gy": below}, {"gy": above}, {"gz": before}, {"gz": after}]
    for peer in peers:
        pl.semaphore_signal(barrier, inc=1, device_id=peer, device_id_type=MESH)

    pairs = [(src_h, src), (fluid_h, fluid), (dst_h, dst), (old_h, old), (diag_h, diag),
             (pat_h, pat), (blocks_h, blocks), (liquid_h, liquid)]
    loads = [pltpu.make_async_copy(a, b, load_sem.at[i]) for i, (a, b) in enumerate(pairs)]
    for load in loads:
        load.start()

    def send(source, target, send_sem, recv_sem, device):
        return pltpu.make_async_remote_copy(
            src_ref=source, dst_ref=target, send_sem=send_sem, recv_sem=recv_sem,
            device_id=device, device_id_type=MESH)

    outp[...] = jnp.zeros_like(outp)
    ext[...] = jnp.zeros_like(ext)
    loads[0].wait()

    def make_hot(c):
        for j in range(group):
            ids = src[c * group + j, 0]
            row = ids >> 7
            for s in range(0, rows, 128):
                hit = rows_of((128, width)) + s == row
                hot[c, s:s + 128, j * width:(j + 1) * width] = jnp.where(hit, 1.0, 0.0).astype(BF16)

    repeat(chunks, make_hot)

    for load in loads[2:5]:
        load.wait()
    diagonal = diag[0]
    inverse = 1.0 / diagonal
    fixed = diagonal * old[0]
    for side, lo in ((0, 0), (1, tiles - REACH)):
        for q in range(senders):
            pre_out[side, q:q + 1, :] = dst[q, 0].astype(F32)
        pre_out[side, senders:senders + REACH, :] = fixed[lo:lo + REACH]
        pre_out[side, senders + REACH:senders + 2 * REACH, :] = inverse[lo:lo + REACH]
    pl.semaphore_wait(barrier, len(peers))

    pre_l = send(pre_out.at[0], pre_in.at[1], pre_send.at[0], pre_recv.at[1], {"gx": left})
    pre_r = send(pre_out.at[1], pre_in.at[0], pre_send.at[1], pre_recv.at[0], {"gx": right})
    halo_l = [send(halo_out.at[k, 0], halo.at[k, 1], halo_send.at[k, 0], halo_recv.at[k, 1],
                   {"gx": left}) for k in range(SWEEPS - 1)]
    halo_r = [send(halo_out.at[k, 1], halo.at[k, 0], halo_send.at[k, 1], halo_recv.at[k, 0],
                   {"gx": right}) for k in range(SWEEPS - 1)]

    @pl.when(has_left)
    def _():
        pre_l.start()

    @pl.when(has_right)
    def _():
        pre_r.start()

    @pl.when(jnp.logical_not(has_left))
    def _():
        pre_in[0] = jnp.zeros_like(pre_in[0])
        for k in range(SWEEPS - 1):
            halo[k, 0] = jnp.zeros_like(halo[k, 0])

    @pl.when(jnp.logical_not(has_right))
    def _():
        pre_in[1] = jnp.zeros_like(pre_in[1])
        for k in range(SWEEPS - 1):
            halo[k, 1] = jnp.zeros_like(halo[k, 1])

    loads[1].wait()
    per = 128 // cy
    for s in range(rows // 128):
        flipped = fluid[s * per:(s + 1) * per].reshape(128, cz).T
        high, low = split(flipped)
        table[0:cz, s * 128:(s + 1) * 128] = high
        table[cz:2 * cz, s * 128:(s + 1) * 128] = low
        z_out[0, :, s * 128:(s + 1) * 128] = flipped[0:1]
        z_out[1, :, s * 128:(s + 1) * 128] = flipped[cz - 1:cz]

    def pick(c):
        picked = dot(table[...], hot[c])
        picked = picked[0:cz] + picked[cz:2 * cz]
        for j in range(group):
            depth = src[c * group + j, 0] & (cz - 1)
            part = picked[:, j * width:(j + 1) * width]
            part = jnp.where(rows_of((cz, width)) == depth, part, 0.0)
            outp[c * group + j + 1] = jnp.sum(part, axis=0, keepdims=True)

    repeat(chunks, pick)
    arrivals = []
    for d in range(1, senders):
        peer = lax.rem(me + d, senders)
        arrivals.append(send(outp.at[pl.ds(peer, 3)], arr.at[me], arr_send.at[d], arr_recv.at[d],
                             {"gx": peer}))
        arrivals[-1].start()
    arr[pl.ds(me, 1)] = outp[pl.ds(me, 3)][None]

    y_out[0] = fluid[:, 0, :]
    y_out[1] = fluid[:, cy - 1, :]
    faces = [
        send(fluid.at[0], x_in.at[1], face_send.at[0], face_recv.at[0], {"gx": left}),
        send(fluid.at[cx - 1], x_in.at[0], face_send.at[1], face_recv.at[1], {"gx": right}),
        send(y_out.at[0], y_in.at[1], face_send.at[2], face_recv.at[2], {"gy": below}),
        send(y_out.at[1], y_in.at[0], face_send.at[3], face_recv.at[3], {"gy": above}),
        send(z_out.at[0], z_in.at[1], face_send.at[4], face_recv.at[4], {"gz": before}),
        send(z_out.at[1], z_in.at[0], face_send.at[5], face_recv.at[5], {"gz": after}),
    ]
    for face in faces:
        face.start()

    loads[7].wait()
    lane = lax.broadcasted_iota(jnp.int32, (cy, cz), 1)
    line = lax.broadcasted_iota(jnp.int32, (cy, cz), 0)
    for i in range(cx):
        here = fluid[i]
        near = jnp.where(line == 0, 0.0, pltpu.roll(here, 1, 0))
        near = near + jnp.where(line == cy - 1, 0.0, pltpu.roll(here, cy - 1, 0))
        near = near + jnp.where(lane == 0, 0.0, pltpu.roll(here, 1, 1))
        near = near + jnp.where(lane == cz - 1, 0.0, pltpu.roll(here, cz - 1, 1))
        if i > 0:
            near = near + fluid[i - 1]
        if i < cx - 1:
            near = near + fluid[i + 1]
        dry = liquid[i].astype(F32) * jnp.maximum(here - SATURATION, 0.0)
        base[i] = here + DIFFUSION * (near - 6.0 * here) - EVAPORATION * dry

    for load in loads[5:7]:
        load.wait()
    mask = [jnp.broadcast_to(pat[0, :, o:o + 1].astype(F32), (tiles, width)) for o in range(NB)]
    ones = jnp.ones((2 * width, width), BF16)
    eye = rows_of((width, width)) == lax.broadcasted_iota(jnp.int32, (width, width), 1)

    @pl.when(has_left)
    def _():
        pre_r_in = send(pre_out.at[1], pre_in.at[0], pre_send.at[1], pre_recv.at[0], {"gx": left})
        pre_r_in.wait_recv()

    @pl.when(has_right)
    def _():
        pre_l_in = send(pre_out.at[0], pre_in.at[1], pre_send.at[0], pre_recv.at[1], {"gx": right})
        pre_l_in.wait_recv()

    def own_ids(q):
        return dst[q, 0]

    def near_ids(side):
        return lambda q: pre_in[side, pl.ds(q, 1), :].astype(jnp.int32)

    for copy in arrivals:
        copy.wait_recv()

    def spread(run, ids_of):
        gather[run] = jnp.zeros((2 * tiles, width), F32)

        def add_group(c):
            lhs, rhs = [], []
            for j in range(group):
                q = c * group + j
                ids = ids_of(q)
                placed = jnp.where(rows_of((tiles, width)) == ids >> 7, arr[q, run], 0.0)
                high, low = split(placed)
                lhs.append(jnp.concatenate([high, low], axis=0))
                hit = rows_of((width, width)) == ids & (width - 1)
                rhs.append(jnp.where(hit, 1.0, 0.0).astype(BF16))
            gather[run] += dot_nt(jnp.concatenate(lhs, axis=1), jnp.concatenate(rhs, axis=1))

        repeat(chunks, add_group)
        both = gather[run]
        return both[0:tiles] + both[tiles:2 * tiles]

    right_side = fixed + spread(1, own_ids)
    iterate = inverse * right_side
    for side, run, lo, at in ((0, 0, tiles - REACH, 0), (1, 2, 0, tiles + REACH)):
        summed = spread(run, near_ids(side))[lo:lo + REACH]
        fixed_near = pre_in[side, senders:senders + REACH, :]
        inverse_near = pre_in[side, senders + REACH:senders + 2 * REACH, :]
        ext[at:at + REACH, :] = inverse_near * (fixed_near + summed)

    def windows():
        for o in range(NB):
            win[o] = mask[o] * ext[o:o + tiles, :]

    def couple(slot, pairs_of):
        for t, offsets in pairs_of:
            total = None
            for o in offsets:
                term = blocks[0, t, o] * win[o, t:t + 1, :]
                total = term if total is None else total + term
            high, low = split(total)
            summed = dot(jnp.concatenate([high, low], axis=1), ones)
            sums[slot, t:t + 1, :] = jnp.sum(jnp.where(eye, summed, 0.0), axis=0, keepdims=True)

    def inside(t, o):
        return 0 <= t + o - REACH < tiles

    every = [(t, list(range(NB))) for t in range(tiles)]
    local = [(t, [o for o in range(NB) if inside(t, o)]) for t in range(tiles)]
    outer = [(t, [o for o in range(NB) if not inside(t, o)]) for t in range(tiles)]
    outer = [(t, offsets) for t, offsets in outer if offsets]

    def pass_on(k):
        halo_out[k, 0] = iterate[0:REACH]
        halo_out[k, 1] = iterate[tiles - REACH:tiles]

        @pl.when(has_left)
        def _():
            halo_l[k].start()

        @pl.when(has_right)
        def _():
            halo_r[k].start()

    def take(k):
        @pl.when(has_left)
        def _():
            halo_r[k].wait_recv()

        @pl.when(has_right)
        def _():
            halo_l[k].wait_recv()

    ext[REACH:REACH + tiles, :] = iterate
    windows()
    couple(0, every)
    update = inverse * (right_side - diagonal * iterate - sums[0])
    iterate = iterate + update
    sums[1] = jnp.zeros((tiles, width), F32)
    rho_old = 0.5
    for k in range(SWEEPS - 1):
        pass_on(k)
        rho_next = 1.0 / (4.0 - rho_old)
        ext[...] = jnp.zeros_like(ext)
        ext[REACH:REACH + tiles, :] = iterate
        windows()
        couple(0, local)
        part = right_side - diagonal * iterate - sums[0]
        if k == 0:
            for face in faces:
                face.wait_recv()
            base[0] += DIFFUSION * x_in[0]
            base[cx - 1] += DIFFUSION * x_in[1]
            base[:, 0, :] += DIFFUSION * y_in[0]
            base[:, cy - 1, :] += DIFFUSION * y_in[1]
        if k == 1:
            deep = rows_of((cz, 128))
            for s in range(rows // 128):
                cut = slice(s * 128, (s + 1) * 128)
                layer = jnp.where(deep == 0, z_in[0, :, cut], 0.0)
                layer = layer + jnp.where(deep == cz - 1, z_in[1, :, cut], 0.0)
                base[s * per:(s + 1) * per] += DIFFUSION * layer.T.reshape(per, cy, cz)
        take(k)
        ext[0:REACH, :] = halo[k, 0]
        ext[tiles + REACH:tiles + 2 * REACH, :] = halo[k, 1]
        windows()
        couple(1, outer)
        residual = part - sums[1]
        update = rho_next * rho_old * update + 4.0 * rho_next * inverse * residual
        iterate = iterate + update
        rho_old = rho_next

    high, low = split(iterate)
    pair = jnp.concatenate([high, low], axis=0)

    def pick_back(c):
        rhs = []
        for j in range(group):
            hit = rows_of((width, width)) == dst[c * group + j, 0] & (width - 1)
            rhs.append(jnp.where(hit, 1.0, 0.0).astype(BF16))
        picked = dot(pair, jnp.concatenate(rhs, axis=1))
        picked = picked[0:tiles] + picked[tiles:2 * tiles]
        for j in range(group):
            row = dst[c * group + j, 0] >> 7
            part = jnp.where(rows_of((tiles, width)) == row, picked[:, j * width:(j + 1) * width], 0.0)
            sent[c * group + j] = jnp.sum(part, axis=0, keepdims=True)

    repeat(chunks, pick_back)
    backs = []
    for d in range(1, senders):
        peer = lax.rem(me + d, senders)
        backs.append(send(sent.at[peer], ret.at[me], ret_send.at[d], ret_recv.at[d], {"gx": peer}))
        backs[-1].start()
    ret[pl.ds(me, 1)] = sent[pl.ds(me, 1)]
    solid_ref[0] = iterate
    for copy in arrivals + faces:
        copy.wait_send()

    @pl.when(has_left)
    def _():
        for copy in [pre_l] + halo_l:
            copy.wait_send()

    @pl.when(has_right)
    def _():
        for copy in [pre_r] + halo_r:
            copy.wait_send()

    for copy in backs:
        copy.wait_recv()

    def spread_back(c):
        halves = []
        for j in range(group):
            q = c * group + j
            depth = src[q, 0] & (cz - 1)
            value = WALL_COUPLING * (ret[q] - outp[q + 1])
            placed = jnp.where(rows_of((cz, width)) == depth, value, 0.0)
            halves.append(jnp.concatenate(split(placed), axis=0))
        placed = jnp.concatenate(halves, axis=1)
        for s in range(0, rows, 256):
            both = dot_nt(hot[c, s:s + 256, :], placed)
            both = (both[:, 0:cz] + both[:, cz:2 * cz]).reshape(256 // cy, cy, cz)
            cut = slice(s // cy, (s + 256) // cy)
            if chunks == 1:
                new_ref[cut] = base[cut] + both
            else:
                base[cut] += both

    repeat(chunks, spread_back)
    if chunks > 1:
        new_ref[...] = base[...]
    for copy in backs:
        copy.wait_send()


def per_device(fluid_temp, liquid, face_src, face_dst, solid_old, solid_diag, blocks, pattern):
    senders = lax.axis_size("gx")
    group = 2 if senders % 2 == 0 else 1
    cx, cy, cz = fluid_temp.shape
    rows = cx * cy
    tiles, width = solid_old.shape[1:]
    pre_rows = (senders + 2 * REACH + 7) // 8 * 8
    ext_rows = (tiles + 2 * REACH + 7) // 8 * 8
    dma = pltpu.SemaphoreType.DMA
    args = (fluid_temp, liquid, face_src, face_dst, solid_old, solid_diag, blocks, pattern)
    scratch = [pltpu.VMEM(a.shape, a.dtype) for a in args]
    scratch += [
        pltpu.VMEM((senders // group, rows, group * width), BF16),
        pltpu.VMEM((2 * cz, rows), BF16),
        pltpu.VMEM((cx, cy, cz), F32),
        pltpu.VMEM((senders + 2, 1, width), F32),
        pltpu.VMEM((senders, 3, 1, width), F32),
        pltpu.VMEM((senders, 1, width), F32),
        pltpu.VMEM((senders, 1, width), F32),
        pltpu.VMEM((2, pre_rows, width), F32),
        pltpu.VMEM((2, pre_rows, width), F32),
        pltpu.VMEM((SWEEPS - 1, 2, REACH, width), F32),
        pltpu.VMEM((SWEEPS - 1, 2, REACH, width), F32),
        pltpu.VMEM((2, cy, cz), F32),
        pltpu.VMEM((2, cx, cz), F32),
        pltpu.VMEM((2, cx, cz), F32),
        pltpu.VMEM((2, 1, rows), F32),
        pltpu.VMEM((2, 1, rows), F32),
        pltpu.VMEM((ext_rows, width), F32),
        pltpu.VMEM((3, 2 * tiles, width), F32),
        pltpu.VMEM((NB, tiles, width), F32),
        pltpu.VMEM((2, tiles, width), F32),
        dma((8,)),
        dma((senders,)), dma((senders,)),
        dma((senders,)), dma((senders,)),
        dma((2,)), dma((2,)),
        dma((SWEEPS - 1, 2)), dma((SWEEPS - 1, 2)),
        dma((6,)), dma((6,)),
    ]
    return pl.pallas_call(
        functools.partial(kernel, senders, group),
        out_shape=(
            jax.ShapeDtypeStruct(fluid_temp.shape, F32),
            jax.ShapeDtypeStruct(solid_old.shape, F32),
        ),
        in_specs=[pl.BlockSpec(memory_space=pl.ANY)] * 8,
        out_specs=(pl.BlockSpec(memory_space=pltpu.VMEM),) * 2,
        scratch_shapes=scratch,
        compiler_params=pltpu.CompilerParams(
            collective_id=0, has_side_effects=True, vmem_limit_bytes=56 * 1024 * 1024
        ),
    )(*args)


def solution(mesh):
    return jax.shard_map(
        per_device,
        mesh=mesh,
        in_specs=(
            P("gx", "gy", "gz"),
            P("gx", "gy", "gz"),
            P("gx", "gy", "gz", None),
            P("gx", "gy", "gz", None),
            P(("gy", "gz"), "gx", None),
            P(("gy", "gz"), "gx", None),
            P(("gy", "gz"), "gx", None, None, None),
            P(("gy", "gz"), "gx", None),
        ),
        out_specs=(P("gx", "gy", "gz"), P(("gy", "gz"), "gx", None)),
        check_vma=False,
    )
```

```python
import functools

import jax
import jax.numpy as jnp
from jax import lax
from jax.experimental import pallas as pl
from jax.experimental.pallas import tpu as pltpu
from jax.sharding import PartitionSpec as P

REACH = 2
SWEEPS = 4
NB = 5
DIFFUSION = 0.12
EVAPORATION = 0.5
SATURATION = 0.25
WALL_COUPLING = 0.2
MESH = pl.DeviceIdType.MESH
F32 = jnp.float32
BF16 = jnp.bfloat16


def split(values):
    high = values.astype(BF16)
    return high, (values - high.astype(F32)).astype(BF16)


def dot(a, b):
    return jnp.dot(a, b, preferred_element_type=F32)


def dot_nt(a, b):
    return lax.dot_general(a, b, (((1,), (1,)), ((), ())), preferred_element_type=F32)


def rows_of(shape):
    return lax.broadcasted_iota(jnp.int32, shape, 0)


def repeat(count, body):
    if count == 1:
        body(0)
    else:
        pl.loop(0, count)(body)


def kernel(
    senders, group,
    fluid_h, liquid_h, src_h, dst_h, old_h, diag_h, blocks_h, pat_h,
    base, hot, src, wall, solid,
    fluid, liquid, dst, old, diag, blocks, pat,
    spot, table, outp, arr, sent, ret, pre_out, pre_in, halo_out, halo,
    x_in, y_out, y_in, z_out, z_in, ext, gather, sums,
    load_sem, arr_send, arr_recv, ret_send, ret_recv, pre_send, pre_recv,
    halo_send, halo_recv, face_send, face_recv, go, cross,
):
    cx, cy, cz = fluid.shape
    rows = cx * cy
    tiles, width = old.shape[1], old.shape[2]
    chunks = senders // group
    me = lax.axis_index("gx")
    gy, gz = lax.axis_index("gy"), lax.axis_index("gz")
    ny, nz = lax.axis_size("gy"), lax.axis_size("gz")
    left, right = lax.rem(me + senders - 1, senders), lax.rem(me + 1, senders)
    below, above = lax.rem(gy + ny - 1, ny), lax.rem(gy + 1, ny)
    before, after = lax.rem(gz + nz - 1, nz), lax.rem(gz + 1, nz)
    has_left, has_right = me > 0, me < senders - 1
    late = lax.rem(gz, 2) == 1
    barrier = pltpu.get_barrier_semaphore()

    @pl.when(me != 0)
    def _():
        pl.semaphore_signal(barrier, inc=1, device_id={"gx": 0}, device_id_type=MESH)

    pairs = [(src_h, src), (fluid_h, fluid), (dst_h, dst), (old_h, old), (diag_h, diag),
             (pat_h, pat), (blocks_h, blocks), (liquid_h, liquid)]
    loads = [pltpu.make_async_copy(a, b, load_sem.at[i]) for i, (a, b) in enumerate(pairs)]
    for load in loads:
        load.start()

    def send(source, target, send_sem, recv_sem, device):
        return pltpu.make_async_remote_copy(
            src_ref=source, dst_ref=target, send_sem=send_sem, recv_sem=recv_sem,
            device_id=device, device_id_type=MESH)

    outp[...] = jnp.zeros_like(outp)
    ext[...] = jnp.zeros_like(ext)
    sums[...] = jnp.zeros_like(sums)
    loads[0].wait()

    def make_hot(c):
        for j in range(group):
            row = src[c * group + j, 0] >> 7
            for s in range(0, rows, 128):
                hit = rows_of((128, width)) + s == row
                hot[c, s:s + 128, j * width:(j + 1) * width] = jnp.where(hit, 1.0, 0.0).astype(BF16)

    repeat(chunks, make_hot)

    @pl.when(me == 0)
    def _():
        pl.semaphore_wait(barrier, senders - 1)
        for d in range(1, senders):
            pl.semaphore_signal(go, inc=1, device_id={"gx": d}, device_id_type=MESH)

    for load in loads[2:5]:
        load.wait()
    diagonal = diag[0]
    inverse = 1.0 / diagonal
    fixed = diagonal * old[0]
    for side, lo in ((0, 0), (1, tiles - REACH)):
        for q in range(senders):
            pre_out[side, q:q + 1, :] = dst[q, 0].astype(F32)
        pre_out[side, senders:senders + REACH, :] = fixed[lo:lo + REACH]
        pre_out[side, senders + REACH:senders + 2 * REACH, :] = inverse[lo:lo + REACH]

    loads[1].wait()
    per = 128 // cy
    for s in range(rows // 128):
        flipped = fluid[s * per:(s + 1) * per].reshape(128, cz).T
        high, low = split(flipped)
        table[0:cz, s * 128:(s + 1) * 128] = high
        table[cz:2 * cz, s * 128:(s + 1) * 128] = low
        z_out[0, :, s * 128:(s + 1) * 128] = flipped[0:1]
        z_out[1, :, s * 128:(s + 1) * 128] = flipped[cz - 1:cz]

    def pick(c):
        picked = dot(table[...], hot[c])
        picked = picked[0:cz] + picked[cz:2 * cz]
        for j in range(group):
            depth = src[c * group + j, 0] & (cz - 1)
            part = picked[:, j * width:(j + 1) * width]
            part = jnp.where(rows_of((cz, width)) == depth, part, 0.0)
            outp[c * group + j + 1] = jnp.sum(part, axis=0, keepdims=True)

    repeat(chunks, pick)

    @pl.when(me != 0)
    def _():
        pl.semaphore_wait(go, 1)

    @pl.when(me == 1)
    def _():
        for peer in ({"gy": below}, {"gy": above}, {"gz": before}, {"gz": after}):
            pl.semaphore_signal(barrier, inc=1, device_id=peer, device_id_type=MESH)

    pre_l = send(pre_out.at[0], pre_in.at[1], pre_send.at[0], pre_recv.at[1], {"gx": left})
    pre_r = send(pre_out.at[1], pre_in.at[0], pre_send.at[1], pre_recv.at[0], {"gx": right})
    halo_l = [send(halo_out.at[k, 0], halo.at[k, 1], halo_send.at[k, 0], halo_recv.at[k, 1],
                   {"gx": left}) for k in range(SWEEPS - 1)]
    halo_r = [send(halo_out.at[k, 1], halo.at[k, 0], halo_send.at[k, 1], halo_recv.at[k, 0],
                   {"gx": right}) for k in range(SWEEPS - 1)]
    arrivals = []
    for d in range(1, senders):
        peer = lax.rem(me + d, senders)
        arrivals.append(send(outp.at[pl.ds(peer, 3)], arr.at[me], arr_send.at[d], arr_recv.at[d],
                             {"gx": peer}))

    @pl.when(has_left)
    def _():
        pre_l.start()

    @pl.when(has_right)
    def _():
        pre_r.start()

    for copy in arrivals:
        copy.start()
    faces = [
        send(fluid.at[0], x_in.at[1], face_send.at[0], face_recv.at[0], {"gx": left}),
        send(fluid.at[cx - 1], x_in.at[0], face_send.at[1], face_recv.at[1], {"gx": right}),
        send(y_out.at[0], y_in.at[1], face_send.at[2], face_recv.at[2], {"gy": below}),
        send(y_out.at[1], y_in.at[0], face_send.at[3], face_recv.at[3], {"gy": above}),
        send(z_out.at[0], z_in.at[1], face_send.at[4], face_recv.at[4], {"gz": before}),
        send(z_out.at[1], z_in.at[0], face_send.at[5], face_recv.at[5], {"gz": after}),
    ]
    for face in faces[0:2]:
        face.start()
    arr[pl.ds(me, 1)] = outp[pl.ds(me, 3)][None]
    y_out[0] = fluid[:, 0, :]
    y_out[1] = fluid[:, cy - 1, :]

    @pl.when(jnp.logical_not(has_left))
    def _():
        pre_in[0] = jnp.zeros_like(pre_in[0])
        for k in range(SWEEPS - 1):
            halo[k, 0] = jnp.zeros_like(halo[k, 0])

    @pl.when(jnp.logical_not(has_right))
    def _():
        pre_in[1] = jnp.zeros_like(pre_in[1])
        for k in range(SWEEPS - 1):
            halo[k, 1] = jnp.zeros_like(halo[k, 1])

    for load in loads[5:7]:
        load.wait()
    small = rows_of((tiles, tiles)) == lax.broadcasted_iota(jnp.int32, (tiles, tiles), 1)
    for o in range(NB):
        row = jnp.broadcast_to(pat[o].astype(F32), (tiles, tiles))
        column = jnp.sum(jnp.where(small, row, 0.0), axis=1, keepdims=True)
        mask = jnp.broadcast_to(column, (tiles, width))
        for t in range(tiles):
            blocks[0, t, o] = blocks[0, t, o] * mask[t:t + 1]

    @pl.when(has_left)
    def _():
        send(pre_out.at[1], pre_in.at[0], pre_send.at[1], pre_recv.at[0], {"gx": left}).wait_recv()

    @pl.when(has_right)
    def _():
        send(pre_out.at[0], pre_in.at[1], pre_send.at[0], pre_recv.at[1], {"gx": right}).wait_recv()

    def ids_at(run, q):
        if run == 1:
            return dst[q, 0]
        return pre_in[run // 2, pl.ds(q, 1), :].astype(jnp.int32)

    def make_spot(c):
        for run in range(3):
            for j in range(group):
                hit = rows_of((width, width)) == ids_at(run, c * group + j) & (width - 1)
                spot[run, c, :, j * width:(j + 1) * width] = jnp.where(hit, 1.0, 0.0).astype(BF16)

    repeat(chunks, make_spot)
    ones = jnp.ones((2 * width, width), BF16)
    eye = rows_of((width, width)) == lax.broadcasted_iota(jnp.int32, (width, width), 1)
    for copy in arrivals:
        copy.wait_recv()

    gather[...] = jnp.zeros_like(gather)

    def add_group(c):
        for run in range(3):
            lhs = []
            for j in range(group):
                q = c * group + j
                hit = rows_of((tiles, width)) == ids_at(run, q) >> 7
                high, low = split(jnp.where(hit, arr[q, run], 0.0))
                lhs.append(jnp.concatenate([high, low], axis=0))
            gather[run] += dot_nt(jnp.concatenate(lhs, axis=1), spot[run, c])

    repeat(chunks, add_group)
    gathered = [gather[run, 0:tiles] + gather[run, tiles:2 * tiles] for run in range(3)]
    right_side = fixed + gathered[1]
    iterate = inverse * right_side
    ext[REACH:REACH + tiles, :] = iterate
    for side, run, lo, at in ((0, 0, tiles - REACH, 0), (1, 2, 0, tiles + REACH)):
        fixed_near = pre_in[side, senders:senders + REACH, :]
        inverse_near = pre_in[side, senders + REACH:senders + 2 * REACH, :]
        ext[at:at + REACH, :] = inverse_near * (fixed_near + gathered[run][lo:lo + REACH])

    def couple(slot, pairs_of):
        for t, offsets in pairs_of:
            total = None
            for o in offsets:
                term = blocks[0, t, o] * ext[t + o:t + o + 1, :]
                total = term if total is None else total + term
            high, low = split(total)
            summed = dot(jnp.concatenate([high, low], axis=1), ones)
            sums[slot, t:t + 1, :] = jnp.sum(jnp.where(eye, summed, 0.0), axis=0, keepdims=True)

    def inside(t, o):
        return 0 <= t + o - REACH < tiles

    every = list(range(NB))
    edge = [(t, every) for t in range(tiles) if t < REACH or t >= tiles - REACH]
    middle = [(t, every) for t in range(tiles) if REACH <= t < tiles - REACH]
    local = [(t, [o for o in every if inside(t, o)]) for t in range(tiles)]
    outer = [(t, [o for o in every if not inside(t, o)]) for t in range(tiles)]
    outer = [(t, offsets) for t, offsets in outer if offsets]

    def pass_on(k, values):
        halo_out[k, 0] = values[0:REACH]
        halo_out[k, 1] = values[tiles - REACH:tiles]

        @pl.when(has_left)
        def _():
            halo_l[k].start()

        @pl.when(has_right)
        def _():
            halo_r[k].start()

    def take(k):
        @pl.when(has_left)
        def _():
            halo_r[k].wait_recv()

        @pl.when(has_right)
        def _():
            halo_l[k].wait_recv()

    def meet_first(turn):
        @pl.when(jnp.logical_and(turn, me == 1))
        def _():
            pl.semaphore_wait(barrier, 4)
            for d in range(1, senders):
                pl.semaphore_signal(cross, inc=1, device_id={"gx": lax.rem(me + d, senders)},
                                    device_id_type=MESH)
            for face in faces[2:]:
                face.start()

    def meet_rest(turn):
        @pl.when(jnp.logical_and(turn, me != 1))
        def _():
            pl.semaphore_wait(cross, 1)
            for face in faces[2:]:
                face.start()

    lane = lax.broadcasted_iota(jnp.int32, (cy, cz), 1)
    line = lax.broadcasted_iota(jnp.int32, (cy, cz), 0)

    def stencil(first, last):
        for i in range(first, last):
            here = fluid[i]
            near = jnp.where(line == 0, 0.0, pltpu.roll(here, 1, 0))
            near = near + jnp.where(line == cy - 1, 0.0, pltpu.roll(here, cy - 1, 0))
            near = near + jnp.where(lane == 0, 0.0, pltpu.roll(here, 1, 1))
            near = near + jnp.where(lane == cz - 1, 0.0, pltpu.roll(here, cz - 1, 1))
            if i > 0:
                near = near + fluid[i - 1]
            if i < cx - 1:
                near = near + fluid[i + 1]
            dry = liquid[i].astype(F32) * jnp.maximum(here - SATURATION, 0.0)
            base[i] = here + DIFFUSION * (near - 6.0 * here) - EVAPORATION * dry

    couple(0, edge)
    pass_on(0, iterate + inverse * (right_side - diagonal * iterate - sums[0]))
    couple(0, middle)
    update = inverse * (right_side - diagonal * iterate - sums[0])
    iterate = iterate + update
    rho_old = 0.5
    for k in range(SWEEPS - 1):
        if k > 0:
            pass_on(k, iterate)
        if k == 0:
            meet_first(late)
        if k == SWEEPS - 2:
            meet_first(jnp.logical_not(late))
        rho_next = 1.0 / (4.0 - rho_old)
        ext[REACH:REACH + tiles, :] = iterate
        couple(0, local)
        part = right_side - diagonal * iterate - sums[0]
        if k == 0:
            loads[7].wait()
            stencil(0, cx // 2)
            meet_rest(late)
        if k == 1:
            stencil(cx // 2, cx)
        if k == SWEEPS - 2:
            for face in faces[0:2]:
                face.wait_recv()
            base[0] += DIFFUSION * x_in[0]
            base[cx - 1] += DIFFUSION * x_in[1]
            meet_rest(jnp.logical_not(late))
        take(k)
        ext[0:REACH, :] = halo[k, 0]
        ext[tiles + REACH:tiles + 2 * REACH, :] = halo[k, 1]
        couple(1, outer)
        residual = part - sums[1]
        update = rho_next * rho_old * update + 4.0 * rho_next * inverse * residual
        iterate = iterate + update
        rho_old = rho_next

    high, low = split(iterate)
    both = jnp.concatenate([high, low], axis=0)

    def pick_back(c):
        picked = dot(both, spot[1, c])
        picked = picked[0:tiles] + picked[tiles:2 * tiles]
        for j in range(group):
            row = dst[c * group + j, 0] >> 7
            part = jnp.where(rows_of((tiles, width)) == row, picked[:, j * width:(j + 1) * width], 0.0)
            sent[c * group + j] = jnp.sum(part, axis=0, keepdims=True)

    repeat(chunks, pick_back)
    backs = []
    for d in range(1, senders):
        peer = lax.rem(me + d, senders)
        backs.append(send(sent.at[peer], ret.at[me], ret_send.at[d], ret_recv.at[d], {"gx": peer}))
        backs[-1].start()
    ret[pl.ds(me, 1)] = sent[pl.ds(me, 1)]
    solid[0] = iterate

    for face in faces[2:]:
        face.wait_recv()
    base[:, 0, :] += DIFFUSION * y_in[0]
    base[:, cy - 1, :] += DIFFUSION * y_in[1]
    deep = rows_of((cz, 128))
    for s in range(rows // 128):
        cut = slice(s * 128, (s + 1) * 128)
        layer = jnp.where(deep == 0, z_in[0, :, cut], 0.0)
        layer = layer + jnp.where(deep == cz - 1, z_in[1, :, cut], 0.0)
        base[s * per:(s + 1) * per] += DIFFUSION * layer.T.reshape(per, cy, cz)

    for copy in arrivals + faces:
        copy.wait_send()

    @pl.when(has_left)
    def _():
        for copy in [pre_l] + halo_l:
            copy.wait_send()

    @pl.when(has_right)
    def _():
        for copy in [pre_r] + halo_r:
            copy.wait_send()

    for copy in backs:
        copy.wait()
    wall[...] = WALL_COUPLING * (ret[...] - outp[1:senders + 1])


def finish(group, base, hot, src, wall, solid, new_h, solid_h, new, sems):
    cx, cy, cz = base.shape
    rows = cx * cy
    chunks, width = hot.shape[0], src.shape[-1]
    solid_copy = pltpu.make_async_copy(solid, solid_h, sems.at[0])
    solid_copy.start()

    def placed_of(c):
        halves = []
        for j in range(group):
            q = c * group + j
            placed = jnp.where(rows_of((cz, width)) == src[q, 0] & (cz - 1), wall[q], 0.0)
            halves.append(jnp.concatenate(split(placed), axis=0))
        return jnp.concatenate(halves, axis=1)

    step = rows // 4
    cuts = [slice(s * step // cy, (s + 1) * step // cy) for s in range(4)]

    def added(c, s, placed):
        both = dot_nt(hot[c, s * step:(s + 1) * step, :], placed)
        return (both[:, 0:cz] + both[:, cz:2 * cz]).reshape(step // cy, cy, cz)

    if chunks > 1:
        def add_chunk(c):
            placed = placed_of(c)
            for s in range(4):
                base_now = jnp.where(c == 0, base[cuts[s]], new[cuts[s]])
                new[cuts[s]] = base_now + added(c, s, placed)

        pl.loop(0, chunks)(add_chunk)
    else:
        placed = placed_of(0)
    copies = []
    for s in range(4):
        if chunks == 1:
            new[cuts[s]] = base[cuts[s]] + added(0, s, placed)
        copies.append(pltpu.make_async_copy(new.at[cuts[s]], new_h.at[cuts[s]], sems.at[s + 1]))
        copies[-1].start()
    for copy in [solid_copy] + copies:
        copy.wait()


def per_device(fluid_temp, liquid, face_src, face_dst, solid_old, solid_diag, blocks, pattern):
    senders = lax.axis_size("gx")
    group = 2 if senders % 2 == 0 else 1
    chunks = senders // group
    cx, cy, cz = fluid_temp.shape
    rows = cx * cy
    tiles, width = solid_old.shape[1:]
    pre_rows = (senders + 2 * REACH + 7) // 8 * 8
    ext_rows = (tiles + 2 * REACH + 7) // 8 * 8
    dma = pltpu.SemaphoreType.DMA
    pattern = jnp.transpose(pattern, (2, 0, 1))
    args = (fluid_temp, liquid, face_src, face_dst, solid_old, solid_diag, blocks, pattern)
    args = tuple(pltpu.with_memory_space_constraint(a, pltpu.HBM) for a in args)
    scratch = [pltpu.VMEM(a.shape, a.dtype)
               for a in (fluid_temp, liquid, face_dst, solid_old, solid_diag, blocks, pattern)]
    scratch += [
        pltpu.VMEM((3, chunks, width, group * width), BF16),
        pltpu.VMEM((2 * cz, rows), BF16),
        pltpu.VMEM((senders + 2, 1, width), F32),
        pltpu.VMEM((senders, 3, 1, width), F32),
        pltpu.VMEM((senders, 1, width), F32),
        pltpu.VMEM((senders, 1, width), F32),
        pltpu.VMEM((2, pre_rows, width), F32),
        pltpu.VMEM((2, pre_rows, width), F32),
        pltpu.VMEM((SWEEPS - 1, 2, REACH, width), F32),
        pltpu.VMEM((SWEEPS - 1, 2, REACH, width), F32),
        pltpu.VMEM((2, cy, cz), F32),
        pltpu.VMEM((2, cx, cz), F32),
        pltpu.VMEM((2, cx, cz), F32),
        pltpu.VMEM((2, 1, rows), F32),
        pltpu.VMEM((2, 1, rows), F32),
        pltpu.VMEM((ext_rows, width), F32),
        pltpu.VMEM((3, 2 * tiles, width), F32),
        pltpu.VMEM((2, tiles, width), F32),
        dma((8,)),
        dma((senders,)), dma((senders,)),
        dma((senders,)), dma((senders,)),
        dma((2,)), dma((2,)),
        dma((SWEEPS - 1, 2)), dma((SWEEPS - 1, 2)),
        dma((6,)), dma((6,)),
        pltpu.SemaphoreType.REGULAR, pltpu.SemaphoreType.REGULAR,
    ]
    parts = pl.pallas_call(
        functools.partial(kernel, senders, group),
        out_shape=(
            pltpu.VMEM(fluid_temp.shape, F32),
            pltpu.VMEM((chunks, rows, group * width), BF16),
            pltpu.VMEM(face_src.shape, jnp.int32),
            pltpu.VMEM((senders, 1, width), F32),
            pltpu.VMEM(solid_old.shape, F32),
        ),
        in_specs=[pl.BlockSpec(memory_space=pltpu.HBM)] * 8,
        out_specs=(pl.BlockSpec(memory_space=pltpu.VMEM),) * 5,
        scratch_shapes=scratch,
        compiler_params=pltpu.CompilerParams(
            collective_id=0, has_side_effects=True, vmem_limit_bytes=24 * 1024 * 1024
        ),
    )(*args)
    parts = tuple(pltpu.with_memory_space_constraint(p, pltpu.VMEM) for p in parts)
    return pl.pallas_call(
        functools.partial(finish, group),
        out_shape=(
            jax.ShapeDtypeStruct(fluid_temp.shape, F32),
            jax.ShapeDtypeStruct(solid_old.shape, F32),
        ),
        in_specs=[pl.BlockSpec(memory_space=pltpu.VMEM)] * 5,
        out_specs=(pl.BlockSpec(memory_space=pl.ANY),) * 2,
        scratch_shapes=[pltpu.VMEM(fluid_temp.shape, F32), dma((5,))],
        compiler_params=pltpu.CompilerParams(vmem_limit_bytes=16 * 1024 * 1024),
    )(*parts)


def solution(mesh):
    return jax.shard_map(
        per_device,
        mesh=mesh,
        in_specs=(
            P("gx", "gy", "gz"),
            P("gx", "gy", "gz"),
            P("gx", "gy", "gz", None),
            P("gx", "gy", "gz", None),
            P(("gy", "gz"), "gx", None),
            P(("gy", "gz"), "gx", None),
            P(("gy", "gz"), "gx", None, None, None),
            P(("gy", "gz"), "gx", None),
        ),
        out_specs=(P("gx", "gy", "gz"), P(("gy", "gz"), "gx", None)),
        check_vma=False,
    )
```

```python
import functools

import jax
import jax.numpy as jnp
from jax import lax
from jax.experimental import pallas as pl
from jax.experimental.pallas import tpu as pltpu
from jax.sharding import PartitionSpec as P

REACH = 2
SWEEPS = 4
NB = 5
DIFFUSION = 0.12
EVAPORATION = 0.5
SATURATION = 0.25
WALL_COUPLING = 0.2
MESH = pl.DeviceIdType.MESH
F32 = jnp.float32
BF16 = jnp.bfloat16


def split(values):
    high = values.astype(BF16)
    return high, (values - high.astype(F32)).astype(BF16)


def dot(a, b):
    return jnp.dot(a, b, preferred_element_type=F32)


def dot_nt(a, b):
    return lax.dot_general(a, b, (((1,), (1,)), ((), ())), preferred_element_type=F32)


def rows_of(shape):
    return lax.broadcasted_iota(jnp.int32, shape, 0)


def repeat(count, body):
    if count == 1:
        body(0)
    else:
        pl.loop(0, count)(body)


def kernel(
    senders, group,
    fluid_h, liquid_h, src_h, dst_h, old_h, diag_h, blocks_h, pat_h,
    base, hot, src, wall, solid,
    fluid, liquid, dst, old, diag, blocks, pat,
    spot, table, outp, arr, sent, ret, pre_out, pre_in, halo_out, halo,
    x_in, y_out, y_in, z_out, z_in, ext, gather, sums,
    load_sem, arr_send, arr_recv, ret_send, ret_recv, pre_send, pre_recv,
    halo_send, halo_recv, face_send, face_recv, go, cross, near,
):
    cx, cy, cz = fluid.shape
    rows = cx * cy
    tiles, width = old.shape[1], old.shape[2]
    chunks = senders // group
    me = lax.axis_index("gx")
    gy, gz = lax.axis_index("gy"), lax.axis_index("gz")
    ny, nz = lax.axis_size("gy"), lax.axis_size("gz")
    left, right = lax.rem(me + senders - 1, senders), lax.rem(me + 1, senders)
    below, above = lax.rem(gy + ny - 1, ny), lax.rem(gy + 1, ny)
    before, after = lax.rem(gz + nz - 1, nz), lax.rem(gz + 1, nz)
    has_left, has_right = me > 0, me < senders - 1
    late = lax.rem(gz, 2) == 1
    early = jnp.logical_not(late)
    barrier = pltpu.get_barrier_semaphore()

    def signal(semaphore, device):
        pl.semaphore_signal(semaphore, inc=1, device_id=device, device_id_type=MESH)

    @pl.when(late)
    def _():
        for d in range(1, senders):
            signal(barrier, {"gx": lax.rem(me + d, senders)})
        signal(barrier, {"gy": below})
        signal(barrier, {"gy": above})

    @pl.when(early)
    def _():
        signal(barrier, {"gz": before})
        signal(barrier, {"gz": after})

    @pl.when(jnp.logical_and(early, me != 0))
    def _():
        signal(barrier, {"gx": 0})

    pairs = [(src_h, src), (fluid_h, fluid), (dst_h, dst), (old_h, old), (diag_h, diag),
             (pat_h, pat), (blocks_h, blocks), (liquid_h, liquid)]
    loads = [pltpu.make_async_copy(a, b, load_sem.at[i]) for i, (a, b) in enumerate(pairs)]
    for load in loads:
        load.start()

    def send(source, target, send_sem, recv_sem, device):
        return pltpu.make_async_remote_copy(
            src_ref=source, dst_ref=target, send_sem=send_sem, recv_sem=recv_sem,
            device_id=device, device_id_type=MESH)

    outp[...] = jnp.zeros_like(outp)
    ext[...] = jnp.zeros_like(ext)
    sums[...] = jnp.zeros_like(sums)
    loads[0].wait()

    def make_hot(c):
        for j in range(group):
            row = src[c * group + j, 0] >> 7
            for s in range(0, rows, 128):
                hit = rows_of((128, width)) + s == row
                hot[c, s:s + 128, j * width:(j + 1) * width] = jnp.where(hit, 1.0, 0.0).astype(BF16)

    repeat(chunks, make_hot)

    @pl.when(jnp.logical_and(early, me == 0))
    def _():
        pl.semaphore_wait(barrier, senders - 1)
        for d in range(1, senders):
            signal(go, {"gx": d})

    for load in loads[2:5]:
        load.wait()
    diagonal = diag[0]
    inverse = 1.0 / diagonal
    fixed = diagonal * old[0]
    for side, lo in ((0, 0), (1, tiles - REACH)):
        for q in range(senders):
            pre_out[side, q:q + 1, :] = dst[q, 0].astype(F32)
        pre_out[side, senders:senders + REACH, :] = fixed[lo:lo + REACH]
        pre_out[side, senders + REACH:senders + 2 * REACH, :] = inverse[lo:lo + REACH]

    loads[1].wait()
    per = 128 // cy
    for s in range(rows // 128):
        flipped = fluid[s * per:(s + 1) * per].reshape(128, cz).T
        high, low = split(flipped)
        table[0:cz, s * 128:(s + 1) * 128] = high
        table[cz:2 * cz, s * 128:(s + 1) * 128] = low
        z_out[0, :, s * 128:(s + 1) * 128] = flipped[0:1]
        z_out[1, :, s * 128:(s + 1) * 128] = flipped[cz - 1:cz]

    def pick(c):
        picked = dot(table[...], hot[c])
        picked = picked[0:cz] + picked[cz:2 * cz]
        for j in range(group):
            depth = src[c * group + j, 0] & (cz - 1)
            part = picked[:, j * width:(j + 1) * width]
            part = jnp.where(rows_of((cz, width)) == depth, part, 0.0)
            outp[c * group + j + 1] = jnp.sum(part, axis=0, keepdims=True)

    repeat(chunks, pick)

    @pl.when(late)
    def _():
        pl.semaphore_wait(barrier, senders + 3)
        signal(near, {"gz": before})
        signal(near, {"gz": after})

    @pl.when(jnp.logical_and(early, me != 0))
    def _():
        pl.semaphore_wait(go, 1)

    @pl.when(jnp.logical_and(early, me == 1))
    def _():
        signal(barrier, {"gy": below})
        signal(barrier, {"gy": above})

    pre_l = send(pre_out.at[0], pre_in.at[1], pre_send.at[0], pre_recv.at[1], {"gx": left})
    pre_r = send(pre_out.at[1], pre_in.at[0], pre_send.at[1], pre_recv.at[0], {"gx": right})
    halo_l = [send(halo_out.at[k, 0], halo.at[k, 1], halo_send.at[k, 0], halo_recv.at[k, 1],
                   {"gx": left}) for k in range(SWEEPS - 1)]
    halo_r = [send(halo_out.at[k, 1], halo.at[k, 0], halo_send.at[k, 1], halo_recv.at[k, 0],
                   {"gx": right}) for k in range(SWEEPS - 1)]
    arrivals = []
    for d in range(1, senders):
        peer = lax.rem(me + d, senders)
        arrivals.append(send(outp.at[pl.ds(peer, 3)], arr.at[me], arr_send.at[d], arr_recv.at[d],
                             {"gx": peer}))

    @pl.when(has_left)
    def _():
        pre_l.start()

    @pl.when(has_right)
    def _():
        pre_r.start()

    for copy in arrivals:
        copy.start()
    y_out[0] = fluid[:, 0, :]
    y_out[1] = fluid[:, cy - 1, :]
    faces = [
        send(fluid.at[0], x_in.at[1], face_send.at[0], face_recv.at[0], {"gx": left}),
        send(fluid.at[cx - 1], x_in.at[0], face_send.at[1], face_recv.at[1], {"gx": right}),
        send(y_out.at[0], y_in.at[1], face_send.at[2], face_recv.at[2], {"gy": below}),
        send(y_out.at[1], y_in.at[0], face_send.at[3], face_recv.at[3], {"gy": above}),
        send(z_out.at[0], z_in.at[1], face_send.at[4], face_recv.at[4], {"gz": before}),
        send(z_out.at[1], z_in.at[0], face_send.at[5], face_recv.at[5], {"gz": after}),
    ]

    @pl.when(late)
    def _():
        for face in faces[2:]:
            face.start()

    for face in faces[0:2]:
        face.start()
    arr[pl.ds(me, 1)] = outp[pl.ds(me, 3)][None]

    @pl.when(jnp.logical_not(has_left))
    def _():
        pre_in[0] = jnp.zeros_like(pre_in[0])
        for k in range(SWEEPS - 1):
            halo[k, 0] = jnp.zeros_like(halo[k, 0])

    @pl.when(jnp.logical_not(has_right))
    def _():
        pre_in[1] = jnp.zeros_like(pre_in[1])
        for k in range(SWEEPS - 1):
            halo[k, 1] = jnp.zeros_like(halo[k, 1])

    for load in loads[5:7]:
        load.wait()
    small = rows_of((tiles, tiles)) == lax.broadcasted_iota(jnp.int32, (tiles, tiles), 1)
    for o in range(NB):
        row = jnp.broadcast_to(pat[o].astype(F32), (tiles, tiles))
        column = jnp.sum(jnp.where(small, row, 0.0), axis=1, keepdims=True)
        mask = jnp.broadcast_to(column, (tiles, width))
        for t in range(tiles):
            blocks[0, t, o] = blocks[0, t, o] * mask[t:t + 1]

    @pl.when(has_left)
    def _():
        send(pre_out.at[1], pre_in.at[0], pre_send.at[1], pre_recv.at[0], {"gx": left}).wait_recv()

    @pl.when(has_right)
    def _():
        send(pre_out.at[0], pre_in.at[1], pre_send.at[0], pre_recv.at[1], {"gx": right}).wait_recv()

    def ids_at(run, q):
        if run == 1:
            return dst[q, 0]
        return pre_in[run // 2, pl.ds(q, 1), :].astype(jnp.int32)

    def make_spot(c):
        for run in range(3):
            for j in range(group):
                hit = rows_of((width, width)) == ids_at(run, c * group + j) & (width - 1)
                spot[run, c, :, j * width:(j + 1) * width] = jnp.where(hit, 1.0, 0.0).astype(BF16)

    repeat(chunks, make_spot)
    ones = jnp.ones((2 * width, width), BF16)
    eye = rows_of((width, width)) == lax.broadcasted_iota(jnp.int32, (width, width), 1)
    for copy in arrivals:
        copy.wait_recv()

    gather[...] = jnp.zeros_like(gather)

    def add_group(c):
        for run in range(3):
            lhs = []
            for j in range(group):
                q = c * group + j
                hit = rows_of((tiles, width)) == ids_at(run, q) >> 7
                high, low = split(jnp.where(hit, arr[q, run], 0.0))
                lhs.append(jnp.concatenate([high, low], axis=0))
            gather[run] += dot_nt(jnp.concatenate(lhs, axis=1), spot[run, c])

    repeat(chunks, add_group)
    gathered = [gather[run, 0:tiles] + gather[run, tiles:2 * tiles] for run in range(3)]
    right_side = fixed + gathered[1]
    iterate = inverse * right_side
    ext[REACH:REACH + tiles, :] = iterate
    for side, run, lo, at in ((0, 0, tiles - REACH, 0), (1, 2, 0, tiles + REACH)):
        fixed_near = pre_in[side, senders:senders + REACH, :]
        inverse_near = pre_in[side, senders + REACH:senders + 2 * REACH, :]
        ext[at:at + REACH, :] = inverse_near * (fixed_near + gathered[run][lo:lo + REACH])

    def couple(slot, pairs_of):
        for t, offsets in pairs_of:
            total = None
            for o in offsets:
                term = blocks[0, t, o] * ext[t + o:t + o + 1, :]
                total = term if total is None else total + term
            high, low = split(total)
            summed = dot(jnp.concatenate([high, low], axis=1), ones)
            sums[slot, t:t + 1, :] = jnp.sum(jnp.where(eye, summed, 0.0), axis=0, keepdims=True)

    def inside(t, o):
        return 0 <= t + o - REACH < tiles

    every = list(range(NB))
    edge = [(t, every) for t in range(tiles) if t < REACH or t >= tiles - REACH]
    middle = [(t, every) for t in range(tiles) if REACH <= t < tiles - REACH]
    local = [(t, [o for o in every if inside(t, o)]) for t in range(tiles)]
    outer = [(t, [o for o in every if not inside(t, o)]) for t in range(tiles)]
    outer = [(t, offsets) for t, offsets in outer if offsets]

    def pass_on(k, values):
        halo_out[k, 0] = values[0:REACH]
        halo_out[k, 1] = values[tiles - REACH:tiles]

        @pl.when(has_left)
        def _():
            halo_l[k].start()

        @pl.when(has_right)
        def _():
            halo_r[k].start()

    def take(k):
        @pl.when(has_left)
        def _():
            halo_r[k].wait_recv()

        @pl.when(has_right)
        def _():
            halo_l[k].wait_recv()

    def meet_first():
        @pl.when(jnp.logical_and(early, me == 1))
        def _():
            pl.semaphore_wait(barrier, 2)
            for d in range(1, senders):
                signal(cross, {"gx": lax.rem(me + d, senders)})
            for face in faces[2:4]:
                face.start()

    def meet_rest():
        @pl.when(jnp.logical_and(early, me != 1))
        def _():
            pl.semaphore_wait(cross, 1)
            for face in faces[2:4]:
                face.start()

    lane = lax.broadcasted_iota(jnp.int32, (cy, cz), 1)
    line = lax.broadcasted_iota(jnp.int32, (cy, cz), 0)

    def stencil(first, last):
        for i in range(first, last):
            here = fluid[i]
            near = jnp.where(line == 0, 0.0, pltpu.roll(here, 1, 0))
            near = near + jnp.where(line == cy - 1, 0.0, pltpu.roll(here, cy - 1, 0))
            near = near + jnp.where(lane == 0, 0.0, pltpu.roll(here, 1, 1))
            near = near + jnp.where(lane == cz - 1, 0.0, pltpu.roll(here, cz - 1, 1))
            if i > 0:
                near = near + fluid[i - 1]
            if i < cx - 1:
                near = near + fluid[i + 1]
            dry = liquid[i].astype(F32) * jnp.maximum(here - SATURATION, 0.0)
            base[i] = here + DIFFUSION * (near - 6.0 * here) - EVAPORATION * dry

    couple(0, edge)
    pass_on(0, iterate + inverse * (right_side - diagonal * iterate - sums[0]))
    couple(0, middle)
    update = inverse * (right_side - diagonal * iterate - sums[0])
    iterate = iterate + update
    rho_old = 0.5
    for k in range(SWEEPS - 1):
        if k > 0:
            pass_on(k, iterate)
        if k == 1:
            meet_first()
        rho_next = 1.0 / (4.0 - rho_old)
        ext[REACH:REACH + tiles, :] = iterate
        couple(0, local)
        part = right_side - diagonal * iterate - sums[0]
        if k == 0:
            loads[7].wait()
            stencil(0, cx // 2)
        if k == 1:
            stencil(cx // 2, cx)
            meet_rest()
        if k == SWEEPS - 2:
            for face in faces[0:2]:
                face.wait_recv()
            base[0] += DIFFUSION * x_in[0]
            base[cx - 1] += DIFFUSION * x_in[1]
        take(k)
        ext[0:REACH, :] = halo[k, 0]
        ext[tiles + REACH:tiles + 2 * REACH, :] = halo[k, 1]
        couple(1, outer)
        residual = part - sums[1]
        update = rho_next * rho_old * update + 4.0 * rho_next * inverse * residual
        iterate = iterate + update
        rho_old = rho_next

    high, low = split(iterate)
    both = jnp.concatenate([high, low], axis=0)

    def pick_back(c):
        picked = dot(both, spot[1, c])
        picked = picked[0:tiles] + picked[tiles:2 * tiles]
        for j in range(group):
            row = dst[c * group + j, 0] >> 7
            part = jnp.where(rows_of((tiles, width)) == row, picked[:, j * width:(j + 1) * width], 0.0)
            sent[c * group + j] = jnp.sum(part, axis=0, keepdims=True)

    repeat(chunks, pick_back)
    backs = []
    for d in range(1, senders):
        peer = lax.rem(me + d, senders)
        backs.append(send(sent.at[peer], ret.at[me], ret_send.at[d], ret_recv.at[d], {"gx": peer}))
        backs[-1].start()

    @pl.when(early)
    def _():
        pl.semaphore_wait(near, 2)
        for face in faces[4:]:
            face.start()

    ret[pl.ds(me, 1)] = sent[pl.ds(me, 1)]
    solid[0] = iterate

    for face in faces[2:]:
        face.wait_recv()
    base[:, 0, :] += DIFFUSION * y_in[0]
    base[:, cy - 1, :] += DIFFUSION * y_in[1]
    deep = rows_of((cz, 128))
    for s in range(rows // 128):
        cut = slice(s * 128, (s + 1) * 128)
        layer = jnp.where(deep == 0, z_in[0, :, cut], 0.0)
        layer = layer + jnp.where(deep == cz - 1, z_in[1, :, cut], 0.0)
        base[s * per:(s + 1) * per] += DIFFUSION * layer.T.reshape(per, cy, cz)

    for copy in arrivals + faces:
        copy.wait_send()

    @pl.when(has_left)
    def _():
        for copy in [pre_l] + halo_l:
            copy.wait_send()

    @pl.when(has_right)
    def _():
        for copy in [pre_r] + halo_r:
            copy.wait_send()

    for copy in backs:
        copy.wait()
    wall[...] = WALL_COUPLING * (ret[...] - outp[1:senders + 1])


def finish(group, base, hot, src, wall, solid, new_h, solid_h, new, sems):
    cx, cy, cz = base.shape
    rows = cx * cy
    chunks, width = hot.shape[0], src.shape[-1]
    solid_copy = pltpu.make_async_copy(solid, solid_h, sems.at[0])
    solid_copy.start()

    def placed_of(c):
        halves = []
        for j in range(group):
            q = c * group + j
            placed = jnp.where(rows_of((cz, width)) == src[q, 0] & (cz - 1), wall[q], 0.0)
            halves.append(jnp.concatenate(split(placed), axis=0))
        return jnp.concatenate(halves, axis=1)

    step = rows // 4
    cuts = [slice(s * step // cy, (s + 1) * step // cy) for s in range(4)]

    def added(c, s, placed):
        both = dot_nt(hot[c, s * step:(s + 1) * step, :], placed)
        return (both[:, 0:cz] + both[:, cz:2 * cz]).reshape(step // cy, cy, cz)

    if chunks > 1:
        def add_chunk(c):
            placed = placed_of(c)
            for s in range(4):
                base_now = jnp.where(c == 0, base[cuts[s]], new[cuts[s]])
                new[cuts[s]] = base_now + added(c, s, placed)

        pl.loop(0, chunks)(add_chunk)
    else:
        placed = placed_of(0)
    copies = []
    for s in range(4):
        if chunks == 1:
            new[cuts[s]] = base[cuts[s]] + added(0, s, placed)
        copies.append(pltpu.make_async_copy(new.at[cuts[s]], new_h.at[cuts[s]], sems.at[s + 1]))
        copies[-1].start()
    for copy in [solid_copy] + copies:
        copy.wait()


def per_device(fluid_temp, liquid, face_src, face_dst, solid_old, solid_diag, blocks, pattern):
    senders = lax.axis_size("gx")
    group = 2 if senders % 2 == 0 else 1
    chunks = senders // group
    cx, cy, cz = fluid_temp.shape
    rows = cx * cy
    tiles, width = solid_old.shape[1:]
    pre_rows = (senders + 2 * REACH + 7) // 8 * 8
    ext_rows = (tiles + 2 * REACH + 7) // 8 * 8
    dma = pltpu.SemaphoreType.DMA
    pattern = jnp.transpose(pattern, (2, 0, 1))
    args = (fluid_temp, liquid, face_src, face_dst, solid_old, solid_diag, blocks, pattern)
    args = tuple(pltpu.with_memory_space_constraint(a, pltpu.HBM) for a in args)
    scratch = [pltpu.VMEM(a.shape, a.dtype)
               for a in (fluid_temp, liquid, face_dst, solid_old, solid_diag, blocks, pattern)]
    scratch += [
        pltpu.VMEM((3, chunks, width, group * width), BF16),
        pltpu.VMEM((2 * cz, rows), BF16),
        pltpu.VMEM((senders + 2, 1, width), F32),
        pltpu.VMEM((senders, 3, 1, width), F32),
        pltpu.VMEM((senders, 1, width), F32),
        pltpu.VMEM((senders, 1, width), F32),
        pltpu.VMEM((2, pre_rows, width), F32),
        pltpu.VMEM((2, pre_rows, width), F32),
        pltpu.VMEM((SWEEPS - 1, 2, REACH, width), F32),
        pltpu.VMEM((SWEEPS - 1, 2, REACH, width), F32),
        pltpu.VMEM((2, cy, cz), F32),
        pltpu.VMEM((2, cx, cz), F32),
        pltpu.VMEM((2, cx, cz), F32),
        pltpu.VMEM((2, 1, rows), F32),
        pltpu.VMEM((2, 1, rows), F32),
        pltpu.VMEM((ext_rows, width), F32),
        pltpu.VMEM((3, 2 * tiles, width), F32),
        pltpu.VMEM((2, tiles, width), F32),
        dma((8,)),
        dma((senders,)), dma((senders,)),
        dma((senders,)), dma((senders,)),
        dma((2,)), dma((2,)),
        dma((SWEEPS - 1, 2)), dma((SWEEPS - 1, 2)),
        dma((6,)), dma((6,)),
        pltpu.SemaphoreType.REGULAR, pltpu.SemaphoreType.REGULAR, pltpu.SemaphoreType.REGULAR,
    ]
    parts = pl.pallas_call(
        functools.partial(kernel, senders, group),
        out_shape=(
            pltpu.VMEM(fluid_temp.shape, F32),
            pltpu.VMEM((chunks, rows, group * width), BF16),
            pltpu.VMEM(face_src.shape, jnp.int32),
            pltpu.VMEM((senders, 1, width), F32),
            pltpu.VMEM(solid_old.shape, F32),
        ),
        in_specs=[pl.BlockSpec(memory_space=pltpu.HBM)] * 8,
        out_specs=(pl.BlockSpec(memory_space=pltpu.VMEM),) * 5,
        scratch_shapes=scratch,
        compiler_params=pltpu.CompilerParams(
            collective_id=0, has_side_effects=True, vmem_limit_bytes=24 * 1024 * 1024
        ),
    )(*args)
    parts = tuple(pltpu.with_memory_space_constraint(p, pltpu.VMEM) for p in parts)
    return pl.pallas_call(
        functools.partial(finish, group),
        out_shape=(
            jax.ShapeDtypeStruct(fluid_temp.shape, F32),
            jax.ShapeDtypeStruct(solid_old.shape, F32),
        ),
        in_specs=[pl.BlockSpec(memory_space=pltpu.VMEM)] * 5,
        out_specs=(pl.BlockSpec(memory_space=pl.ANY),) * 2,
        scratch_shapes=[pltpu.VMEM(fluid_temp.shape, F32), dma((5,))],
        compiler_params=pltpu.CompilerParams(vmem_limit_bytes=16 * 1024 * 1024),
    )(*parts)


def solution(mesh):
    return jax.shard_map(
        per_device,
        mesh=mesh,
        in_specs=(
            P("gx", "gy", "gz"),
            P("gx", "gy", "gz"),
            P("gx", "gy", "gz", None),
            P("gx", "gy", "gz", None),
            P(("gy", "gz"), "gx", None),
            P(("gy", "gz"), "gx", None),
            P(("gy", "gz"), "gx", None, None, None),
            P(("gy", "gz"), "gx", None),
        ),
        out_specs=(P("gx", "gy", "gz"), P(("gy", "gz"), "gx", None)),
        check_vma=False,
    )
```

```python
import functools

import jax
import jax.numpy as jnp
from jax import lax
from jax.experimental import pallas as pl
from jax.experimental.pallas import tpu as pltpu
from jax.sharding import PartitionSpec as P

REACH = 2
SWEEPS = 4
NB = 5
DIFFUSION = 0.12
EVAPORATION = 0.5
SATURATION = 0.25
WALL_COUPLING = 0.2
MESH = pl.DeviceIdType.MESH
F32 = jnp.float32
BF16 = jnp.bfloat16


def split(values):
    high = values.astype(BF16)
    return high, (values - high.astype(F32)).astype(BF16)


def dot(a, b):
    return jnp.dot(a, b, preferred_element_type=F32)


def dot_nt(a, b):
    return lax.dot_general(a, b, (((1,), (1,)), ((), ())), preferred_element_type=F32)


def rows_of(shape):
    return lax.broadcasted_iota(jnp.int32, shape, 0)


def repeat(count, body):
    if count == 1:
        body(0)
    else:
        pl.loop(0, count)(body)


def kernel(
    senders, group,
    fluid_h, liquid_h, src_h, dst_h, old_h, diag_h, blocks_h, pat_h,
    base, hot, src, wall, solid,
    fluid, liquid, dst, old, diag, blocks, pat,
    spot, back, table, outp, arr, sent, ret, pre_out, pre_in, halo_out, halo,
    x_in, y_out, y_in, z_out, z_in, ext, gather, sums,
    load_sem, arr_send, arr_recv, ret_send, ret_recv, pre_send, pre_recv,
    halo_send, halo_recv, face_send, face_recv,
):
    cx, cy, cz = fluid.shape
    rows = cx * cy
    tiles, width = old.shape[1], old.shape[2]
    chunks = senders // group
    me = lax.axis_index("gx")
    gy, gz = lax.axis_index("gy"), lax.axis_index("gz")
    ny, nz = lax.axis_size("gy"), lax.axis_size("gz")
    left, right = lax.rem(me + senders - 1, senders), lax.rem(me + 1, senders)
    below, above = lax.rem(gy + ny - 1, ny), lax.rem(gy + 1, ny)
    before, after = lax.rem(gz + nz - 1, nz), lax.rem(gz + 1, nz)
    has_left, has_right = me > 0, me < senders - 1
    barrier = pltpu.get_barrier_semaphore()

    peers = [{"gx": lax.rem(me + d, senders)} for d in range(1, senders)]
    peers += [{"gy": below}, {"gy": above}, {"gz": before}, {"gz": after}]
    for peer in peers:
        pl.semaphore_signal(barrier, inc=1, device_id=peer, device_id_type=MESH)

    pairs = [(src_h, src), (fluid_h, fluid), (dst_h, dst), (old_h, old), (diag_h, diag),
             (pat_h, pat), (blocks_h, blocks), (liquid_h, liquid)]
    loads = [pltpu.make_async_copy(a, b, load_sem.at[i]) for i, (a, b) in enumerate(pairs)]
    for load in loads:
        load.start()

    def send(source, target, send_sem, recv_sem, device):
        return pltpu.make_async_remote_copy(
            src_ref=source, dst_ref=target, send_sem=send_sem, recv_sem=recv_sem,
            device_id=device, device_id_type=MESH)

    outp[...] = jnp.zeros_like(outp)
    ext[...] = jnp.zeros_like(ext)
    sums[...] = jnp.zeros_like(sums)
    loads[0].wait()

    def make_hot(c):
        for j in range(group):
            row = src[c * group + j, 0] >> 7
            for s in range(0, rows, 128):
                hit = rows_of((128, width)) + s == row
                hot[c, s:s + 128, j * width:(j + 1) * width] = jnp.where(hit, 1.0, 0.0).astype(BF16)

    repeat(chunks, make_hot)

    for load in loads[2:5]:
        load.wait()
    diagonal = diag[0]
    inverse = 1.0 / diagonal
    fixed = diagonal * old[0]
    for side, lo in ((0, 0), (1, tiles - REACH)):
        for q in range(senders):
            pre_out[side, q:q + 1, :] = dst[q, 0].astype(F32)
        pre_out[side, senders:senders + REACH, :] = fixed[lo:lo + REACH]
        pre_out[side, senders + REACH:senders + 2 * REACH, :] = inverse[lo:lo + REACH]

    loads[1].wait()
    per = 128 // cy
    for s in range(rows // 128):
        flipped = fluid[s * per:(s + 1) * per].reshape(128, cz).T
        high, low = split(flipped)
        table[0:cz, s * 128:(s + 1) * 128] = high
        table[cz:2 * cz, s * 128:(s + 1) * 128] = low
        z_out[0, :, s * 128:(s + 1) * 128] = flipped[0:1]
        z_out[1, :, s * 128:(s + 1) * 128] = flipped[cz - 1:cz]

    def pick(c):
        picked = dot(table[...], hot[c])
        picked = picked[0:cz] + picked[cz:2 * cz]
        for j in range(group):
            depth = src[c * group + j, 0] & (cz - 1)
            part = picked[:, j * width:(j + 1) * width]
            part = jnp.where(rows_of((cz, width)) == depth, part, 0.0)
            outp[c * group + j + 1] = jnp.sum(part, axis=0, keepdims=True)

    repeat(chunks, pick)

    pl.semaphore_wait(barrier, len(peers))

    pre_l = send(pre_out.at[0], pre_in.at[1], pre_send.at[0], pre_recv.at[1], {"gx": left})
    pre_r = send(pre_out.at[1], pre_in.at[0], pre_send.at[1], pre_recv.at[0], {"gx": right})
    halo_l = [send(halo_out.at[k, 0], halo.at[k, 1], halo_send.at[k, 0], halo_recv.at[k, 1],
                   {"gx": left}) for k in range(SWEEPS - 1)]
    halo_r = [send(halo_out.at[k, 1], halo.at[k, 0], halo_send.at[k, 1], halo_recv.at[k, 0],
                   {"gx": right}) for k in range(SWEEPS - 1)]
    arrivals = []
    for d in range(1, senders):
        peer = lax.rem(me + d, senders)
        arrivals.append(send(outp.at[pl.ds(peer, 3)], arr.at[me], arr_send.at[d], arr_recv.at[d],
                             {"gx": peer}))

    @pl.when(has_left)
    def _():
        pre_l.start()

    @pl.when(has_right)
    def _():
        pre_r.start()

    for copy in arrivals:
        copy.start()
    y_out[0] = fluid[:, 0, :]
    y_out[1] = fluid[:, cy - 1, :]
    faces = [
        send(fluid.at[0], x_in.at[1], face_send.at[0], face_recv.at[0], {"gx": left}),
        send(fluid.at[cx - 1], x_in.at[0], face_send.at[1], face_recv.at[1], {"gx": right}),
        send(y_out.at[0], y_in.at[1], face_send.at[2], face_recv.at[2], {"gy": below}),
        send(y_out.at[1], y_in.at[0], face_send.at[3], face_recv.at[3], {"gy": above}),
        send(z_out.at[0], z_in.at[1], face_send.at[4], face_recv.at[4], {"gz": before}),
        send(z_out.at[1], z_in.at[0], face_send.at[5], face_recv.at[5], {"gz": after}),
    ]
    for face in faces:
        face.start()
    arr[pl.ds(me, 1)] = outp[pl.ds(me, 3)][None]

    @pl.when(jnp.logical_not(has_left))
    def _():
        pre_in[0] = jnp.zeros_like(pre_in[0])

    @pl.when(jnp.logical_not(has_right))
    def _():
        pre_in[1] = jnp.zeros_like(pre_in[1])

    for load in loads[5:7]:
        load.wait()
    small = rows_of((tiles, tiles)) == lax.broadcasted_iota(jnp.int32, (tiles, tiles), 1)
    for o in range(NB):
        row = jnp.broadcast_to(pat[o].astype(F32), (tiles, tiles))
        column = jnp.sum(jnp.where(small, row, 0.0), axis=1, keepdims=True)
        mask = jnp.broadcast_to(column, (tiles, width))
        for t in range(tiles):
            blocks[0, t, o] = blocks[0, t, o] * mask[t:t + 1]

    @pl.when(has_left)
    def _():
        send(pre_out.at[1], pre_in.at[0], pre_send.at[1], pre_recv.at[0], {"gx": left}).wait_recv()

    @pl.when(has_right)
    def _():
        send(pre_out.at[0], pre_in.at[1], pre_send.at[0], pre_recv.at[1], {"gx": right}).wait_recv()

    def ids_at(run, q):
        if run == 1:
            return dst[q, 0]
        return pre_in[run // 2, pl.ds(q, 1), :].astype(jnp.int32)

    def make_spot(c):
        for run in range(3):
            for j in range(group):
                hit = rows_of((width, width)) == ids_at(run, c * group + j) & (width - 1)
                hit = jnp.where(hit, 1.0, 0.0)
                back[run, c, j * width:(j + 1) * width, :] = hit.T.astype(BF16)
                if run == 1:
                    spot[c, :, j * width:(j + 1) * width] = hit.astype(BF16)

    repeat(chunks, make_spot)
    ones = jnp.ones((2 * width, width), BF16)
    eye = rows_of((width, width)) == lax.broadcasted_iota(jnp.int32, (width, width), 1)
    for copy in arrivals:
        copy.wait_recv()

    gather[...] = jnp.zeros_like(gather)

    def add_group(c):
        for run in range(3):
            lhs = []
            for j in range(group):
                q = c * group + j
                hit = rows_of((tiles, width)) == ids_at(run, q) >> 7
                high, low = split(jnp.where(hit, arr[q, run], 0.0))
                lhs.append(jnp.concatenate([high, low], axis=0))
            gather[run] += dot(jnp.concatenate(lhs, axis=1), back[run, c])

    repeat(chunks, add_group)
    gathered = [gather[run, 0:tiles] + gather[run, tiles:2 * tiles] for run in range(3)]
    right_side = fixed + gathered[1]
    iterate = inverse * right_side
    ext[REACH:REACH + tiles, :] = iterate
    for side, run, lo, at in ((0, 0, tiles - REACH, 0), (1, 2, 0, tiles + REACH)):
        fixed_near = pre_in[side, senders:senders + REACH, :]
        inverse_near = pre_in[side, senders + REACH:senders + 2 * REACH, :]
        ext[at:at + REACH, :] = inverse_near * (fixed_near + gathered[run][lo:lo + REACH])

    def couple(slot, pairs_of):
        for t, offsets in pairs_of:
            total = None
            for o in offsets:
                term = blocks[0, t, o] * ext[t + o:t + o + 1, :]
                total = term if total is None else total + term
            high, low = split(total)
            summed = dot(jnp.concatenate([high, low], axis=1), ones)
            sums[slot, t:t + 1, :] = jnp.sum(jnp.where(eye, summed, 0.0), axis=0, keepdims=True)

    def inside(t, o):
        return 0 <= t + o - REACH < tiles

    every = list(range(NB))
    middle = [(t, every) for t in range(REACH, tiles - REACH)]
    local = [(t, [o for o in every if inside(t, o)]) for t in range(tiles)]
    first = [(t, every) for t in range(REACH)]
    last = [(t, every) for t in range(tiles - REACH, tiles)]
    outer_first = [(t, [o for o in every if t + o < REACH]) for t in range(REACH)]
    outer_last = [(t, [o for o in every if t + o >= tiles + REACH]) for t in range(tiles - REACH, tiles)]
    no_left, no_right = jnp.logical_not(has_left), jnp.logical_not(has_right)

    def pass_on(k, values):
        @pl.when(has_left)
        def _():
            halo_out[k, 0] = values[0:REACH]
            halo_l[k].start()

        @pl.when(has_right)
        def _():
            halo_out[k, 1] = values[tiles - REACH:tiles]
            halo_r[k].start()

    def take(k):
        @pl.when(has_left)
        def _():
            halo_r[k].wait_recv()
            ext[0:REACH, :] = halo[k, 0]
            couple(1, outer_first)

        @pl.when(has_right)
        def _():
            halo_l[k].wait_recv()
            ext[tiles + REACH:tiles + 2 * REACH, :] = halo[k, 1]
            couple(1, outer_last)

    lane = lax.broadcasted_iota(jnp.int32, (cy, cz), 1)
    line = lax.broadcasted_iota(jnp.int32, (cy, cz), 0)

    def stencil(first, last):
        for i in range(first, last):
            here = fluid[i]
            near = jnp.where(line == 0, 0.0, pltpu.roll(here, 1, 0))
            near = near + jnp.where(line == cy - 1, 0.0, pltpu.roll(here, cy - 1, 0))
            near = near + jnp.where(lane == 0, 0.0, pltpu.roll(here, 1, 1))
            near = near + jnp.where(lane == cz - 1, 0.0, pltpu.roll(here, cz - 1, 1))
            if i > 0:
                near = near + fluid[i - 1]
            if i < cx - 1:
                near = near + fluid[i + 1]
            dry = liquid[i].astype(F32) * jnp.maximum(here - SATURATION, 0.0)
            base[i] = here + DIFFUSION * (near - 6.0 * here) - EVAPORATION * dry

    def step(lo):
        cut = slice(lo, lo + REACH)
        rest = right_side[cut] - diagonal[cut] * iterate[cut] - sums[0, cut, :]
        return iterate[cut] + inverse[cut] * rest

    @pl.when(has_left)
    def _():
        couple(0, first)
        halo_out[0, 0] = step(0)
        halo_l[0].start()

    @pl.when(has_right)
    def _():
        couple(0, last)
        halo_out[0, 1] = step(tiles - REACH)
        halo_r[0].start()

    @pl.when(no_left)
    def _():
        couple(0, first)

    @pl.when(no_right)
    def _():
        couple(0, last)

    couple(0, middle)
    update = inverse * (right_side - diagonal * iterate - sums[0])
    iterate = iterate + update
    rho_old = 0.5
    for k in range(SWEEPS - 1):
        if k > 0:
            pass_on(k, iterate)
        rho_next = 1.0 / (4.0 - rho_old)
        ext[REACH:REACH + tiles, :] = iterate
        couple(0, local)
        part = right_side - diagonal * iterate - sums[0]
        if k == 0:
            loads[7].wait()
            stencil(0, cx // 2)
        if k == 1:
            stencil(cx // 2, cx)
        if k == SWEEPS - 2:
            for face in faces[0:2]:
                face.wait_recv()
            base[0] += DIFFUSION * x_in[0]
            base[cx - 1] += DIFFUSION * x_in[1]
        take(k)
        residual = part - sums[1]
        update = rho_next * rho_old * update + 4.0 * rho_next * inverse * residual
        iterate = iterate + update
        rho_old = rho_next

    high, low = split(iterate)
    both = jnp.concatenate([high, low], axis=0)

    def pick_back(c):
        picked = dot(both, spot[c])
        picked = picked[0:tiles] + picked[tiles:2 * tiles]
        for j in range(group):
            row = dst[c * group + j, 0] >> 7
            part = jnp.where(rows_of((tiles, width)) == row, picked[:, j * width:(j + 1) * width], 0.0)
            sent[c * group + j] = jnp.sum(part, axis=0, keepdims=True)

    repeat(chunks, pick_back)
    backs = []
    for d in range(1, senders):
        peer = lax.rem(me + d, senders)
        backs.append(send(sent.at[peer], ret.at[me], ret_send.at[d], ret_recv.at[d], {"gx": peer}))
        backs[-1].start()
    ret[pl.ds(me, 1)] = sent[pl.ds(me, 1)]
    solid[0] = iterate

    for face in faces[2:]:
        face.wait_recv()
    base[:, 0, :] += DIFFUSION * y_in[0]
    base[:, cy - 1, :] += DIFFUSION * y_in[1]
    deep = rows_of((cz, 128))
    for s in range(rows // 128):
        cut = slice(s * 128, (s + 1) * 128)
        layer = jnp.where(deep == 0, z_in[0, :, cut], 0.0)
        layer = layer + jnp.where(deep == cz - 1, z_in[1, :, cut], 0.0)
        base[s * per:(s + 1) * per] += DIFFUSION * layer.T.reshape(per, cy, cz)

    for copy in arrivals + faces:
        copy.wait_send()

    @pl.when(has_left)
    def _():
        for copy in [pre_l] + halo_l:
            copy.wait_send()

    @pl.when(has_right)
    def _():
        for copy in [pre_r] + halo_r:
            copy.wait_send()

    for copy in backs:
        copy.wait()
    wall[...] = WALL_COUPLING * (ret[...] - outp[1:senders + 1])


def finish(group, base, hot, src, wall, solid, new_h, solid_h, new, sems):
    cx, cy, cz = base.shape
    rows = cx * cy
    chunks, width = hot.shape[0], src.shape[-1]
    solid_copy = pltpu.make_async_copy(solid, solid_h, sems.at[0])
    solid_copy.start()

    def placed_of(c):
        halves = []
        for j in range(group):
            q = c * group + j
            placed = jnp.where(rows_of((cz, width)) == src[q, 0] & (cz - 1), wall[q], 0.0)
            halves.append(jnp.concatenate(split(placed), axis=0))
        return jnp.concatenate(halves, axis=1)

    step = rows // 4
    cuts = [slice(s * step // cy, (s + 1) * step // cy) for s in range(4)]

    def added(c, s, placed):
        both = dot_nt(hot[c, s * step:(s + 1) * step, :], placed)
        return (both[:, 0:cz] + both[:, cz:2 * cz]).reshape(step // cy, cy, cz)

    if chunks > 1:
        def add_chunk(c):
            placed = placed_of(c)
            for s in range(4):
                base_now = jnp.where(c == 0, base[cuts[s]], new[cuts[s]])
                new[cuts[s]] = base_now + added(c, s, placed)

        pl.loop(0, chunks)(add_chunk)
    else:
        placed = placed_of(0)
    copies = []
    for s in range(4):
        if chunks == 1:
            new[cuts[s]] = base[cuts[s]] + added(0, s, placed)
        copies.append(pltpu.make_async_copy(new.at[cuts[s]], new_h.at[cuts[s]], sems.at[s + 1]))
        copies[-1].start()
    for copy in [solid_copy] + copies:
        copy.wait()


def per_device(fluid_temp, liquid, face_src, face_dst, solid_old, solid_diag, blocks, pattern):
    senders = lax.axis_size("gx")
    group = 2 if senders % 2 == 0 else 1
    chunks = senders // group
    cx, cy, cz = fluid_temp.shape
    rows = cx * cy
    tiles, width = solid_old.shape[1:]
    pre_rows = (senders + 2 * REACH + 7) // 8 * 8
    ext_rows = (tiles + 2 * REACH + 7) // 8 * 8
    dma = pltpu.SemaphoreType.DMA
    pattern = jnp.transpose(pattern, (2, 0, 1))
    args = (fluid_temp, liquid, face_src, face_dst, solid_old, solid_diag, blocks, pattern)
    args = tuple(pltpu.with_memory_space_constraint(a, pltpu.HBM) for a in args)
    scratch = [pltpu.VMEM(a.shape, a.dtype)
               for a in (fluid_temp, liquid, face_dst, solid_old, solid_diag, blocks, pattern)]
    scratch += [
        pltpu.VMEM((chunks, width, group * width), BF16),
        pltpu.VMEM((3, chunks, group * width, width), BF16),
        pltpu.VMEM((2 * cz, rows), BF16),
        pltpu.VMEM((senders + 2, 1, width), F32),
        pltpu.VMEM((senders, 3, 1, width), F32),
        pltpu.VMEM((senders, 1, width), F32),
        pltpu.VMEM((senders, 1, width), F32),
        pltpu.VMEM((2, pre_rows, width), F32),
        pltpu.VMEM((2, pre_rows, width), F32),
        pltpu.VMEM((SWEEPS - 1, 2, REACH, width), F32),
        pltpu.VMEM((SWEEPS - 1, 2, REACH, width), F32),
        pltpu.VMEM((2, cy, cz), F32),
        pltpu.VMEM((2, cx, cz), F32),
        pltpu.VMEM((2, cx, cz), F32),
        pltpu.VMEM((2, 1, rows), F32),
        pltpu.VMEM((2, 1, rows), F32),
        pltpu.VMEM((ext_rows, width), F32),
        pltpu.VMEM((3, 2 * tiles, width), F32),
        pltpu.VMEM((2, tiles, width), F32),
        dma((8,)),
        dma((senders,)), dma((senders,)),
        dma((senders,)), dma((senders,)),
        dma((2,)), dma((2,)),
        dma((SWEEPS - 1, 2)), dma((SWEEPS - 1, 2)),
        dma((6,)), dma((6,)),
    ]
    parts = pl.pallas_call(
        functools.partial(kernel, senders, group),
        out_shape=(
            pltpu.VMEM(fluid_temp.shape, F32),
            pltpu.VMEM((chunks, rows, group * width), BF16),
            pltpu.VMEM(face_src.shape, jnp.int32),
            pltpu.VMEM((senders, 1, width), F32),
            pltpu.VMEM(solid_old.shape, F32),
        ),
        in_specs=[pl.BlockSpec(memory_space=pltpu.HBM)] * 8,
        out_specs=(pl.BlockSpec(memory_space=pltpu.VMEM),) * 5,
        scratch_shapes=scratch,
        compiler_params=pltpu.CompilerParams(
            collective_id=0, has_side_effects=True, vmem_limit_bytes=24 * 1024 * 1024
        ),
    )(*args)
    parts = tuple(pltpu.with_memory_space_constraint(p, pltpu.VMEM) for p in parts)
    return pl.pallas_call(
        functools.partial(finish, group),
        out_shape=(
            jax.ShapeDtypeStruct(fluid_temp.shape, F32),
            jax.ShapeDtypeStruct(solid_old.shape, F32),
        ),
        in_specs=[pl.BlockSpec(memory_space=pltpu.VMEM)] * 5,
        out_specs=(pl.BlockSpec(memory_space=pl.ANY),) * 2,
        scratch_shapes=[pltpu.VMEM(fluid_temp.shape, F32), dma((5,))],
        compiler_params=pltpu.CompilerParams(vmem_limit_bytes=16 * 1024 * 1024),
    )(*parts)


def solution(mesh):
    return jax.shard_map(
        per_device,
        mesh=mesh,
        in_specs=(
            P("gx", "gy", "gz"),
            P("gx", "gy", "gz"),
            P("gx", "gy", "gz", None),
            P("gx", "gy", "gz", None),
            P(("gy", "gz"), "gx", None),
            P(("gy", "gz"), "gx", None),
            P(("gy", "gz"), "gx", None, None, None),
            P(("gy", "gz"), "gx", None),
        ),
        out_specs=(P("gx", "gy", "gz"), P(("gy", "gz"), "gx", None)),
        check_vma=False,
    )
```

```python
import functools

import jax
import jax.numpy as jnp
from jax import lax
from jax.experimental import pallas as pl
from jax.experimental.pallas import tpu as pltpu
from jax.sharding import PartitionSpec as P

REACH = 2
SWEEPS = 4
NB = 5
DIFFUSION = 0.12
EVAPORATION = 0.5
SATURATION = 0.25
WALL_COUPLING = 0.2
MESH = pl.DeviceIdType.MESH
F32 = jnp.float32
BF16 = jnp.bfloat16


def split(values):
    high = values.astype(BF16)
    return high, (values - high.astype(F32)).astype(BF16)


def dot(a, b):
    return jnp.dot(a, b, preferred_element_type=F32)


def dot_nt(a, b):
    return lax.dot_general(a, b, (((1,), (1,)), ((), ())), preferred_element_type=F32)


def rows_of(shape):
    return lax.broadcasted_iota(jnp.int32, shape, 0)


def repeat(count, body):
    if count == 1:
        body(0)
    else:
        pl.loop(0, count)(body)


def kernel(
    senders, group,
    fluid_h, liquid_h, src_h, dst_h, old_h, diag_h, blocks_h, pat_h,
    base, hot, src, wall, solid,
    fluid, liquid, dst, old, diag, blocks, pat,
    spot, back, table, outp, arr, sent, ret, pre_out, pre_in, halo_out, halo,
    x_in, y_out, y_in, z_out, z_in, ext, gather, sums, edge,
    load_sem, arr_send, arr_recv, ret_send, ret_recv, pre_send, pre_recv,
    halo_send, halo_recv, face_send, face_recv, near_sem,
):
    cx, cy, cz = fluid.shape
    rows = cx * cy
    tiles, width = old.shape[1], old.shape[2]
    chunks = senders // group
    me = lax.axis_index("gx")
    gy, gz = lax.axis_index("gy"), lax.axis_index("gz")
    ny, nz = lax.axis_size("gy"), lax.axis_size("gz")
    left, right = lax.rem(me + senders - 1, senders), lax.rem(me + 1, senders)
    below, above = lax.rem(gy + ny - 1, ny), lax.rem(gy + 1, ny)
    before, after = lax.rem(gz + nz - 1, nz), lax.rem(gz + 1, nz)
    has_left, has_right = me > 0, me < senders - 1
    barrier = pltpu.get_barrier_semaphore()

    line_peers = [{"gx": lax.rem(me + d, senders)} for d in range(1, senders)]
    cross_peers = [{"gy": below}, {"gy": above}, {"gz": before}, {"gz": after}]
    odd = lax.rem(gy + gz, 2) == 1
    even = jnp.logical_not(odd)

    def signal(semaphore, device):
        pl.semaphore_signal(semaphore, inc=1, device_id=device, device_id_type=MESH)

    for peer in line_peers:
        signal(barrier, peer)

    @pl.when(even)
    def _():
        for peer in cross_peers:
            signal(barrier, peer)

    pairs = [(src_h, src), (fluid_h, fluid), (dst_h, dst), (old_h, old), (diag_h, diag),
             (pat_h, pat), (blocks_h, blocks), (liquid_h, liquid)]
    loads = [pltpu.make_async_copy(a, b, load_sem.at[i]) for i, (a, b) in enumerate(pairs)]
    for load in loads:
        load.start()

    def send(source, target, send_sem, recv_sem, device):
        return pltpu.make_async_remote_copy(
            src_ref=source, dst_ref=target, send_sem=send_sem, recv_sem=recv_sem,
            device_id=device, device_id_type=MESH)

    outp[...] = jnp.zeros_like(outp)
    ext[...] = jnp.zeros_like(ext)
    sums[...] = jnp.zeros_like(sums)
    loads[0].wait()

    def make_hot(c):
        for j in range(group):
            row = src[c * group + j, 0] >> 7
            for s in range(0, rows, 128):
                hit = rows_of((128, width)) + s == row
                hot[c, s:s + 128, j * width:(j + 1) * width] = jnp.where(hit, 1.0, 0.0).astype(BF16)

    repeat(chunks, make_hot)

    for load in loads[2:5]:
        load.wait()
    diagonal = diag[0]
    inverse = 1.0 / diagonal
    fixed = diagonal * old[0]
    for side, lo in ((0, 0), (1, tiles - REACH)):
        for q in range(senders):
            pre_out[side, q:q + 1, :] = dst[q, 0].astype(F32)
        pre_out[side, senders:senders + REACH, :] = fixed[lo:lo + REACH]
        pre_out[side, senders + REACH:senders + 2 * REACH, :] = inverse[lo:lo + REACH]

    loads[1].wait()
    per = 128 // cy
    for s in range(rows // 128):
        flipped = fluid[s * per:(s + 1) * per].reshape(128, cz).T
        high, low = split(flipped)
        table[0:cz, s * 128:(s + 1) * 128] = high
        table[cz:2 * cz, s * 128:(s + 1) * 128] = low
        z_out[0, :, s * 128:(s + 1) * 128] = flipped[0:1]
        z_out[1, :, s * 128:(s + 1) * 128] = flipped[cz - 1:cz]

    def pick(c):
        picked = dot(table[...], hot[c])
        picked = picked[0:cz] + picked[cz:2 * cz]
        for j in range(group):
            depth = src[c * group + j, 0] & (cz - 1)
            part = picked[:, j * width:(j + 1) * width]
            part = jnp.where(rows_of((cz, width)) == depth, part, 0.0)
            outp[c * group + j + 1] = jnp.sum(part, axis=0, keepdims=True)

    repeat(chunks, pick)

    pl.semaphore_wait(barrier, jnp.where(odd, len(line_peers) + len(cross_peers), len(line_peers)))

    pre_l = send(pre_out.at[0], pre_in.at[1], pre_send.at[0], pre_recv.at[1], {"gx": left})
    pre_r = send(pre_out.at[1], pre_in.at[0], pre_send.at[1], pre_recv.at[0], {"gx": right})
    halo_l = [send(halo_out.at[k, 0], halo.at[k, 1], halo_send.at[k, 0], halo_recv.at[k, 1],
                   {"gx": left}) for k in range(SWEEPS - 1)]
    halo_r = [send(halo_out.at[k, 1], halo.at[k, 0], halo_send.at[k, 1], halo_recv.at[k, 0],
                   {"gx": right}) for k in range(SWEEPS - 1)]
    arrivals = []
    for d in range(1, senders):
        peer = lax.rem(me + d, senders)
        arrivals.append(send(outp.at[pl.ds(peer, 3)], arr.at[me], arr_send.at[d], arr_recv.at[d],
                             {"gx": peer}))

    @pl.when(has_left)
    def _():
        pre_l.start()

    @pl.when(has_right)
    def _():
        pre_r.start()

    for copy in arrivals:
        copy.start()
    y_out[0] = fluid[:, 0, :]
    y_out[1] = fluid[:, cy - 1, :]
    faces = [
        send(fluid.at[0], x_in.at[1], face_send.at[0], face_recv.at[0], {"gx": left}),
        send(fluid.at[cx - 1], x_in.at[0], face_send.at[1], face_recv.at[1], {"gx": right}),
        send(y_out.at[0], y_in.at[1], face_send.at[2], face_recv.at[2], {"gy": below}),
        send(y_out.at[1], y_in.at[0], face_send.at[3], face_recv.at[3], {"gy": above}),
        send(z_out.at[0], z_in.at[1], face_send.at[4], face_recv.at[4], {"gz": before}),
        send(z_out.at[1], z_in.at[0], face_send.at[5], face_recv.at[5], {"gz": after}),
    ]

    @pl.when(odd)
    def _():
        for peer in cross_peers:
            signal(near_sem, peer)
        for face in faces[2:]:
            face.start()

    for face in faces[0:2]:
        face.start()
    arr[pl.ds(me, 1)] = outp[pl.ds(me, 3)][None]

    @pl.when(jnp.logical_not(has_left))
    def _():
        pre_in[0] = jnp.zeros_like(pre_in[0])

    @pl.when(jnp.logical_not(has_right))
    def _():
        pre_in[1] = jnp.zeros_like(pre_in[1])

    for load in loads[5:7]:
        load.wait()
    small = rows_of((tiles, tiles)) == lax.broadcasted_iota(jnp.int32, (tiles, tiles), 1)
    for o in range(NB):
        row = jnp.broadcast_to(pat[o].astype(F32), (tiles, tiles))
        column = jnp.sum(jnp.where(small, row, 0.0), axis=1, keepdims=True)
        mask = jnp.broadcast_to(column, (tiles, width))
        for t in range(tiles):
            blocks[0, t, o] = blocks[0, t, o] * mask[t:t + 1]

    @pl.when(has_left)
    def _():
        send(pre_out.at[1], pre_in.at[0], pre_send.at[1], pre_recv.at[0], {"gx": left}).wait_recv()

    @pl.when(has_right)
    def _():
        send(pre_out.at[0], pre_in.at[1], pre_send.at[0], pre_recv.at[1], {"gx": right}).wait_recv()

    def ids_at(run, q):
        if run == 1:
            return dst[q, 0]
        return pre_in[run // 2, pl.ds(q, 1), :].astype(jnp.int32)

    def make_spot(c):
        for run in range(3):
            for j in range(group):
                hit = rows_of((width, width)) == ids_at(run, c * group + j) & (width - 1)
                hit = jnp.where(hit, 1.0, 0.0)
                back[run, c, j * width:(j + 1) * width, :] = hit.T.astype(BF16)
                if run == 1:
                    spot[c, :, j * width:(j + 1) * width] = hit.astype(BF16)

    repeat(chunks, make_spot)
    ones = jnp.ones((2 * width, width), BF16)
    eye = rows_of((width, width)) == lax.broadcasted_iota(jnp.int32, (width, width), 1)
    for copy in arrivals:
        copy.wait_recv()

    gather[...] = jnp.zeros_like(gather)

    def add_group(c):
        for run in range(3):
            lhs = []
            for j in range(group):
                q = c * group + j
                hit = rows_of((tiles, width)) == ids_at(run, q) >> 7
                high, low = split(jnp.where(hit, arr[q, run], 0.0))
                lhs.append(jnp.concatenate([high, low], axis=0))
            gather[run] += dot(jnp.concatenate(lhs, axis=1), back[run, c])

    repeat(chunks, add_group)
    gathered = [gather[run, 0:tiles] + gather[run, tiles:2 * tiles] for run in range(3)]
    right_side = fixed + gathered[1]
    iterate = inverse * right_side
    ext[REACH:REACH + tiles, :] = iterate
    for side, run, lo, at in ((0, 0, tiles - REACH, 0), (1, 2, 0, tiles + REACH)):
        fixed_near = pre_in[side, senders:senders + REACH, :]
        inverse_near = pre_in[side, senders + REACH:senders + 2 * REACH, :]
        ext[at:at + REACH, :] = inverse_near * (fixed_near + gathered[run][lo:lo + REACH])

    def couple(slot, pairs_of):
        for t, offsets in pairs_of:
            total = None
            for o in offsets:
                term = blocks[0, t, o] * ext[t + o:t + o + 1, :]
                total = term if total is None else total + term
            high, low = split(total)
            summed = dot(jnp.concatenate([high, low], axis=1), ones)
            sums[slot, t:t + 1, :] = jnp.sum(jnp.where(eye, summed, 0.0), axis=0, keepdims=True)

    def inside(t, o):
        return 0 <= t + o - REACH < tiles

    every = list(range(NB))
    middle = [(t, every) for t in range(REACH, tiles - REACH)]
    local = [(t, [o for o in every if inside(t, o)]) for t in range(tiles)]
    first = [(t, every) for t in range(REACH)]
    last = [(t, every) for t in range(tiles - REACH, tiles)]
    no_left, no_right = jnp.logical_not(has_left), jnp.logical_not(has_right)

    sides = ((0, has_left, 0, 0, halo_r, halo_l),
             (1, has_right, tiles - REACH, tiles + REACH, halo_l, halo_r))

    def make_edges():
        for side, has, lo, at, _, _ in sides:
            @pl.when(has)
            def _():
                for i in range(REACH):
                    for j in range(REACH):
                        o = at + i - lo - j
                        block = jnp.zeros((width, width), F32)
                        if 0 <= o < NB:
                            block = blocks[0, lo + j, o].T
                        for part, values in enumerate(split(block)):
                            column = (part * REACH + j) * width
                            edge[side, i * width:(i + 1) * width, column:column + width] = values

    def take(k, part, scale_old, scale_new):
        for side, has, lo, _, copy_in, copy_out in sides:
            @pl.when(has)
            def _():
                copy_in[k].wait_recv()
                flat = jnp.concatenate([halo[k, side, i:i + 1, :] for i in range(REACH)], axis=1)
                high = flat.astype(BF16).astype(F32)
                lhs = [jnp.broadcast_to(v, (8, REACH * width)) for v in (high, flat - high)]
                product = dot(jnp.concatenate(lhs, axis=0).astype(BF16), edge[side])
                product = product[0:1] + product[8:9]
                product = product[:, 0:REACH * width] + product[:, REACH * width:]
                summed = [product[:, j * width:(j + 1) * width] for j in range(REACH)]
                summed = jnp.concatenate(summed, axis=0)
                cut = slice(lo, lo + REACH)
                if k + 1 < SWEEPS - 1:
                    change = scale_old * update[cut] + scale_new * inverse[cut] * (part[cut] - summed)
                    halo_out[k + 1, side] = iterate[cut] + change
                    copy_out[k + 1].start()
                sums[1, cut, :] = summed

    lane = lax.broadcasted_iota(jnp.int32, (cy, cz), 1)
    line = lax.broadcasted_iota(jnp.int32, (cy, cz), 0)

    def stencil(first, last):
        for i in range(first, last):
            here = fluid[i]
            near = jnp.where(line == 0, 0.0, pltpu.roll(here, 1, 0))
            near = near + jnp.where(line == cy - 1, 0.0, pltpu.roll(here, cy - 1, 0))
            near = near + jnp.where(lane == 0, 0.0, pltpu.roll(here, 1, 1))
            near = near + jnp.where(lane == cz - 1, 0.0, pltpu.roll(here, cz - 1, 1))
            if i > 0:
                near = near + fluid[i - 1]
            if i < cx - 1:
                near = near + fluid[i + 1]
            dry = liquid[i].astype(F32) * jnp.maximum(here - SATURATION, 0.0)
            base[i] = here + DIFFUSION * (near - 6.0 * here) - EVAPORATION * dry

    def step(lo):
        cut = slice(lo, lo + REACH)
        rest = right_side[cut] - diagonal[cut] * iterate[cut] - sums[0, cut, :]
        return iterate[cut] + inverse[cut] * rest

    @pl.when(has_left)
    def _():
        couple(0, first)
        halo_out[0, 0] = step(0)
        halo_l[0].start()

    @pl.when(has_right)
    def _():
        couple(0, last)
        halo_out[0, 1] = step(tiles - REACH)
        halo_r[0].start()

    @pl.when(no_left)
    def _():
        couple(0, first)

    @pl.when(no_right)
    def _():
        couple(0, last)

    couple(0, middle)
    update = inverse * (right_side - diagonal * iterate - sums[0])
    iterate = iterate + update
    rho_old = 0.5
    for k in range(SWEEPS - 1):
        rho_next = 1.0 / (4.0 - rho_old)
        ext[REACH:REACH + tiles, :] = iterate
        couple(0, local)
        part = right_side - diagonal * iterate - sums[0]
        if k == 0:
            loads[7].wait()
            stencil(0, cx // 2)
        if k == 1:
            stencil(cx // 2, cx)

            @pl.when(even)
            def _():
                pl.semaphore_wait(near_sem, len(cross_peers))
                for face in faces[2:]:
                    face.start()

        if k == SWEEPS - 2:
            for face in faces[0:2]:
                face.wait_recv()
            base[0] += DIFFUSION * x_in[0]
            base[cx - 1] += DIFFUSION * x_in[1]
        if k == 0:
            make_edges()
        take(k, part, rho_next * rho_old, 4.0 * rho_next)
        residual = part - sums[1]
        update = rho_next * rho_old * update + 4.0 * rho_next * inverse * residual
        iterate = iterate + update
        rho_old = rho_next

    high, low = split(iterate)
    both = jnp.concatenate([high, low], axis=0)

    def pick_back(c):
        picked = dot(both, spot[c])
        picked = picked[0:tiles] + picked[tiles:2 * tiles]
        for j in range(group):
            row = dst[c * group + j, 0] >> 7
            part = jnp.where(rows_of((tiles, width)) == row, picked[:, j * width:(j + 1) * width], 0.0)
            sent[c * group + j] = jnp.sum(part, axis=0, keepdims=True)

    repeat(chunks, pick_back)
    backs = []
    for d in range(1, senders):
        peer = lax.rem(me + d, senders)
        backs.append(send(sent.at[peer], ret.at[me], ret_send.at[d], ret_recv.at[d], {"gx": peer}))
        backs[-1].start()
    ret[pl.ds(me, 1)] = sent[pl.ds(me, 1)]
    solid[0] = iterate

    for face in faces[2:]:
        face.wait_recv()
    base[:, 0, :] += DIFFUSION * y_in[0]
    base[:, cy - 1, :] += DIFFUSION * y_in[1]
    deep = rows_of((cz, 128))
    for s in range(rows // 128):
        cut = slice(s * 128, (s + 1) * 128)
        layer = jnp.where(deep == 0, z_in[0, :, cut], 0.0)
        layer = layer + jnp.where(deep == cz - 1, z_in[1, :, cut], 0.0)
        base[s * per:(s + 1) * per] += DIFFUSION * layer.T.reshape(per, cy, cz)

    for copy in arrivals + faces:
        copy.wait_send()

    @pl.when(has_left)
    def _():
        for copy in [pre_l] + halo_l:
            copy.wait_send()

    @pl.when(has_right)
    def _():
        for copy in [pre_r] + halo_r:
            copy.wait_send()

    for copy in backs:
        copy.wait()
    wall[...] = WALL_COUPLING * (ret[...] - outp[1:senders + 1])


def finish(group, base, hot, src, wall, solid, new_h, solid_h, new, sems):
    cx, cy, cz = base.shape
    rows = cx * cy
    chunks, width = hot.shape[0], src.shape[-1]
    solid_copy = pltpu.make_async_copy(solid, solid_h, sems.at[0])
    solid_copy.start()

    def placed_of(c):
        halves = []
        for j in range(group):
            q = c * group + j
            placed = jnp.where(rows_of((cz, width)) == src[q, 0] & (cz - 1), wall[q], 0.0)
            halves.append(jnp.concatenate(split(placed), axis=0))
        return jnp.concatenate(halves, axis=1)

    step = rows // 4
    cuts = [slice(s * step // cy, (s + 1) * step // cy) for s in range(4)]

    def added(c, s, placed):
        both = dot_nt(hot[c, s * step:(s + 1) * step, :], placed)
        return (both[:, 0:cz] + both[:, cz:2 * cz]).reshape(step // cy, cy, cz)

    if chunks > 1:
        def add_chunk(c):
            placed = placed_of(c)
            for s in range(4):
                base_now = jnp.where(c == 0, base[cuts[s]], new[cuts[s]])
                new[cuts[s]] = base_now + added(c, s, placed)

        pl.loop(0, chunks)(add_chunk)
    else:
        placed = placed_of(0)
    copies = []
    for s in range(4):
        if chunks == 1:
            new[cuts[s]] = base[cuts[s]] + added(0, s, placed)
        copies.append(pltpu.make_async_copy(new.at[cuts[s]], new_h.at[cuts[s]], sems.at[s + 1]))
        copies[-1].start()
    for copy in [solid_copy] + copies:
        copy.wait()


def per_device(fluid_temp, liquid, face_src, face_dst, solid_old, solid_diag, blocks, pattern):
    senders = lax.axis_size("gx")
    group = 2 if senders % 2 == 0 else 1
    chunks = senders // group
    cx, cy, cz = fluid_temp.shape
    rows = cx * cy
    tiles, width = solid_old.shape[1:]
    pre_rows = (senders + 2 * REACH + 7) // 8 * 8
    ext_rows = (tiles + 2 * REACH + 7) // 8 * 8
    dma = pltpu.SemaphoreType.DMA
    pattern = jnp.transpose(pattern, (2, 0, 1))
    args = (fluid_temp, liquid, face_src, face_dst, solid_old, solid_diag, blocks, pattern)
    args = tuple(pltpu.with_memory_space_constraint(a, pltpu.HBM) for a in args)
    scratch = [pltpu.VMEM(a.shape, a.dtype)
               for a in (fluid_temp, liquid, face_dst, solid_old, solid_diag, blocks, pattern)]
    scratch += [
        pltpu.VMEM((chunks, width, group * width), BF16),
        pltpu.VMEM((3, chunks, group * width, width), BF16),
        pltpu.VMEM((2 * cz, rows), BF16),
        pltpu.VMEM((senders + 2, 1, width), F32),
        pltpu.VMEM((senders, 3, 1, width), F32),
        pltpu.VMEM((senders, 1, width), F32),
        pltpu.VMEM((senders, 1, width), F32),
        pltpu.VMEM((2, pre_rows, width), F32),
        pltpu.VMEM((2, pre_rows, width), F32),
        pltpu.VMEM((SWEEPS - 1, 2, REACH, width), F32),
        pltpu.VMEM((SWEEPS - 1, 2, REACH, width), F32),
        pltpu.VMEM((2, cy, cz), F32),
        pltpu.VMEM((2, cx, cz), F32),
        pltpu.VMEM((2, cx, cz), F32),
        pltpu.VMEM((2, 1, rows), F32),
        pltpu.VMEM((2, 1, rows), F32),
        pltpu.VMEM((ext_rows, width), F32),
        pltpu.VMEM((3, 2 * tiles, width), F32),
        pltpu.VMEM((2, tiles, width), F32),
        pltpu.VMEM((2, REACH * width, 2 * REACH * width), BF16),
        dma((8,)),
        dma((senders,)), dma((senders,)),
        dma((senders,)), dma((senders,)),
        dma((2,)), dma((2,)),
        dma((SWEEPS - 1, 2)), dma((SWEEPS - 1, 2)),
        dma((6,)), dma((6,)),
        pltpu.SemaphoreType.REGULAR,
    ]
    parts = pl.pallas_call(
        functools.partial(kernel, senders, group),
        out_shape=(
            pltpu.VMEM(fluid_temp.shape, F32),
            pltpu.VMEM((chunks, rows, group * width), BF16),
            pltpu.VMEM(face_src.shape, jnp.int32),
            pltpu.VMEM((senders, 1, width), F32),
            pltpu.VMEM(solid_old.shape, F32),
        ),
        in_specs=[pl.BlockSpec(memory_space=pltpu.HBM)] * 8,
        out_specs=(pl.BlockSpec(memory_space=pltpu.VMEM),) * 5,
        scratch_shapes=scratch,
        compiler_params=pltpu.CompilerParams(
            collective_id=0, has_side_effects=True, vmem_limit_bytes=24 * 1024 * 1024
        ),
    )(*args)
    parts = tuple(pltpu.with_memory_space_constraint(p, pltpu.VMEM) for p in parts)
    return pl.pallas_call(
        functools.partial(finish, group),
        out_shape=(
            jax.ShapeDtypeStruct(fluid_temp.shape, F32),
            jax.ShapeDtypeStruct(solid_old.shape, F32),
        ),
        in_specs=[pl.BlockSpec(memory_space=pltpu.VMEM)] * 5,
        out_specs=(pl.BlockSpec(memory_space=pl.ANY),) * 2,
        scratch_shapes=[pltpu.VMEM(fluid_temp.shape, F32), dma((5,))],
        compiler_params=pltpu.CompilerParams(vmem_limit_bytes=16 * 1024 * 1024),
    )(*parts)


def solution(mesh):
    return jax.shard_map(
        per_device,
        mesh=mesh,
        in_specs=(
            P("gx", "gy", "gz"),
            P("gx", "gy", "gz"),
            P("gx", "gy", "gz", None),
            P("gx", "gy", "gz", None),
            P(("gy", "gz"), "gx", None),
            P(("gy", "gz"), "gx", None),
            P(("gy", "gz"), "gx", None, None, None),
            P(("gy", "gz"), "gx", None),
        ),
        out_specs=(P("gx", "gy", "gz"), P(("gy", "gz"), "gx", None)),
        check_vma=False,
    )
```

```python
import functools

import jax
import jax.numpy as jnp
from jax import lax
from jax.experimental import pallas as pl
from jax.experimental.pallas import tpu as pltpu
from jax.sharding import PartitionSpec as P

REACH = 2
SWEEPS = 4
NB = 5
DIFFUSION = 0.12
EVAPORATION = 0.5
SATURATION = 0.25
WALL_COUPLING = 0.2
MESH = pl.DeviceIdType.MESH
F32 = jnp.float32
BF16 = jnp.bfloat16


def split(values):
    high = values.astype(BF16)
    return high, (values - high.astype(F32)).astype(BF16)


def dot(a, b):
    return jnp.dot(a, b, preferred_element_type=F32)


def dot_nt(a, b):
    return lax.dot_general(a, b, (((1,), (1,)), ((), ())), preferred_element_type=F32)


def rows_of(shape):
    return lax.broadcasted_iota(jnp.int32, shape, 0)


def repeat(count, body):
    if count == 1:
        body(0)
    else:
        pl.loop(0, count)(body)


def kernel(
    senders, group,
    fluid_h, liquid_h, src_h, dst_h, old_h, diag_h, blocks_h, pat_h,
    base, hot, src, wall, solid,
    fluid, liquid, dst, old, diag, blocks, pat,
    spot, back, table, outp, arr, sent, ret, pre_out, pre_in, halo_out, halo,
    x_in, y_out, y_in, z_out, z_in, ext, gather, sums, edge, far_in, far_edge, own,
    load_sem, arr_send, arr_recv, ret_send, ret_recv, pre_send, pre_recv,
    halo_send, halo_recv, face_send, face_recv, near_sem, far_send, far_recv,
):
    cx, cy, cz = fluid.shape
    rows = cx * cy
    tiles, width = old.shape[1], old.shape[2]
    chunks = senders // group
    me = lax.axis_index("gx")
    gy, gz = lax.axis_index("gy"), lax.axis_index("gz")
    ny, nz = lax.axis_size("gy"), lax.axis_size("gz")
    left, right = lax.rem(me + senders - 1, senders), lax.rem(me + 1, senders)
    below, above = lax.rem(gy + ny - 1, ny), lax.rem(gy + 1, ny)
    before, after = lax.rem(gz + nz - 1, nz), lax.rem(gz + 1, nz)
    has_left, has_right = me > 0, me < senders - 1
    barrier = pltpu.get_barrier_semaphore()

    line_peers = [{"gx": lax.rem(me + d, senders)} for d in range(1, senders)]
    cross_peers = [{"gy": below}, {"gy": above}, {"gz": before}, {"gz": after}]
    odd = lax.rem(gy + gz, 2) == 1
    even = jnp.logical_not(odd)

    def signal(semaphore, device):
        pl.semaphore_signal(semaphore, inc=1, device_id=device, device_id_type=MESH)

    for peer in line_peers:
        signal(barrier, peer)

    @pl.when(even)
    def _():
        for peer in cross_peers:
            signal(barrier, peer)

    pairs = [(src_h, src), (fluid_h, fluid), (dst_h, dst), (old_h, old), (diag_h, diag),
             (pat_h, pat), (blocks_h, blocks), (liquid_h, liquid)]
    loads = [pltpu.make_async_copy(a, b, load_sem.at[i]) for i, (a, b) in enumerate(pairs)]
    for load in loads:
        load.start()

    def send(source, target, send_sem, recv_sem, device):
        return pltpu.make_async_remote_copy(
            src_ref=source, dst_ref=target, send_sem=send_sem, recv_sem=recv_sem,
            device_id=device, device_id_type=MESH)

    outp[...] = jnp.zeros_like(outp)
    ext[...] = jnp.zeros_like(ext)
    sums[...] = jnp.zeros_like(sums)
    loads[0].wait()

    def make_hot(c):
        for j in range(group):
            row = src[c * group + j, 0] >> 7
            for s in range(0, rows, 128):
                hit = rows_of((128, width)) + s == row
                hot[c, s:s + 128, j * width:(j + 1) * width] = jnp.where(hit, 1.0, 0.0).astype(BF16)

    repeat(chunks, make_hot)

    for load in loads[2:5]:
        load.wait()
    diagonal = diag[0]
    inverse = 1.0 / diagonal
    fixed = diagonal * old[0]
    for side, lo in ((0, 0), (1, tiles - REACH)):
        for q in range(senders):
            pre_out[side, q:q + 1, :] = dst[q, 0].astype(F32)
        pre_out[side, senders:senders + REACH, :] = fixed[lo:lo + REACH]
        pre_out[side, senders + REACH:senders + 2 * REACH, :] = inverse[lo:lo + REACH]

    loads[1].wait()
    per = 128 // cy
    for s in range(rows // 128):
        flipped = fluid[s * per:(s + 1) * per].reshape(128, cz).T
        high, low = split(flipped)
        table[0:cz, s * 128:(s + 1) * 128] = high
        table[cz:2 * cz, s * 128:(s + 1) * 128] = low
        z_out[0, :, s * 128:(s + 1) * 128] = flipped[0:1]
        z_out[1, :, s * 128:(s + 1) * 128] = flipped[cz - 1:cz]

    def pick(c):
        picked = dot(table[...], hot[c])
        picked = picked[0:cz] + picked[cz:2 * cz]
        for j in range(group):
            depth = src[c * group + j, 0] & (cz - 1)
            part = picked[:, j * width:(j + 1) * width]
            part = jnp.where(rows_of((cz, width)) == depth, part, 0.0)
            outp[c * group + j + 1] = jnp.sum(part, axis=0, keepdims=True)

    repeat(chunks, pick)

    pl.semaphore_wait(barrier, jnp.where(odd, len(line_peers) + len(cross_peers), len(line_peers)))

    pre_l = send(pre_out.at[0], pre_in.at[1], pre_send.at[0], pre_recv.at[1], {"gx": left})
    pre_r = send(pre_out.at[1], pre_in.at[0], pre_send.at[1], pre_recv.at[0], {"gx": right})
    halo_l = [send(halo_out.at[k, 0], halo.at[k, 1], halo_send.at[k, 0], halo_recv.at[k, 1],
                   {"gx": left}) for k in range(SWEEPS - 1)]
    halo_r = [send(halo_out.at[k, 1], halo.at[k, 0], halo_send.at[k, 1], halo_recv.at[k, 0],
                   {"gx": right}) for k in range(SWEEPS - 1)]
    arrivals = []
    for d in range(1, senders):
        peer = lax.rem(me + d, senders)
        arrivals.append(send(outp.at[pl.ds(peer, 3)], arr.at[me], arr_send.at[d], arr_recv.at[d],
                             {"gx": peer}))

    @pl.when(has_left)
    def _():
        pre_l.start()

    @pl.when(has_right)
    def _():
        pre_r.start()

    for copy in arrivals:
        copy.start()
    y_out[0] = fluid[:, 0, :]
    y_out[1] = fluid[:, cy - 1, :]
    faces = [
        send(fluid.at[0], x_in.at[1], face_send.at[0], face_recv.at[0], {"gx": left}),
        send(fluid.at[cx - 1], x_in.at[0], face_send.at[1], face_recv.at[1], {"gx": right}),
        send(y_out.at[0], y_in.at[1], face_send.at[2], face_recv.at[2], {"gy": below}),
        send(y_out.at[1], y_in.at[0], face_send.at[3], face_recv.at[3], {"gy": above}),
        send(z_out.at[0], z_in.at[1], face_send.at[4], face_recv.at[4], {"gz": before}),
        send(z_out.at[1], z_in.at[0], face_send.at[5], face_recv.at[5], {"gz": after}),
    ]

    @pl.when(odd)
    def _():
        for peer in cross_peers:
            signal(near_sem, peer)
        for face in faces[2:]:
            face.start()

    for face in faces[0:2]:
        face.start()
    arr[pl.ds(me, 1)] = outp[pl.ds(me, 3)][None]

    @pl.when(jnp.logical_not(has_left))
    def _():
        pre_in[0] = jnp.zeros_like(pre_in[0])

    @pl.when(jnp.logical_not(has_right))
    def _():
        pre_in[1] = jnp.zeros_like(pre_in[1])

    for load in loads[5:7]:
        load.wait()
    small = rows_of((tiles, tiles)) == lax.broadcasted_iota(jnp.int32, (tiles, tiles), 1)
    for o in range(NB):
        row = jnp.broadcast_to(pat[o].astype(F32), (tiles, tiles))
        column = jnp.sum(jnp.where(small, row, 0.0), axis=1, keepdims=True)
        mask = jnp.broadcast_to(column, (tiles, width))
        for t in range(tiles):
            blocks[0, t, o] = blocks[0, t, o] * mask[t:t + 1]

    @pl.when(has_left)
    def _():
        send(pre_out.at[1], pre_in.at[0], pre_send.at[1], pre_recv.at[0], {"gx": left}).wait_recv()

    @pl.when(has_right)
    def _():
        send(pre_out.at[0], pre_in.at[1], pre_send.at[0], pre_recv.at[1], {"gx": right}).wait_recv()

    def ids_at(run, q):
        if run == 1:
            return dst[q, 0]
        return pre_in[run // 2, pl.ds(q, 1), :].astype(jnp.int32)

    def make_spot(c):
        for run in range(3):
            for j in range(group):
                hit = rows_of((width, width)) == ids_at(run, c * group + j) & (width - 1)
                hit = jnp.where(hit, 1.0, 0.0)
                back[run, c, j * width:(j + 1) * width, :] = hit.T.astype(BF16)
                if run == 1:
                    spot[c, :, j * width:(j + 1) * width] = hit.astype(BF16)

    repeat(chunks, make_spot)
    ones = jnp.ones((2 * width, width), BF16)
    eye = rows_of((width, width)) == lax.broadcasted_iota(jnp.int32, (width, width), 1)
    for copy in arrivals:
        copy.wait_recv()

    gather[...] = jnp.zeros_like(gather)

    def add_group(c):
        for run in range(3):
            lhs = []
            for j in range(group):
                q = c * group + j
                hit = rows_of((tiles, width)) == ids_at(run, q) >> 7
                high, low = split(jnp.where(hit, arr[q, run], 0.0))
                lhs.append(jnp.concatenate([high, low], axis=0))
            gather[run] += dot(jnp.concatenate(lhs, axis=1), back[run, c])

    repeat(chunks, add_group)
    gathered = [gather[run, 0:tiles] + gather[run, tiles:2 * tiles] for run in range(3)]
    right_side = fixed + gathered[1]
    iterate = inverse * right_side
    ext[REACH:REACH + tiles, :] = iterate
    for side, run, lo, at in ((0, 0, tiles - REACH, 0), (1, 2, 0, tiles + REACH)):
        fixed_near = pre_in[side, senders:senders + REACH, :]
        inverse_near = pre_in[side, senders + REACH:senders + 2 * REACH, :]
        ext[at:at + REACH, :] = inverse_near * (fixed_near + gathered[run][lo:lo + REACH])

    def couple(slot, pairs_of):
        for t, offsets in pairs_of:
            total = None
            for o in offsets:
                term = blocks[0, t, o] * ext[t + o:t + o + 1, :]
                total = term if total is None else total + term
            high, low = split(total)
            summed = dot(jnp.concatenate([high, low], axis=1), ones)
            sums[slot, t:t + 1, :] = jnp.sum(jnp.where(eye, summed, 0.0), axis=0, keepdims=True)

    def inside(t, o):
        return 0 <= t + o - REACH < tiles

    every = list(range(NB))
    middle = [(t, every) for t in range(REACH, tiles - REACH)]
    local = [(t, [o for o in every if inside(t, o)]) for t in range(tiles)]
    first = [(t, every) for t in range(REACH)]
    last = [(t, every) for t in range(tiles - REACH, tiles)]
    no_left, no_right = jnp.logical_not(has_left), jnp.logical_not(has_right)

    sides = ((0, has_left, 0, 0, halo_r, halo_l),
             (1, has_right, tiles - REACH, tiles + REACH, halo_l, halo_r))

    def make_edges():
        for side, has, lo, at, _, _ in sides:
            @pl.when(has)
            def _():
                for i in range(REACH):
                    for j in range(REACH):
                        o = at + i - lo - j
                        block = jnp.zeros((width, width), F32)
                        if 0 <= o < NB:
                            block = blocks[0, lo + j, o].T
                        for part, values in enumerate(split(block)):
                            column = (part * REACH + j) * width
                            edge[side, i * width:(i + 1) * width, column:column + width] = values

    def times_edge(values, matrix):
        flat = jnp.concatenate([values[i:i + 1] for i in range(REACH)], axis=1)
        high = flat.astype(BF16).astype(F32)
        lhs = [jnp.broadcast_to(v, (8, REACH * width)) for v in (high, flat - high)]
        product = dot(jnp.concatenate(lhs, axis=0).astype(BF16), matrix)
        product = product[0:1] + product[8:9]
        product = product[:, 0:REACH * width] + product[:, REACH * width:]
        return jnp.concatenate([product[:, j * width:(j + 1) * width] for j in range(REACH)], axis=0)

    merged = senders == 2
    places = [(i, j) for i in range(REACH) for j in range(REACH)]

    def far_blocks(side):
        _, _, lo, at, _, _ = sides[side]
        found = [(n, i, j, at + i - lo - j) for n, (i, j) in enumerate(places)]
        return [entry for entry in found if 0 <= entry[3] < NB]

    def far_copies(side):
        lo = sides[side][2]
        return [send(blocks.at[0, lo + j, o], far_in.at[n], far_send.at[n], far_recv.at[n],
                     {"gx": left if side == 0 else right}) for n, i, j, o in far_blocks(side)]

    def send_far():
        for side, has, _, _, _, _ in sides:
            @pl.when(has)
            def _():
                for copy in far_copies(side):
                    copy.start()

    def correct(scale_new):
        for side, has, lo, _, _, _ in sides:
            @pl.when(has)
            def _():
                for copy in far_copies(1 - side):
                    copy.wait_recv()
                far_edge[...] = jnp.zeros_like(far_edge)
                for n, i, j, _ in far_blocks(1 - side):
                    for half, values in enumerate(split(far_in[n].T)):
                        column = (half * REACH + j) * width
                        far_edge[i * width:(i + 1) * width, column:column + width] = values
                summed = times_edge(iterate[lo:lo + REACH], far_edge[...])
                change = -scale_new * pre_in[side, senders + REACH:senders + 2 * REACH, :] * summed
                ids = pre_in[side, pl.ds(me, 1), :].astype(jnp.int32)
                hit = rows_of((width, width)) == ids & (width - 1)
                change = jnp.concatenate([change, jnp.zeros((8 - REACH, width), F32)], axis=0)
                picked = dot(jnp.concatenate(split(change), axis=0), jnp.where(hit, 1.0, 0.0).astype(BF16))
                picked = picked[0:8] + picked[8:16]
                row = (ids >> 7) - (0 if side == 1 else tiles - REACH)
                live = jnp.logical_and(rows_of((8, width)) == row, rows_of((8, width)) < REACH)
                sums[0, 0:1, :] = jnp.sum(jnp.where(live, picked, 0.0), axis=0, keepdims=True)

    def take(k, part, scale_old, scale_new):
        for side, has, lo, _, copy_in, copy_out in sides:
            @pl.when(has)
            def _():
                copy_in[k].wait_recv()
                summed = times_edge(halo[k, side], edge[side])
                cut = slice(lo, lo + REACH)
                if k + 1 < SWEEPS - 1:
                    change = scale_old * update[cut] + scale_new * inverse[cut] * (part[cut] - summed)
                    halo_out[k + 1, side] = iterate[cut] + change
                    copy_out[k + 1].start()
                sums[1, cut, :] = summed

    lane = lax.broadcasted_iota(jnp.int32, (cy, cz), 1)
    line = lax.broadcasted_iota(jnp.int32, (cy, cz), 0)

    def stencil(first, last):
        for i in range(first, last):
            here = fluid[i]
            near = jnp.where(line == 0, 0.0, pltpu.roll(here, 1, 0))
            near = near + jnp.where(line == cy - 1, 0.0, pltpu.roll(here, cy - 1, 0))
            near = near + jnp.where(lane == 0, 0.0, pltpu.roll(here, 1, 1))
            near = near + jnp.where(lane == cz - 1, 0.0, pltpu.roll(here, cz - 1, 1))
            if i > 0:
                near = near + fluid[i - 1]
            if i < cx - 1:
                near = near + fluid[i + 1]
            dry = liquid[i].astype(F32) * jnp.maximum(here - SATURATION, 0.0)
            base[i] = here + DIFFUSION * (near - 6.0 * here) - EVAPORATION * dry

    def finish_faces():
        for face in faces[2:]:
            face.wait_recv()
        base[:, 0, :] += DIFFUSION * y_in[0]
        base[:, cy - 1, :] += DIFFUSION * y_in[1]
        deep = rows_of((cz, 128))
        for s in range(rows // 128):
            cut = slice(s * 128, (s + 1) * 128)
            layer = jnp.where(deep == 0, z_in[0, :, cut], 0.0)
            layer = layer + jnp.where(deep == cz - 1, z_in[1, :, cut], 0.0)
            base[s * per:(s + 1) * per] += DIFFUSION * layer.T.reshape(per, cy, cz)

    def pick_back(values, target):
        both = jnp.concatenate(split(values), axis=0)

        def pick_chunk(c):
            picked = dot(both, spot[c])
            picked = picked[0:tiles] + picked[tiles:2 * tiles]
            for j in range(group):
                row = dst[c * group + j, 0] >> 7
                part = picked[:, j * width:(j + 1) * width]
                part = jnp.where(rows_of((tiles, width)) == row, part, 0.0)
                target[c * group + j] = jnp.sum(part, axis=0, keepdims=True)

        repeat(chunks, pick_chunk)

    backs = []
    for d in range(1, senders):
        peer = lax.rem(me + d, senders)
        backs.append(send(sent.at[peer], ret.at[me], ret_send.at[d], ret_recv.at[d], {"gx": peer}))

    def step(lo):
        cut = slice(lo, lo + REACH)
        rest = right_side[cut] - diagonal[cut] * iterate[cut] - sums[0, cut, :]
        return iterate[cut] + inverse[cut] * rest

    @pl.when(has_left)
    def _():
        couple(0, first)
        halo_out[0, 0] = step(0)
        halo_l[0].start()

    @pl.when(has_right)
    def _():
        couple(0, last)
        halo_out[0, 1] = step(tiles - REACH)
        halo_r[0].start()

    @pl.when(no_left)
    def _():
        couple(0, first)

    @pl.when(no_right)
    def _():
        couple(0, last)

    couple(0, middle)
    update = inverse * (right_side - diagonal * iterate - sums[0])
    iterate = iterate + update
    rho_old = 0.5
    for k in range(SWEEPS - 1):
        rho_next = 1.0 / (4.0 - rho_old)
        ext[REACH:REACH + tiles, :] = iterate
        if merged and k == 1:
            send_far()
        couple(0, local)
        part = right_side - diagonal * iterate - sums[0]
        if k == 0:
            loads[7].wait()
            stencil(0, cx // 2)

            @pl.when(even)
            def _():
                pl.semaphore_wait(near_sem, len(cross_peers))
                for face in faces[2:]:
                    face.start()

        if k == 1:
            stencil(cx // 2, cx)
        if merged and k == SWEEPS - 2:
            change = rho_next * rho_old * update + 4.0 * rho_next * inverse * part
            pick_back(iterate + change, sent)
            for copy in backs:
                copy.start()
            correct(4.0 * rho_next)
        if k == SWEEPS - 2:
            for face in faces[0:2]:
                face.wait_recv()
            base[0] += DIFFUSION * x_in[0]
            base[cx - 1] += DIFFUSION * x_in[1]
            if merged:
                finish_faces()
        if k == 0:
            make_edges()
        take(k, part, rho_next * rho_old, 4.0 * rho_next)
        residual = part - sums[1]
        update = rho_next * rho_old * update + 4.0 * rho_next * inverse * residual
        iterate = iterate + update
        rho_old = rho_next

    if merged:
        pick_back(iterate, own)
        ret[pl.ds(me, 1)] = own[pl.ds(me, 1)]
    else:
        pick_back(iterate, sent)
        for copy in backs:
            copy.start()
        ret[pl.ds(me, 1)] = sent[pl.ds(me, 1)]
    solid[0] = iterate
    if not merged:
        finish_faces()

    for copy in arrivals + faces:
        copy.wait_send()

    @pl.when(has_left)
    def _():
        for copy in [pre_l] + halo_l:
            copy.wait_send()

    @pl.when(has_right)
    def _():
        for copy in [pre_r] + halo_r:
            copy.wait_send()

    for copy in backs:
        copy.wait()
    wall[...] = WALL_COUPLING * (ret[...] - outp[1:senders + 1])
    if merged:
        other = pl.ds(1 - me, 1)
        wall[other] = wall[other] + WALL_COUPLING * sums[0, 0:1, :][None]
        for side, has, _, _, _, _ in sides:
            @pl.when(has)
            def _():
                for copy in far_copies(side):
                    copy.wait_send()


def finish(group, base, hot, src, wall, solid, new_h, solid_h, new, sems):
    cx, cy, cz = base.shape
    rows = cx * cy
    chunks, width = hot.shape[0], src.shape[-1]
    solid_copy = pltpu.make_async_copy(solid, solid_h, sems.at[0])
    solid_copy.start()

    def placed_of(c):
        halves = []
        for j in range(group):
            q = c * group + j
            placed = jnp.where(rows_of((cz, width)) == src[q, 0] & (cz - 1), wall[q], 0.0)
            halves.append(jnp.concatenate(split(placed), axis=0))
        return jnp.concatenate(halves, axis=1)

    step = rows // 4
    cuts = [slice(s * step // cy, (s + 1) * step // cy) for s in range(4)]

    def added(c, s, placed):
        both = dot_nt(hot[c, s * step:(s + 1) * step, :], placed)
        return (both[:, 0:cz] + both[:, cz:2 * cz]).reshape(step // cy, cy, cz)

    if chunks > 1:
        def add_chunk(c):
            placed = placed_of(c)
            for s in range(4):
                base_now = jnp.where(c == 0, base[cuts[s]], new[cuts[s]])
                new[cuts[s]] = base_now + added(c, s, placed)

        pl.loop(0, chunks)(add_chunk)
    else:
        placed = placed_of(0)
    copies = []
    for s in range(4):
        if chunks == 1:
            new[cuts[s]] = base[cuts[s]] + added(0, s, placed)
        copies.append(pltpu.make_async_copy(new.at[cuts[s]], new_h.at[cuts[s]], sems.at[s + 1]))
        copies[-1].start()
    for copy in [solid_copy] + copies:
        copy.wait()


def per_device(fluid_temp, liquid, face_src, face_dst, solid_old, solid_diag, blocks, pattern):
    senders = lax.axis_size("gx")
    group = 2 if senders % 2 == 0 else 1
    chunks = senders // group
    cx, cy, cz = fluid_temp.shape
    rows = cx * cy
    tiles, width = solid_old.shape[1:]
    pre_rows = (senders + 2 * REACH + 7) // 8 * 8
    ext_rows = (tiles + 2 * REACH + 7) // 8 * 8
    dma = pltpu.SemaphoreType.DMA
    pattern = jnp.transpose(pattern, (2, 0, 1))
    args = (fluid_temp, liquid, face_src, face_dst, solid_old, solid_diag, blocks, pattern)
    args = tuple(pltpu.with_memory_space_constraint(a, pltpu.HBM) for a in args)
    scratch = [pltpu.VMEM(a.shape, a.dtype)
               for a in (fluid_temp, liquid, face_dst, solid_old, solid_diag, blocks, pattern)]
    scratch += [
        pltpu.VMEM((chunks, width, group * width), BF16),
        pltpu.VMEM((3, chunks, group * width, width), BF16),
        pltpu.VMEM((2 * cz, rows), BF16),
        pltpu.VMEM((senders + 2, 1, width), F32),
        pltpu.VMEM((senders, 3, 1, width), F32),
        pltpu.VMEM((senders, 1, width), F32),
        pltpu.VMEM((senders, 1, width), F32),
        pltpu.VMEM((2, pre_rows, width), F32),
        pltpu.VMEM((2, pre_rows, width), F32),
        pltpu.VMEM((SWEEPS - 1, 2, REACH, width), F32),
        pltpu.VMEM((SWEEPS - 1, 2, REACH, width), F32),
        pltpu.VMEM((2, cy, cz), F32),
        pltpu.VMEM((2, cx, cz), F32),
        pltpu.VMEM((2, cx, cz), F32),
        pltpu.VMEM((2, 1, rows), F32),
        pltpu.VMEM((2, 1, rows), F32),
        pltpu.VMEM((ext_rows, width), F32),
        pltpu.VMEM((3, 2 * tiles, width), F32),
        pltpu.VMEM((2, tiles, width), F32),
        pltpu.VMEM((2, REACH * width, 2 * REACH * width), BF16),
        pltpu.VMEM((REACH * REACH, width, width), F32),
        pltpu.VMEM((REACH * width, 2 * REACH * width), BF16),
        pltpu.VMEM((senders, 1, width), F32),
        dma((8,)),
        dma((senders,)), dma((senders,)),
        dma((senders,)), dma((senders,)),
        dma((2,)), dma((2,)),
        dma((SWEEPS - 1, 2)), dma((SWEEPS - 1, 2)),
        dma((6,)), dma((6,)),
        pltpu.SemaphoreType.REGULAR,
        dma((4,)), dma((4,)),
    ]
    parts = pl.pallas_call(
        functools.partial(kernel, senders, group),
        out_shape=(
            pltpu.VMEM(fluid_temp.shape, F32),
            pltpu.VMEM((chunks, rows, group * width), BF16),
            pltpu.VMEM(face_src.shape, jnp.int32),
            pltpu.VMEM((senders, 1, width), F32),
            pltpu.VMEM(solid_old.shape, F32),
        ),
        in_specs=[pl.BlockSpec(memory_space=pltpu.HBM)] * 8,
        out_specs=(pl.BlockSpec(memory_space=pltpu.VMEM),) * 5,
        scratch_shapes=scratch,
        compiler_params=pltpu.CompilerParams(
            collective_id=0, has_side_effects=True, vmem_limit_bytes=24 * 1024 * 1024
        ),
    )(*args)
    parts = tuple(pltpu.with_memory_space_constraint(p, pltpu.VMEM) for p in parts)
    return pl.pallas_call(
        functools.partial(finish, group),
        out_shape=(
            jax.ShapeDtypeStruct(fluid_temp.shape, F32),
            jax.ShapeDtypeStruct(solid_old.shape, F32),
        ),
        in_specs=[pl.BlockSpec(memory_space=pltpu.VMEM)] * 5,
        out_specs=(pl.BlockSpec(memory_space=pl.ANY),) * 2,
        scratch_shapes=[pltpu.VMEM(fluid_temp.shape, F32), dma((5,))],
        compiler_params=pltpu.CompilerParams(vmem_limit_bytes=16 * 1024 * 1024),
    )(*parts)


def solution(mesh):
    return jax.shard_map(
        per_device,
        mesh=mesh,
        in_specs=(
            P("gx", "gy", "gz"),
            P("gx", "gy", "gz"),
            P("gx", "gy", "gz", None),
            P("gx", "gy", "gz", None),
            P(("gy", "gz"), "gx", None),
            P(("gy", "gz"), "gx", None),
            P(("gy", "gz"), "gx", None, None, None),
            P(("gy", "gz"), "gx", None),
        ),
        out_specs=(P("gx", "gy", "gz"), P(("gy", "gz"), "gx", None)),
        check_vma=False,
    )
```

```python
import functools

import jax
import jax.numpy as jnp
from jax import lax
from jax.experimental import pallas as pl
from jax.experimental.pallas import tpu as pltpu
from jax.sharding import PartitionSpec as P

REACH = 2
SWEEPS = 4
NB = 5
DIFFUSION = 0.12
EVAPORATION = 0.5
SATURATION = 0.25
WALL_COUPLING = 0.2
MESH = pl.DeviceIdType.MESH
F32 = jnp.float32
BF16 = jnp.bfloat16


def split(values):
    high = values.astype(BF16)
    return high, (values - high.astype(F32)).astype(BF16)


def dot(a, b):
    return jnp.dot(a, b, preferred_element_type=F32)


def dot_nt(a, b):
    return lax.dot_general(a, b, (((1,), (1,)), ((), ())), preferred_element_type=F32)


def rows_of(shape):
    return lax.broadcasted_iota(jnp.int32, shape, 0)


def repeat(count, body):
    if count == 1:
        body(0)
    else:
        pl.loop(0, count)(body)


def kernel(
    senders, group,
    fluid_h, liquid_h, src_h, dst_h, old_h, diag_h, blocks_h, pat_h,
    base, hot, src, wall, solid,
    fluid, liquid, dst, old, diag, blocks, pat,
    spot, back, table, outp, arr, sent, ret, pre_out, pre_in, halo_out, halo,
    x_in, y_out, y_in, z_out, z_in, ext, gather, sums, edge, far_in, far_edge, own,
    load_sem, arr_send, arr_recv, ret_send, ret_recv, pre_send, pre_recv,
    halo_send, halo_recv, face_send, face_recv, near_sem, far_send, far_recv,
):
    cx, cy, cz = fluid.shape
    rows = cx * cy
    tiles, width = old.shape[1], old.shape[2]
    chunks = senders // group
    me = lax.axis_index("gx")
    gy, gz = lax.axis_index("gy"), lax.axis_index("gz")
    ny, nz = lax.axis_size("gy"), lax.axis_size("gz")
    left, right = lax.rem(me + senders - 1, senders), lax.rem(me + 1, senders)
    below, above = lax.rem(gy + ny - 1, ny), lax.rem(gy + 1, ny)
    before, after = lax.rem(gz + nz - 1, nz), lax.rem(gz + 1, nz)
    has_left, has_right = me > 0, me < senders - 1
    barrier = pltpu.get_barrier_semaphore()

    line_peers = [{"gx": lax.rem(me + d, senders)} for d in range(1, senders)]
    cross_peers = [{"gy": below}, {"gy": above}, {"gz": before}, {"gz": after}]
    odd = lax.rem(gy + gz, 2) == 1
    even = jnp.logical_not(odd)

    def signal(semaphore, device):
        pl.semaphore_signal(semaphore, inc=1, device_id=device, device_id_type=MESH)

    for peer in line_peers:
        signal(barrier, peer)

    @pl.when(even)
    def _():
        for peer in cross_peers:
            signal(barrier, peer)

    pairs = [(src_h, src), (fluid_h, fluid), (dst_h, dst), (old_h, old), (diag_h, diag),
             (pat_h, pat), (blocks_h, blocks), (liquid_h, liquid)]
    loads = [pltpu.make_async_copy(a, b, load_sem.at[i]) for i, (a, b) in enumerate(pairs)]
    for load in loads:
        load.start()

    def send(source, target, send_sem, recv_sem, device):
        return pltpu.make_async_remote_copy(
            src_ref=source, dst_ref=target, send_sem=send_sem, recv_sem=recv_sem,
            device_id=device, device_id_type=MESH)

    outp[...] = jnp.zeros_like(outp)
    ext[...] = jnp.zeros_like(ext)
    sums[...] = jnp.zeros_like(sums)
    loads[0].wait()

    def make_hot(c):
        for j in range(group):
            row = src[c * group + j, 0] >> 7
            for s in range(0, rows, 128):
                hit = rows_of((128, width)) + s == row
                hot[c, s:s + 128, j * width:(j + 1) * width] = jnp.where(hit, 1.0, 0.0).astype(BF16)

    repeat(chunks, make_hot)

    for load in loads[2:5]:
        load.wait()
    diagonal = diag[0]
    inverse = 1.0 / diagonal
    fixed = diagonal * old[0]
    for side, lo in ((0, 0), (1, tiles - REACH)):
        for q in range(senders):
            pre_out[side, q:q + 1, :] = dst[q, 0].astype(F32)
        pre_out[side, senders:senders + REACH, :] = fixed[lo:lo + REACH]
        pre_out[side, senders + REACH:senders + 2 * REACH, :] = inverse[lo:lo + REACH]

    loads[1].wait()
    per = 128 // cy
    for s in range(rows // 128):
        flipped = fluid[s * per:(s + 1) * per].reshape(128, cz).T
        high, low = split(flipped)
        table[0:cz, s * 128:(s + 1) * 128] = high
        table[cz:2 * cz, s * 128:(s + 1) * 128] = low
        z_out[0, :, s * 128:(s + 1) * 128] = flipped[0:1]
        z_out[1, :, s * 128:(s + 1) * 128] = flipped[cz - 1:cz]

    def pick(c):
        picked = dot(table[...], hot[c])
        picked = picked[0:cz] + picked[cz:2 * cz]
        for j in range(group):
            depth = src[c * group + j, 0] & (cz - 1)
            part = picked[:, j * width:(j + 1) * width]
            part = jnp.where(rows_of((cz, width)) == depth, part, 0.0)
            outp[c * group + j + 1] = jnp.sum(part, axis=0, keepdims=True)

    repeat(chunks, pick)

    pl.semaphore_wait(barrier, jnp.where(odd, len(line_peers) + len(cross_peers), len(line_peers)))

    pre_l = send(pre_out.at[0], pre_in.at[1], pre_send.at[0], pre_recv.at[1], {"gx": left})
    pre_r = send(pre_out.at[1], pre_in.at[0], pre_send.at[1], pre_recv.at[0], {"gx": right})
    halo_l = [send(halo_out.at[k, 0], halo.at[k, 1], halo_send.at[k, 0], halo_recv.at[k, 1],
                   {"gx": left}) for k in range(SWEEPS - 1)]
    halo_r = [send(halo_out.at[k, 1], halo.at[k, 0], halo_send.at[k, 1], halo_recv.at[k, 0],
                   {"gx": right}) for k in range(SWEEPS - 1)]
    arrivals = []
    for d in range(1, senders):
        peer = lax.rem(me + d, senders)
        arrivals.append(send(outp.at[pl.ds(peer, 3)], arr.at[me], arr_send.at[d], arr_recv.at[d],
                             {"gx": peer}))

    @pl.when(has_left)
    def _():
        pre_l.start()

    @pl.when(has_right)
    def _():
        pre_r.start()

    for copy in arrivals:
        copy.start()
    y_out[0] = fluid[:, 0, :]
    y_out[1] = fluid[:, cy - 1, :]
    faces = [
        send(fluid.at[0], x_in.at[1], face_send.at[0], face_recv.at[0], {"gx": left}),
        send(fluid.at[cx - 1], x_in.at[0], face_send.at[1], face_recv.at[1], {"gx": right}),
        send(y_out.at[0], y_in.at[1], face_send.at[2], face_recv.at[2], {"gy": below}),
        send(y_out.at[1], y_in.at[0], face_send.at[3], face_recv.at[3], {"gy": above}),
        send(z_out.at[0], z_in.at[1], face_send.at[4], face_recv.at[4], {"gz": before}),
        send(z_out.at[1], z_in.at[0], face_send.at[5], face_recv.at[5], {"gz": after}),
    ]

    @pl.when(odd)
    def _():
        for peer in cross_peers:
            signal(near_sem, peer)
        for face in faces[2:]:
            face.start()

    for face in faces[0:2]:
        face.start()
    arr[pl.ds(me, 1)] = outp[pl.ds(me, 3)][None]

    @pl.when(jnp.logical_not(has_left))
    def _():
        pre_in[0] = jnp.zeros_like(pre_in[0])

    @pl.when(jnp.logical_not(has_right))
    def _():
        pre_in[1] = jnp.zeros_like(pre_in[1])

    for load in loads[5:7]:
        load.wait()
    small = rows_of((tiles, tiles)) == lax.broadcasted_iota(jnp.int32, (tiles, tiles), 1)
    for o in range(NB):
        row = jnp.broadcast_to(pat[o].astype(F32), (tiles, tiles))
        column = jnp.sum(jnp.where(small, row, 0.0), axis=1, keepdims=True)
        mask = jnp.broadcast_to(column, (tiles, width))
        for t in range(tiles):
            blocks[0, t, o] = blocks[0, t, o] * mask[t:t + 1]

    @pl.when(has_left)
    def _():
        send(pre_out.at[1], pre_in.at[0], pre_send.at[1], pre_recv.at[0], {"gx": left}).wait_recv()

    @pl.when(has_right)
    def _():
        send(pre_out.at[0], pre_in.at[1], pre_send.at[0], pre_recv.at[1], {"gx": right}).wait_recv()

    def ids_at(run, q):
        if run == 1:
            return dst[q, 0]
        return pre_in[run // 2, pl.ds(q, 1), :].astype(jnp.int32)

    def make_spot(c):
        for run in range(3):
            for j in range(group):
                hit = rows_of((width, width)) == ids_at(run, c * group + j) & (width - 1)
                hit = jnp.where(hit, 1.0, 0.0)
                back[run, c, j * width:(j + 1) * width, :] = hit.T.astype(BF16)
                if run == 1:
                    spot[c, :, j * width:(j + 1) * width] = hit.astype(BF16)

    repeat(chunks, make_spot)
    ones = jnp.ones((2 * width, width), BF16)
    eye = rows_of((width, width)) == lax.broadcasted_iota(jnp.int32, (width, width), 1)
    for copy in arrivals:
        copy.wait_recv()

    gather[...] = jnp.zeros_like(gather)

    def add_group(c):
        for run in range(3):
            lhs = []
            for j in range(group):
                q = c * group + j
                hit = rows_of((tiles, width)) == ids_at(run, q) >> 7
                high, low = split(jnp.where(hit, arr[q, run], 0.0))
                lhs.append(jnp.concatenate([high, low], axis=0))
            gather[run] += dot(jnp.concatenate(lhs, axis=1), back[run, c])

    repeat(chunks, add_group)
    gathered = [gather[run, 0:tiles] + gather[run, tiles:2 * tiles] for run in range(3)]
    right_side = fixed + gathered[1]
    iterate = inverse * right_side
    ext[REACH:REACH + tiles, :] = iterate
    for side, run, lo, at in ((0, 0, tiles - REACH, 0), (1, 2, 0, tiles + REACH)):
        fixed_near = pre_in[side, senders:senders + REACH, :]
        inverse_near = pre_in[side, senders + REACH:senders + 2 * REACH, :]
        ext[at:at + REACH, :] = inverse_near * (fixed_near + gathered[run][lo:lo + REACH])

    def couple(slot, pairs_of):
        for t, offsets in pairs_of:
            total = None
            for o in offsets:
                term = blocks[0, t, o] * ext[t + o:t + o + 1, :]
                total = term if total is None else total + term
            high, low = split(total)
            summed = dot(jnp.concatenate([high, low], axis=1), ones)
            sums[slot, t:t + 1, :] = jnp.sum(jnp.where(eye, summed, 0.0), axis=0, keepdims=True)

    def inside(t, o):
        return 0 <= t + o - REACH < tiles

    every = list(range(NB))
    middle = [(t, every) for t in range(REACH, tiles - REACH)]
    local = [(t, [o for o in every if inside(t, o)]) for t in range(tiles)]
    first = [(t, every) for t in range(REACH)]
    last = [(t, every) for t in range(tiles - REACH, tiles)]
    no_left, no_right = jnp.logical_not(has_left), jnp.logical_not(has_right)

    sides = ((0, has_left, 0, 0, halo_r, halo_l),
             (1, has_right, tiles - REACH, tiles + REACH, halo_l, halo_r))

    def make_edges():
        for side, has, lo, at, _, _ in sides:
            @pl.when(has)
            def _():
                for i in range(REACH):
                    for j in range(REACH):
                        o = at + i - lo - j
                        block = jnp.zeros((width, width), F32)
                        if 0 <= o < NB:
                            block = blocks[0, lo + j, o].T
                        for part, values in enumerate(split(block)):
                            column = (part * REACH + j) * width
                            edge[side, i * width:(i + 1) * width, column:column + width] = values

    def times_edge(values, matrix):
        flat = jnp.concatenate([values[i:i + 1] for i in range(REACH)], axis=1)
        high = flat.astype(BF16).astype(F32)
        lhs = [jnp.broadcast_to(v, (8, REACH * width)) for v in (high, flat - high)]
        product = dot(jnp.concatenate(lhs, axis=0).astype(BF16), matrix)
        product = product[0:1] + product[8:9]
        product = product[:, 0:REACH * width] + product[:, REACH * width:]
        return jnp.concatenate([product[:, j * width:(j + 1) * width] for j in range(REACH)], axis=0)

    merged = senders == 2
    places = [(i, j) for i in range(REACH) for j in range(REACH)]

    def far_blocks(side):
        _, _, lo, at, _, _ = sides[side]
        found = [(n, i, j, at + i - lo - j) for n, (i, j) in enumerate(places)]
        return [entry for entry in found if 0 <= entry[3] < NB]

    def far_copies(side):
        lo = sides[side][2]
        return [send(blocks.at[0, lo + j, o], far_in.at[n], far_send.at[n], far_recv.at[n],
                     {"gx": left if side == 0 else right}) for n, i, j, o in far_blocks(side)]

    def send_far(turn):
        for side, has, _, _, _, _ in sides:
            @pl.when(has)
            def _():
                copies = far_copies(side)
                for copy in copies[:REACH] if turn == 0 else copies[REACH:]:
                    copy.start()

    def correct(scale_new):
        for side, has, lo, _, _, _ in sides:
            @pl.when(has)
            def _():
                for copy in far_copies(1 - side):
                    copy.wait_recv()
                far_edge[...] = jnp.zeros_like(far_edge)
                for n, i, j, _ in far_blocks(1 - side):
                    for half, values in enumerate(split(far_in[n].T)):
                        column = (half * REACH + j) * width
                        far_edge[i * width:(i + 1) * width, column:column + width] = values
                summed = times_edge(iterate[lo:lo + REACH], far_edge[...])
                change = -scale_new * pre_in[side, senders + REACH:senders + 2 * REACH, :] * summed
                ids = pre_in[side, pl.ds(me, 1), :].astype(jnp.int32)
                hit = rows_of((width, width)) == ids & (width - 1)
                change = jnp.concatenate([change, jnp.zeros((8 - REACH, width), F32)], axis=0)
                picked = dot(jnp.concatenate(split(change), axis=0), jnp.where(hit, 1.0, 0.0).astype(BF16))
                picked = picked[0:8] + picked[8:16]
                row = (ids >> 7) - (0 if side == 1 else tiles - REACH)
                live = jnp.logical_and(rows_of((8, width)) == row, rows_of((8, width)) < REACH)
                sums[0, 0:1, :] = jnp.sum(jnp.where(live, picked, 0.0), axis=0, keepdims=True)

    def take(k, part, scale_old, scale_new):
        for side, has, lo, _, copy_in, copy_out in sides:
            @pl.when(has)
            def _():
                copy_in[k].wait_recv()
                summed = times_edge(halo[k, side], edge[side])
                cut = slice(lo, lo + REACH)
                if k + 1 < SWEEPS - 1:
                    change = scale_old * update[cut] + scale_new * inverse[cut] * (part[cut] - summed)
                    halo_out[k + 1, side] = iterate[cut] + change
                    copy_out[k + 1].start()
                sums[1, cut, :] = summed

    lane = lax.broadcasted_iota(jnp.int32, (cy, cz), 1)
    line = lax.broadcasted_iota(jnp.int32, (cy, cz), 0)

    def stencil(first, last):
        for i in range(first, last):
            here = fluid[i]
            near = jnp.where(line == 0, 0.0, pltpu.roll(here, 1, 0))
            near = near + jnp.where(line == cy - 1, 0.0, pltpu.roll(here, cy - 1, 0))
            near = near + jnp.where(lane == 0, 0.0, pltpu.roll(here, 1, 1))
            near = near + jnp.where(lane == cz - 1, 0.0, pltpu.roll(here, cz - 1, 1))
            if i > 0:
                near = near + fluid[i - 1]
            if i < cx - 1:
                near = near + fluid[i + 1]
            dry = liquid[i].astype(F32) * jnp.maximum(here - SATURATION, 0.0)
            base[i] = here + DIFFUSION * (near - 6.0 * here) - EVAPORATION * dry

    def finish_faces():
        for face in faces[2:]:
            face.wait_recv()
        base[:, 0, :] += DIFFUSION * y_in[0]
        base[:, cy - 1, :] += DIFFUSION * y_in[1]
        deep = rows_of((cz, 128))
        for s in range(rows // 128):
            cut = slice(s * 128, (s + 1) * 128)
            layer = jnp.where(deep == 0, z_in[0, :, cut], 0.0)
            layer = layer + jnp.where(deep == cz - 1, z_in[1, :, cut], 0.0)
            base[s * per:(s + 1) * per] += DIFFUSION * layer.T.reshape(per, cy, cz)

    def pick_back(values, target):
        both = jnp.concatenate(split(values), axis=0)

        def pick_chunk(c):
            picked = dot(both, spot[c])
            picked = picked[0:tiles] + picked[tiles:2 * tiles]
            for j in range(group):
                row = dst[c * group + j, 0] >> 7
                part = picked[:, j * width:(j + 1) * width]
                part = jnp.where(rows_of((tiles, width)) == row, part, 0.0)
                target[c * group + j] = jnp.sum(part, axis=0, keepdims=True)

        repeat(chunks, pick_chunk)

    backs = []
    for d in range(1, senders):
        peer = lax.rem(me + d, senders)
        backs.append(send(sent.at[peer], ret.at[me], ret_send.at[d], ret_recv.at[d], {"gx": peer}))

    def step(lo):
        cut = slice(lo, lo + REACH)
        rest = right_side[cut] - diagonal[cut] * iterate[cut] - sums[0, cut, :]
        return iterate[cut] + inverse[cut] * rest

    @pl.when(has_left)
    def _():
        couple(0, first)
        halo_out[0, 0] = step(0)
        halo_l[0].start()

    @pl.when(has_right)
    def _():
        couple(0, last)
        halo_out[0, 1] = step(tiles - REACH)
        halo_r[0].start()

    @pl.when(no_left)
    def _():
        couple(0, first)

    @pl.when(no_right)
    def _():
        couple(0, last)

    couple(0, middle)
    update = inverse * (right_side - diagonal * iterate - sums[0])
    iterate = iterate + update
    rho_old = 0.5
    for k in range(SWEEPS - 1):
        rho_next = 1.0 / (4.0 - rho_old)
        ext[REACH:REACH + tiles, :] = iterate
        if merged and k < 2:
            send_far(k)
        couple(0, local)
        part = right_side - diagonal * iterate - sums[0]
        if k == 0:
            loads[7].wait()
            stencil(0, cx // 2)
        if k == 1:
            stencil(cx // 2, cx)

            @pl.when(even)
            def _():
                pl.semaphore_wait(near_sem, len(cross_peers))
                for face in faces[2:]:
                    face.start()

        if merged and k == SWEEPS - 2:
            change = rho_next * rho_old * update + 4.0 * rho_next * inverse * part
            pick_back(iterate + change, sent)
            for copy in backs:
                copy.start()
            correct(4.0 * rho_next)
        if k == SWEEPS - 2:
            for face in faces[0:2]:
                face.wait_recv()
            base[0] += DIFFUSION * x_in[0]
            base[cx - 1] += DIFFUSION * x_in[1]
            if merged:
                finish_faces()
        if k == 0:
            make_edges()
        take(k, part, rho_next * rho_old, 4.0 * rho_next)
        residual = part - sums[1]
        update = rho_next * rho_old * update + 4.0 * rho_next * inverse * residual
        iterate = iterate + update
        rho_old = rho_next

    if merged:
        pick_back(iterate, own)
        ret[pl.ds(me, 1)] = own[pl.ds(me, 1)]
    else:
        pick_back(iterate, sent)
        for copy in backs:
            copy.start()
        ret[pl.ds(me, 1)] = sent[pl.ds(me, 1)]
    solid[0] = iterate
    if not merged:
        finish_faces()

    for copy in arrivals + faces:
        copy.wait_send()

    @pl.when(has_left)
    def _():
        for copy in [pre_l] + halo_l:
            copy.wait_send()

    @pl.when(has_right)
    def _():
        for copy in [pre_r] + halo_r:
            copy.wait_send()

    for copy in backs:
        copy.wait()
    wall[...] = WALL_COUPLING * (ret[...] - outp[1:senders + 1])
    if merged:
        other = pl.ds(1 - me, 1)
        wall[other] = wall[other] + WALL_COUPLING * sums[0, 0:1, :][None]
        for side, has, _, _, _, _ in sides:
            @pl.when(has)
            def _():
                for copy in far_copies(side):
                    copy.wait_send()


def finish(group, base, hot, src, wall, solid, new_h, solid_h, new, sems):
    cx, cy, cz = base.shape
    rows = cx * cy
    chunks, width = hot.shape[0], src.shape[-1]
    solid_copy = pltpu.make_async_copy(solid, solid_h, sems.at[0])
    solid_copy.start()

    def placed_of(c):
        halves = []
        for j in range(group):
            q = c * group + j
            placed = jnp.where(rows_of((cz, width)) == src[q, 0] & (cz - 1), wall[q], 0.0)
            halves.append(jnp.concatenate(split(placed), axis=0))
        return jnp.concatenate(halves, axis=1)

    step = rows // 4
    cuts = [slice(s * step // cy, (s + 1) * step // cy) for s in range(4)]

    def added(c, s, placed):
        both = dot_nt(hot[c, s * step:(s + 1) * step, :], placed)
        return (both[:, 0:cz] + both[:, cz:2 * cz]).reshape(step // cy, cy, cz)

    if chunks > 1:
        def add_chunk(c):
            placed = placed_of(c)
            for s in range(4):
                base_now = jnp.where(c == 0, base[cuts[s]], new[cuts[s]])
                new[cuts[s]] = base_now + added(c, s, placed)

        pl.loop(0, chunks)(add_chunk)
    else:
        placed = placed_of(0)
    copies = []
    for s in range(4):
        if chunks == 1:
            new[cuts[s]] = base[cuts[s]] + added(0, s, placed)
        copies.append(pltpu.make_async_copy(new.at[cuts[s]], new_h.at[cuts[s]], sems.at[s + 1]))
        copies[-1].start()
    for copy in [solid_copy] + copies:
        copy.wait()


def per_device(fluid_temp, liquid, face_src, face_dst, solid_old, solid_diag, blocks, pattern):
    senders = lax.axis_size("gx")
    group = 2 if senders % 2 == 0 else 1
    chunks = senders // group
    cx, cy, cz = fluid_temp.shape
    rows = cx * cy
    tiles, width = solid_old.shape[1:]
    pre_rows = (senders + 2 * REACH + 7) // 8 * 8
    ext_rows = (tiles + 2 * REACH + 7) // 8 * 8
    dma = pltpu.SemaphoreType.DMA
    pattern = jnp.transpose(pattern, (2, 0, 1))
    args = (fluid_temp, liquid, face_src, face_dst, solid_old, solid_diag, blocks, pattern)
    args = tuple(pltpu.with_memory_space_constraint(a, pltpu.HBM) for a in args)
    scratch = [pltpu.VMEM(a.shape, a.dtype)
               for a in (fluid_temp, liquid, face_dst, solid_old, solid_diag, blocks, pattern)]
    scratch += [
        pltpu.VMEM((chunks, width, group * width), BF16),
        pltpu.VMEM((3, chunks, group * width, width), BF16),
        pltpu.VMEM((2 * cz, rows), BF16),
        pltpu.VMEM((senders + 2, 1, width), F32),
        pltpu.VMEM((senders, 3, 1, width), F32),
        pltpu.VMEM((senders, 1, width), F32),
        pltpu.VMEM((senders, 1, width), F32),
        pltpu.VMEM((2, pre_rows, width), F32),
        pltpu.VMEM((2, pre_rows, width), F32),
        pltpu.VMEM((SWEEPS - 1, 2, REACH, width), F32),
        pltpu.VMEM((SWEEPS - 1, 2, REACH, width), F32),
        pltpu.VMEM((2, cy, cz), F32),
        pltpu.VMEM((2, cx, cz), F32),
        pltpu.VMEM((2, cx, cz), F32),
        pltpu.VMEM((2, 1, rows), F32),
        pltpu.VMEM((2, 1, rows), F32),
        pltpu.VMEM((ext_rows, width), F32),
        pltpu.VMEM((3, 2 * tiles, width), F32),
        pltpu.VMEM((2, tiles, width), F32),
        pltpu.VMEM((2, REACH * width, 2 * REACH * width), BF16),
        pltpu.VMEM((REACH * REACH, width, width), F32),
        pltpu.VMEM((REACH * width, 2 * REACH * width), BF16),
        pltpu.VMEM((senders, 1, width), F32),
        dma((8,)),
        dma((senders,)), dma((senders,)),
        dma((senders,)), dma((senders,)),
        dma((2,)), dma((2,)),
        dma((SWEEPS - 1, 2)), dma((SWEEPS - 1, 2)),
        dma((6,)), dma((6,)),
        pltpu.SemaphoreType.REGULAR,
        dma((4,)), dma((4,)),
    ]
    parts = pl.pallas_call(
        functools.partial(kernel, senders, group),
        out_shape=(
            pltpu.VMEM(fluid_temp.shape, F32),
            pltpu.VMEM((chunks, rows, group * width), BF16),
            pltpu.VMEM(face_src.shape, jnp.int32),
            pltpu.VMEM((senders, 1, width), F32),
            pltpu.VMEM(solid_old.shape, F32),
        ),
        in_specs=[pl.BlockSpec(memory_space=pltpu.HBM)] * 8,
        out_specs=(pl.BlockSpec(memory_space=pltpu.VMEM),) * 5,
        scratch_shapes=scratch,
        compiler_params=pltpu.CompilerParams(
            collective_id=0, has_side_effects=True, vmem_limit_bytes=24 * 1024 * 1024
        ),
    )(*args)
    parts = tuple(pltpu.with_memory_space_constraint(p, pltpu.VMEM) for p in parts)
    return pl.pallas_call(
        functools.partial(finish, group),
        out_shape=(
            jax.ShapeDtypeStruct(fluid_temp.shape, F32),
            jax.ShapeDtypeStruct(solid_old.shape, F32),
        ),
        in_specs=[pl.BlockSpec(memory_space=pltpu.VMEM)] * 5,
        out_specs=(pl.BlockSpec(memory_space=pl.ANY),) * 2,
        scratch_shapes=[pltpu.VMEM(fluid_temp.shape, F32), dma((5,))],
        compiler_params=pltpu.CompilerParams(vmem_limit_bytes=16 * 1024 * 1024),
    )(*parts)


def solution(mesh):
    return jax.shard_map(
        per_device,
        mesh=mesh,
        in_specs=(
            P("gx", "gy", "gz"),
            P("gx", "gy", "gz"),
            P("gx", "gy", "gz", None),
            P("gx", "gy", "gz", None),
            P(("gy", "gz"), "gx", None),
            P(("gy", "gz"), "gx", None),
            P(("gy", "gz"), "gx", None, None, None),
            P(("gy", "gz"), "gx", None),
        ),
        out_specs=(P("gx", "gy", "gz"), P(("gy", "gz"), "gx", None)),
        check_vma=False,
    )
```

```python
import functools

import jax
import jax.numpy as jnp
from jax import lax
from jax.experimental import pallas as pl
from jax.experimental.pallas import tpu as pltpu
from jax.sharding import PartitionSpec as P

REACH = 2
SWEEPS = 4
NB = 5
DIFFUSION = 0.12
EVAPORATION = 0.5
SATURATION = 0.25
WALL_COUPLING = 0.2
MESH = pl.DeviceIdType.MESH
F32 = jnp.float32
BF16 = jnp.bfloat16


def split(values):
    high = values.astype(BF16)
    return high, (values - high.astype(F32)).astype(BF16)


def dot(a, b):
    return jnp.dot(a, b, preferred_element_type=F32)


def dot_nt(a, b):
    return lax.dot_general(a, b, (((1,), (1,)), ((), ())), preferred_element_type=F32)


def rows_of(shape):
    return lax.broadcasted_iota(jnp.int32, shape, 0)


def repeat(count, body):
    if count == 1:
        body(0)
    else:
        pl.loop(0, count)(body)


def kernel(
    senders, group,
    fluid_h, liquid_h, src_h, dst_h, old_h, diag_h, blocks_h, pat_h,
    base, hot, src, wall, solid,
    fluid, liquid, dst, old, diag, blocks, pat,
    spot, back, table, outp, arr, sent, ret, pre_out, pre_in, halo_out, halo,
    x_in, y_out, y_in, z_out, z_in, ext, gather, sums, edge, far_in, far_edge, own,
    load_sem, arr_send, arr_recv, ret_send, ret_recv, pre_send, pre_recv,
    halo_send, halo_recv, face_send, face_recv, near_sem, far_send, far_recv,
):
    cx, cy, cz = fluid.shape
    rows = cx * cy
    tiles, width = old.shape[1], old.shape[2]
    chunks = senders // group
    me = lax.axis_index("gx")
    gy, gz = lax.axis_index("gy"), lax.axis_index("gz")
    ny, nz = lax.axis_size("gy"), lax.axis_size("gz")
    left, right = lax.rem(me + senders - 1, senders), lax.rem(me + 1, senders)
    below, above = lax.rem(gy + ny - 1, ny), lax.rem(gy + 1, ny)
    before, after = lax.rem(gz + nz - 1, nz), lax.rem(gz + 1, nz)
    has_left, has_right = me > 0, me < senders - 1
    barrier = pltpu.get_barrier_semaphore()

    line_peers = [{"gx": lax.rem(me + d, senders)} for d in range(1, senders)]
    cross_peers = [{"gy": below}, {"gy": above}, {"gz": before}, {"gz": after}]
    odd = lax.rem(gy + gz, 2) == 1
    even = jnp.logical_not(odd)

    def signal(semaphore, device):
        pl.semaphore_signal(semaphore, inc=1, device_id=device, device_id_type=MESH)

    for peer in line_peers:
        signal(barrier, peer)

    @pl.when(even)
    def _():
        for peer in cross_peers:
            signal(barrier, peer)

    pairs = [(src_h, src), (fluid_h, fluid), (dst_h, dst), (old_h, old), (diag_h, diag),
             (pat_h, pat), (blocks_h, blocks), (liquid_h, liquid)]
    loads = [pltpu.make_async_copy(a, b, load_sem.at[i]) for i, (a, b) in enumerate(pairs)]
    for load in loads:
        load.start()

    def send(source, target, send_sem, recv_sem, device):
        return pltpu.make_async_remote_copy(
            src_ref=source, dst_ref=target, send_sem=send_sem, recv_sem=recv_sem,
            device_id=device, device_id_type=MESH)

    outp[...] = jnp.zeros_like(outp)
    ext[...] = jnp.zeros_like(ext)
    sums[...] = jnp.zeros_like(sums)
    loads[0].wait()

    def make_hot(c):
        for j in range(group):
            row = src[c * group + j, 0] >> 7
            for s in range(0, rows, 128):
                hit = rows_of((128, width)) + s == row
                hot[c, s:s + 128, j * width:(j + 1) * width] = jnp.where(hit, 1.0, 0.0).astype(BF16)

    repeat(chunks, make_hot)

    for load in loads[2:5]:
        load.wait()
    diagonal = diag[0]
    inverse = 1.0 / diagonal
    fixed = diagonal * old[0]
    for side, lo in ((0, 0), (1, tiles - REACH)):
        for q in range(senders):
            pre_out[side, q:q + 1, :] = dst[q, 0].astype(F32)
        pre_out[side, senders:senders + REACH, :] = fixed[lo:lo + REACH]
        pre_out[side, senders + REACH:senders + 2 * REACH, :] = inverse[lo:lo + REACH]

    loads[1].wait()
    per = 128 // cy
    for s in range(rows // 128):
        flipped = fluid[s * per:(s + 1) * per].reshape(128, cz).T
        high, low = split(flipped)
        table[0:cz, s * 128:(s + 1) * 128] = high
        table[cz:2 * cz, s * 128:(s + 1) * 128] = low
        z_out[0, :, s * 128:(s + 1) * 128] = flipped[0:1]
        z_out[1, :, s * 128:(s + 1) * 128] = flipped[cz - 1:cz]

    def pick(c):
        picked = dot(table[...], hot[c])
        picked = picked[0:cz] + picked[cz:2 * cz]
        for j in range(group):
            depth = src[c * group + j, 0] & (cz - 1)
            part = picked[:, j * width:(j + 1) * width]
            part = jnp.where(rows_of((cz, width)) == depth, part, 0.0)
            outp[c * group + j + 1] = jnp.sum(part, axis=0, keepdims=True)

    repeat(chunks, pick)

    pl.semaphore_wait(barrier, jnp.where(odd, len(line_peers) + len(cross_peers), len(line_peers)))

    pre_l = send(pre_out.at[0], pre_in.at[1], pre_send.at[0], pre_recv.at[1], {"gx": left})
    pre_r = send(pre_out.at[1], pre_in.at[0], pre_send.at[1], pre_recv.at[0], {"gx": right})
    halo_l = [send(halo_out.at[k, 0], halo.at[k, 1], halo_send.at[k, 0], halo_recv.at[k, 1],
                   {"gx": left}) for k in range(SWEEPS - 1)]
    halo_r = [send(halo_out.at[k, 1], halo.at[k, 0], halo_send.at[k, 1], halo_recv.at[k, 0],
                   {"gx": right}) for k in range(SWEEPS - 1)]
    arrivals = []
    for d in range(1, senders):
        peer = lax.rem(me + d, senders)
        arrivals.append(send(outp.at[pl.ds(peer, 3)], arr.at[me], arr_send.at[d], arr_recv.at[d],
                             {"gx": peer}))

    @pl.when(has_left)
    def _():
        pre_l.start()

    @pl.when(has_right)
    def _():
        pre_r.start()

    for copy in arrivals:
        copy.start()
    y_out[0] = fluid[:, 0, :]
    y_out[1] = fluid[:, cy - 1, :]
    faces = [
        send(fluid.at[0], x_in.at[1], face_send.at[0], face_recv.at[0], {"gx": left}),
        send(fluid.at[cx - 1], x_in.at[0], face_send.at[1], face_recv.at[1], {"gx": right}),
        send(y_out.at[0], y_in.at[1], face_send.at[2], face_recv.at[2], {"gy": below}),
        send(y_out.at[1], y_in.at[0], face_send.at[3], face_recv.at[3], {"gy": above}),
        send(z_out.at[0], z_in.at[1], face_send.at[4], face_recv.at[4], {"gz": before}),
        send(z_out.at[1], z_in.at[0], face_send.at[5], face_recv.at[5], {"gz": after}),
    ]

    @pl.when(odd)
    def _():
        for peer in cross_peers:
            signal(near_sem, peer)
        for face in faces[2:]:
            face.start()

    for face in faces[0:2]:
        face.start()
    arr[pl.ds(me, 1)] = outp[pl.ds(me, 3)][None]

    @pl.when(jnp.logical_not(has_left))
    def _():
        pre_in[0] = jnp.zeros_like(pre_in[0])

    @pl.when(jnp.logical_not(has_right))
    def _():
        pre_in[1] = jnp.zeros_like(pre_in[1])

    for load in loads[5:7]:
        load.wait()
    small = rows_of((tiles, tiles)) == lax.broadcasted_iota(jnp.int32, (tiles, tiles), 1)
    for o in range(NB):
        row = jnp.broadcast_to(pat[o].astype(F32), (tiles, tiles))
        column = jnp.sum(jnp.where(small, row, 0.0), axis=1, keepdims=True)
        mask = jnp.broadcast_to(column, (tiles, width))
        for t in range(tiles):
            blocks[0, t, o] = blocks[0, t, o] * mask[t:t + 1]

    @pl.when(has_left)
    def _():
        send(pre_out.at[1], pre_in.at[0], pre_send.at[1], pre_recv.at[0], {"gx": left}).wait_recv()

    @pl.when(has_right)
    def _():
        send(pre_out.at[0], pre_in.at[1], pre_send.at[0], pre_recv.at[1], {"gx": right}).wait_recv()

    def ids_at(run, q):
        if run == 1:
            return dst[q, 0]
        return pre_in[run // 2, pl.ds(q, 1), :].astype(jnp.int32)

    def make_spot(c):
        for run in range(3):
            for j in range(group):
                hit = rows_of((width, width)) == ids_at(run, c * group + j) & (width - 1)
                hit = jnp.where(hit, 1.0, 0.0)
                back[run, c, j * width:(j + 1) * width, :] = hit.T.astype(BF16)
                if run == 1:
                    spot[c, :, j * width:(j + 1) * width] = hit.astype(BF16)

    repeat(chunks, make_spot)
    ones = jnp.ones((2 * width, width), BF16)
    eye = rows_of((width, width)) == lax.broadcasted_iota(jnp.int32, (width, width), 1)
    for copy in arrivals:
        copy.wait_recv()

    gather[...] = jnp.zeros_like(gather)

    def add_group(c):
        for run in range(3):
            lhs = []
            for j in range(group):
                q = c * group + j
                hit = rows_of((tiles, width)) == ids_at(run, q) >> 7
                high, low = split(jnp.where(hit, arr[q, run], 0.0))
                lhs.append(jnp.concatenate([high, low], axis=0))
            gather[run] += dot(jnp.concatenate(lhs, axis=1), back[run, c])

    repeat(chunks, add_group)
    gathered = [gather[run, 0:tiles] + gather[run, tiles:2 * tiles] for run in range(3)]
    right_side = fixed + gathered[1]
    iterate = inverse * right_side
    ext[REACH:REACH + tiles, :] = iterate
    for side, run, lo, at in ((0, 0, tiles - REACH, 0), (1, 2, 0, tiles + REACH)):
        fixed_near = pre_in[side, senders:senders + REACH, :]
        inverse_near = pre_in[side, senders + REACH:senders + 2 * REACH, :]
        ext[at:at + REACH, :] = inverse_near * (fixed_near + gathered[run][lo:lo + REACH])

    def couple(slot, pairs_of):
        for t, offsets in pairs_of:
            total = None
            for o in offsets:
                term = blocks[0, t, o] * ext[t + o:t + o + 1, :]
                total = term if total is None else total + term
            high, low = split(total)
            summed = dot(jnp.concatenate([high, low], axis=1), ones)
            sums[slot, t:t + 1, :] = jnp.sum(jnp.where(eye, summed, 0.0), axis=0, keepdims=True)

    def inside(t, o):
        return 0 <= t + o - REACH < tiles

    every = list(range(NB))
    middle = [(t, every) for t in range(REACH, tiles - REACH)]
    local = [(t, [o for o in every if inside(t, o)]) for t in range(tiles)]
    from_first = [(t, [o for o in offsets if t + o < 2 * REACH]) for t, offsets in local[:2 * REACH]]
    from_last = [(t, [o for o in offsets if t + o >= tiles]) for t, offsets in local[tiles - 2 * REACH:]]
    first = [(t, every) for t in range(REACH)]
    last = [(t, every) for t in range(tiles - REACH, tiles)]
    no_left, no_right = jnp.logical_not(has_left), jnp.logical_not(has_right)

    sides = ((0, has_left, 0, 0, halo_r, halo_l),
             (1, has_right, tiles - REACH, tiles + REACH, halo_l, halo_r))

    def make_edges():
        for side, has, lo, at, _, _ in sides:
            @pl.when(has)
            def _():
                for i in range(REACH):
                    for j in range(REACH):
                        o = at + i - lo - j
                        block = jnp.zeros((width, width), F32)
                        if 0 <= o < NB:
                            block = blocks[0, lo + j, o].T
                        for part, values in enumerate(split(block)):
                            column = (part * REACH + j) * width
                            edge[side, i * width:(i + 1) * width, column:column + width] = values

    def times_edge(values, matrix):
        flat = jnp.concatenate([values[i:i + 1] for i in range(REACH)], axis=1)
        high = flat.astype(BF16).astype(F32)
        lhs = [jnp.broadcast_to(v, (8, REACH * width)) for v in (high, flat - high)]
        product = dot(jnp.concatenate(lhs, axis=0).astype(BF16), matrix)
        product = product[0:1] + product[8:9]
        product = product[:, 0:REACH * width] + product[:, REACH * width:]
        return jnp.concatenate([product[:, j * width:(j + 1) * width] for j in range(REACH)], axis=0)

    merged = senders == 2
    places = [(i, j) for i in range(REACH) for j in range(REACH)]

    def far_blocks(side):
        _, _, lo, at, _, _ = sides[side]
        found = [(n, i, j, at + i - lo - j) for n, (i, j) in enumerate(places)]
        return [entry for entry in found if 0 <= entry[3] < NB]

    def far_copies(side):
        lo = sides[side][2]
        return [send(blocks.at[0, lo + j, o], far_in.at[n], far_send.at[n], far_recv.at[n],
                     {"gx": left if side == 0 else right}) for n, i, j, o in far_blocks(side)]

    def send_far(turn):
        for side, has, _, _, _, _ in sides:
            @pl.when(has)
            def _():
                copies = far_copies(side)
                for copy in copies[:REACH] if turn == 0 else copies[REACH:]:
                    copy.start()

    def correct(scale_new):
        for side, has, lo, _, _, _ in sides:
            @pl.when(has)
            def _():
                for copy in far_copies(1 - side):
                    copy.wait_recv()
                far_edge[...] = jnp.zeros_like(far_edge)
                for n, i, j, _ in far_blocks(1 - side):
                    for half, values in enumerate(split(far_in[n].T)):
                        column = (half * REACH + j) * width
                        far_edge[i * width:(i + 1) * width, column:column + width] = values
                summed = times_edge(iterate[lo:lo + REACH], far_edge[...])
                change = -scale_new * pre_in[side, senders + REACH:senders + 2 * REACH, :] * summed
                ids = pre_in[side, pl.ds(me, 1), :].astype(jnp.int32)
                hit = rows_of((width, width)) == ids & (width - 1)
                change = jnp.concatenate([change, jnp.zeros((8 - REACH, width), F32)], axis=0)
                picked = dot(jnp.concatenate(split(change), axis=0), jnp.where(hit, 1.0, 0.0).astype(BF16))
                picked = picked[0:8] + picked[8:16]
                row = (ids >> 7) - (0 if side == 1 else tiles - REACH)
                live = jnp.logical_and(rows_of((8, width)) == row, rows_of((8, width)) < REACH)
                sums[0, 0:1, :] = jnp.sum(jnp.where(live, picked, 0.0), axis=0, keepdims=True)

    def take(k, part, scale_old, scale_new):
        for side, has, lo, _, copy_in, copy_out in sides:
            @pl.when(has)
            def _():
                copy_in[k].wait_recv()
                summed = times_edge(halo[k, side], edge[side])
                cut = slice(lo, lo + REACH)
                if k + 1 < SWEEPS - 1:
                    change = scale_old * update[cut] + scale_new * inverse[cut] * (part[cut] - summed)
                    halo_out[k + 1, side] = iterate[cut] + change
                    copy_out[k + 1].start()
                sums[1, cut, :] = summed

    lane = lax.broadcasted_iota(jnp.int32, (cy, cz), 1)
    line = lax.broadcasted_iota(jnp.int32, (cy, cz), 0)

    def stencil(first, last):
        for i in range(first, last):
            here = fluid[i]
            near = jnp.where(line == 0, 0.0, pltpu.roll(here, 1, 0))
            near = near + jnp.where(line == cy - 1, 0.0, pltpu.roll(here, cy - 1, 0))
            near = near + jnp.where(lane == 0, 0.0, pltpu.roll(here, 1, 1))
            near = near + jnp.where(lane == cz - 1, 0.0, pltpu.roll(here, cz - 1, 1))
            if i > 0:
                near = near + fluid[i - 1]
            if i < cx - 1:
                near = near + fluid[i + 1]
            dry = liquid[i].astype(F32) * jnp.maximum(here - SATURATION, 0.0)
            base[i] = here + DIFFUSION * (near - 6.0 * here) - EVAPORATION * dry

    def finish_faces():
        for face in faces[2:]:
            face.wait_recv()
        base[:, 0, :] += DIFFUSION * y_in[0]
        base[:, cy - 1, :] += DIFFUSION * y_in[1]
        deep = rows_of((cz, 128))
        for s in range(rows // 128):
            cut = slice(s * 128, (s + 1) * 128)
            layer = jnp.where(deep == 0, z_in[0, :, cut], 0.0)
            layer = layer + jnp.where(deep == cz - 1, z_in[1, :, cut], 0.0)
            base[s * per:(s + 1) * per] += DIFFUSION * layer.T.reshape(per, cy, cz)

    def pick_back(values, target):
        both = jnp.concatenate(split(values), axis=0)

        def pick_chunk(c):
            picked = dot(both, spot[c])
            picked = picked[0:tiles] + picked[tiles:2 * tiles]
            for j in range(group):
                row = dst[c * group + j, 0] >> 7
                part = picked[:, j * width:(j + 1) * width]
                part = jnp.where(rows_of((tiles, width)) == row, part, 0.0)
                target[c * group + j] = jnp.sum(part, axis=0, keepdims=True)

        repeat(chunks, pick_chunk)

    backs = []
    for d in range(1, senders):
        peer = lax.rem(me + d, senders)
        backs.append(send(sent.at[peer], ret.at[me], ret_send.at[d], ret_recv.at[d], {"gx": peer}))

    def step(lo):
        cut = slice(lo, lo + REACH)
        rest = right_side[cut] - diagonal[cut] * iterate[cut] - sums[0, cut, :]
        return iterate[cut] + inverse[cut] * rest

    @pl.when(has_left)
    def _():
        couple(0, first)
        halo_out[0, 0] = step(0)
        halo_l[0].start()

    @pl.when(has_right)
    def _():
        couple(0, last)
        halo_out[0, 1] = step(tiles - REACH)
        halo_r[0].start()

    @pl.when(no_left)
    def _():
        couple(0, first)

    @pl.when(no_right)
    def _():
        couple(0, last)

    couple(0, middle)
    update = inverse * (right_side - diagonal * iterate - sums[0])
    iterate = iterate + update
    rho_old = 0.5
    for k in range(SWEEPS - 1):
        rho_next = 1.0 / (4.0 - rho_old)
        ext[REACH:REACH + tiles, :] = iterate
        if merged and k < 2:
            send_far(k)
        if k == SWEEPS - 2:
            ext[REACH:REACH + tiles, :] = delta
            for has, touched in ((has_left, from_first), (has_right, from_last)):
                @pl.when(has)
                def _():
                    couple(2, touched)
            part = right_side - diagonal * iterate - (ahead + sums[2])
        else:
            couple(0, local)
            part = right_side - diagonal * iterate - sums[0]
        if k == 0:
            loads[7].wait()
            stencil(0, cx // 2)
        if k == 1:
            stencil(cx // 2, cx)

            @pl.when(even)
            def _():
                pl.semaphore_wait(near_sem, len(cross_peers))
                for face in faces[2:]:
                    face.start()

        if merged and k == SWEEPS - 2:
            change = rho_next * rho_old * update + 4.0 * rho_next * inverse * part
            pick_back(iterate + change, sent)
            for copy in backs:
                copy.start()
            correct(4.0 * rho_next)
        if k == SWEEPS - 2:
            for face in faces[0:2]:
                face.wait_recv()
            base[0] += DIFFUSION * x_in[0]
            base[cx - 1] += DIFFUSION * x_in[1]
            if merged:
                finish_faces()
        if k == 0:
            make_edges()
        if k == SWEEPS - 3:
            ext[REACH:REACH + tiles, :] = iterate + rho_next * rho_old * update + 4.0 * rho_next * inverse * part
            couple(0, local)
            ahead = sums[0]
        take(k, part, rho_next * rho_old, 4.0 * rho_next)
        delta = -4.0 * rho_next * inverse * sums[1]
        residual = part - sums[1]
        update = rho_next * rho_old * update + 4.0 * rho_next * inverse * residual
        iterate = iterate + update
        rho_old = rho_next

    if merged:
        pick_back(iterate, own)
        ret[pl.ds(me, 1)] = own[pl.ds(me, 1)]
    else:
        pick_back(iterate, sent)
        for copy in backs:
            copy.start()
        ret[pl.ds(me, 1)] = sent[pl.ds(me, 1)]
    solid[0] = iterate
    if not merged:
        finish_faces()

    for copy in arrivals + faces:
        copy.wait_send()

    @pl.when(has_left)
    def _():
        for copy in [pre_l] + halo_l:
            copy.wait_send()

    @pl.when(has_right)
    def _():
        for copy in [pre_r] + halo_r:
            copy.wait_send()

    for copy in backs:
        copy.wait()
    wall[...] = WALL_COUPLING * (ret[...] - outp[1:senders + 1])
    if merged:
        other = pl.ds(1 - me, 1)
        wall[other] = wall[other] + WALL_COUPLING * sums[0, 0:1, :][None]
        for side, has, _, _, _, _ in sides:
            @pl.when(has)
            def _():
                for copy in far_copies(side):
                    copy.wait_send()


def finish(group, base, hot, src, wall, solid, new_h, solid_h, new, sems):
    cx, cy, cz = base.shape
    rows = cx * cy
    chunks, width = hot.shape[0], src.shape[-1]
    solid_copy = pltpu.make_async_copy(solid, solid_h, sems.at[0])
    solid_copy.start()

    def placed_of(c):
        halves = []
        for j in range(group):
            q = c * group + j
            placed = jnp.where(rows_of((cz, width)) == src[q, 0] & (cz - 1), wall[q], 0.0)
            halves.append(jnp.concatenate(split(placed), axis=0))
        return jnp.concatenate(halves, axis=1)

    step = rows // 4
    cuts = [slice(s * step // cy, (s + 1) * step // cy) for s in range(4)]

    def added(c, s, placed):
        both = dot_nt(hot[c, s * step:(s + 1) * step, :], placed)
        return (both[:, 0:cz] + both[:, cz:2 * cz]).reshape(step // cy, cy, cz)

    if chunks > 1:
        def add_chunk(c):
            placed = placed_of(c)
            for s in range(4):
                base_now = jnp.where(c == 0, base[cuts[s]], new[cuts[s]])
                new[cuts[s]] = base_now + added(c, s, placed)

        pl.loop(0, chunks)(add_chunk)
    else:
        placed = placed_of(0)
    copies = []
    for s in range(4):
        if chunks == 1:
            new[cuts[s]] = base[cuts[s]] + added(0, s, placed)
        copies.append(pltpu.make_async_copy(new.at[cuts[s]], new_h.at[cuts[s]], sems.at[s + 1]))
        copies[-1].start()
    for copy in [solid_copy] + copies:
        copy.wait()


def per_device(fluid_temp, liquid, face_src, face_dst, solid_old, solid_diag, blocks, pattern):
    senders = lax.axis_size("gx")
    group = 2 if senders % 2 == 0 else 1
    chunks = senders // group
    cx, cy, cz = fluid_temp.shape
    rows = cx * cy
    tiles, width = solid_old.shape[1:]
    pre_rows = (senders + 2 * REACH + 7) // 8 * 8
    ext_rows = (tiles + 2 * REACH + 7) // 8 * 8
    dma = pltpu.SemaphoreType.DMA
    pattern = jnp.transpose(pattern, (2, 0, 1))
    args = (fluid_temp, liquid, face_src, face_dst, solid_old, solid_diag, blocks, pattern)
    args = tuple(pltpu.with_memory_space_constraint(a, pltpu.HBM) for a in args)
    scratch = [pltpu.VMEM(a.shape, a.dtype)
               for a in (fluid_temp, liquid, face_dst, solid_old, solid_diag, blocks, pattern)]
    scratch += [
        pltpu.VMEM((chunks, width, group * width), BF16),
        pltpu.VMEM((3, chunks, group * width, width), BF16),
        pltpu.VMEM((2 * cz, rows), BF16),
        pltpu.VMEM((senders + 2, 1, width), F32),
        pltpu.VMEM((senders, 3, 1, width), F32),
        pltpu.VMEM((senders, 1, width), F32),
        pltpu.VMEM((senders, 1, width), F32),
        pltpu.VMEM((2, pre_rows, width), F32),
        pltpu.VMEM((2, pre_rows, width), F32),
        pltpu.VMEM((SWEEPS - 1, 2, REACH, width), F32),
        pltpu.VMEM((SWEEPS - 1, 2, REACH, width), F32),
        pltpu.VMEM((2, cy, cz), F32),
        pltpu.VMEM((2, cx, cz), F32),
        pltpu.VMEM((2, cx, cz), F32),
        pltpu.VMEM((2, 1, rows), F32),
        pltpu.VMEM((2, 1, rows), F32),
        pltpu.VMEM((ext_rows, width), F32),
        pltpu.VMEM((3, 2 * tiles, width), F32),
        pltpu.VMEM((3, tiles, width), F32),
        pltpu.VMEM((2, REACH * width, 2 * REACH * width), BF16),
        pltpu.VMEM((REACH * REACH, width, width), F32),
        pltpu.VMEM((REACH * width, 2 * REACH * width), BF16),
        pltpu.VMEM((senders, 1, width), F32),
        dma((8,)),
        dma((senders,)), dma((senders,)),
        dma((senders,)), dma((senders,)),
        dma((2,)), dma((2,)),
        dma((SWEEPS - 1, 2)), dma((SWEEPS - 1, 2)),
        dma((6,)), dma((6,)),
        pltpu.SemaphoreType.REGULAR,
        dma((4,)), dma((4,)),
    ]
    parts = pl.pallas_call(
        functools.partial(kernel, senders, group),
        out_shape=(
            pltpu.VMEM(fluid_temp.shape, F32),
            pltpu.VMEM((chunks, rows, group * width), BF16),
            pltpu.VMEM(face_src.shape, jnp.int32),
            pltpu.VMEM((senders, 1, width), F32),
            pltpu.VMEM(solid_old.shape, F32),
        ),
        in_specs=[pl.BlockSpec(memory_space=pltpu.HBM)] * 8,
        out_specs=(pl.BlockSpec(memory_space=pltpu.VMEM),) * 5,
        scratch_shapes=scratch,
        compiler_params=pltpu.CompilerParams(
            collective_id=0, has_side_effects=True, vmem_limit_bytes=24 * 1024 * 1024
        ),
    )(*args)
    parts = tuple(pltpu.with_memory_space_constraint(p, pltpu.VMEM) for p in parts)
    return pl.pallas_call(
        functools.partial(finish, group),
        out_shape=(
            jax.ShapeDtypeStruct(fluid_temp.shape, F32),
            jax.ShapeDtypeStruct(solid_old.shape, F32),
        ),
        in_specs=[pl.BlockSpec(memory_space=pltpu.VMEM)] * 5,
        out_specs=(pl.BlockSpec(memory_space=pl.ANY),) * 2,
        scratch_shapes=[pltpu.VMEM(fluid_temp.shape, F32), dma((5,))],
        compiler_params=pltpu.CompilerParams(vmem_limit_bytes=16 * 1024 * 1024),
    )(*parts)


def solution(mesh):
    return jax.shard_map(
        per_device,
        mesh=mesh,
        in_specs=(
            P("gx", "gy", "gz"),
            P("gx", "gy", "gz"),
            P("gx", "gy", "gz", None),
            P("gx", "gy", "gz", None),
            P(("gy", "gz"), "gx", None),
            P(("gy", "gz"), "gx", None),
            P(("gy", "gz"), "gx", None, None, None),
            P(("gy", "gz"), "gx", None),
        ),
        out_specs=(P("gx", "gy", "gz"), P(("gy", "gz"), "gx", None)),
        check_vma=False,
    )
```
